32 devices in a mesh: tm: 8 (over z, y), head: 4 (over x, core).
Axes of the slice: x: 2, y: 2, z: 4, core: 2. Of those that a mesh axis runs over, the one named last changes fastest.
Arguments:
- series: bfloat16 [2048, 512], P('tm'), may hold values from -6 to 6
- in_weight: bfloat16 [512, 3, 1024], P(None, None, 'head'), may hold values from -0.25 to 0.25
- step_weight: bfloat16 [512, 16], P(None, 'head'), may hold values from -0.25 to 0.25
- step_bias: float32 [16], P('head'), may hold values from -7 to -6
- log_rate: float32 [16], P('head'), as said below
- conv_weight: float32 [4, 2, 1024], P(None, None, 'head'), may hold values from -3 to 3
- conv_bias: float32 [2, 1024], P(None, 'head'), may hold values from -3 to 3
- skip_gain: float32 [16], P('head'), may hold values from 0.5 to 1.5
- norm_gain: float32 [1024], P('head'), may hold values from 0.1 to 1.9
- out_weight: bfloat16 [512, 1024], P(None, 'head'), may hold values from -0.1875 to 0.1875
- cotangent: bfloat16 [2048, 512], P('tm'), may hold values from -6 to 6
Outputs:
- layer_out: bfloat16 [2048, 512], P(('tm', 'head'))
- series_grad: float32 [2048, 512], P(('tm', 'head'))
- w_in_grad: float32 [512, 3, 1024], P('tm', None, 'head')
- w_dt_grad: float32 [512, 16], P('tm', 'head')
- w_out_grad: float32 [512, 1024], P('tm', 'head')
The draws below stay inside these ranges and needn't reach their ends.
Inputs may be any that keep to these rules, and one draw needn't show every extreme that they name: `log_rate`: each head's logarithm of its decay rate.
All inputs are finite; a program needn't handle non-finite values.
Results may differ from the reference program's by a relative error of at most 0.0076.
Values may be sent and summed in bfloat16 or wider, within the bound.
No kernel may reach another device: no remote copies, remote signals or barrier semaphores. Data moves between devices by JAX's collectives and lax.ppermute only.
A program may use at most 64 MiB of HBM per device.

```python
import math
import jax
import jax.numpy as jnp
from jax import lax

D = 512
E = 1024
H = 16
P_SIZE = 64
N = 128
GROUPS = 4
KW = 4
BLOCK = 256
TOKENS = 2048


def draw_log_rate(key, part):
    share = jax.random.uniform(key, (H,), jnp.float32)
    slowest = math.log(1.0 / (40.0 * TOKENS))
    fastest = math.log(1.0 / 30.0)
    return slowest + share * (fastest - slowest) - math.log(0.0025)


def spiked(entries, key, source, target, shards_of, factor):
    owner, partner = [(jnp.arange(entries.shape[position]) // (entries.shape[position] // shards_of)).reshape([-1 if axis == position else 1 for axis in range(entries.ndim)]) for position in (source, target)]
    chosen = jax.random.permutation(key, shards_of)[partner]
    strong = (owner == chosen) | (owner == (partner + shards_of // 2) % shards_of)
    return jnp.where(strong, factor * entries, entries)


def level_of(stream_key, shape, shards, low, top_value):
    factor_of, own = 1.0, jax.random.fold_in(stream_key, 6)
    for dim, blocks in shards:
        steps = jnp.exp(jax.random.uniform(jax.random.fold_in(own, dim), (blocks,), jnp.float32, low / len(shards), top_value / len(shards)))
        factor_of = factor_of * jnp.repeat(steps, shape[dim] // blocks).reshape([-1 if axis == dim else 1 for axis in range(len(shape))])
    return factor_of


def centred(key, shape, spread, bound, cuts=(), held_as=jnp.bfloat16):
    loudness = level_of(key, shape, cuts, -0.22, 0.18) if cuts else 1.0
    array = jax.random.normal(key, shape, jnp.float32) * spread * loudness
    return jnp.minimum(jnp.maximum(array, -bound), bound).astype(held_as)


def noise_with(stream_key, extent, scale, most, pieces, heavy, kind=jnp.bfloat16):
    drawn = scale * jax.random.normal(stream_key, extent, jnp.float32)
    if pieces:
        drawn = drawn * level_of(stream_key, extent, pieces, -0.22, 0.18)
    return jnp.clip(spiked(drawn, jax.random.fold_in(stream_key, 3), *heavy), -most, most).astype(kind)


def setup_inputs(seed: int = 0) -> dict:
    splits = jax.random.split(jax.random.key(seed), 12)
    series = noise_with(splits[0], (TOKENS, D), 1.0, 6.0, ((0, 8),), (0, 1, 8, 2.0))
    in_weight = centred(splits[1], (D, 3, E), D ** -0.5, 0.25, ((2, 4),))
    step_weight = centred(splits[2], (D, H), D ** -0.5, 0.25, ((1, 4),))
    step_bias = jnp.clip(-7.0 + 1.0 * jax.random.uniform(splits[3], (H,), jnp.float32) ** level_of(splits[3], (H,), ((0, 4),), -0.2, 0.2), -7.0, -6.0)
    log_rate = draw_log_rate(jax.random.fold_in(splits[11], 71), 0)
    conv_weight = centred(splits[5], (KW, 2, E), 0.5, 3.0, ((2, 4),), jnp.float32)
    conv_bias = centred(splits[6], (2, E), 0.5, 3.0, ((1, 4),), jnp.float32)
    skip_gain = jnp.clip(0.5 + 1.0 * jax.random.uniform(splits[7], (H,), jnp.float32) ** level_of(splits[7], (H,), ((0, 4),), -0.2, 0.2), 0.5, 1.5)
    norm_gain = jnp.clip(1.0 + 0.18 * jax.random.normal(splits[8], (E,), jnp.float32), 0.1, 1.9)
    out_weight = centred(splits[9], (D, E), E ** -0.5, 0.1875, ((1, 4),))
    cotangent = centred(splits[10], (TOKENS, D), 1.0, 6.0, ((0, 8),))
    return dict(series=series, in_weight=in_weight, step_weight=step_weight, step_bias=step_bias, log_rate=log_rate, conv_weight=conv_weight, conv_bias=conv_bias, skip_gain=skip_gain, norm_gain=norm_gain, out_weight=out_weight, cotangent=cotangent)


NORM_EPSILON = 1e-05
HIGHEST_PRECISION = lax.Precision.HIGHEST
HIGH_PRECISION = lax.Precision.HIGH

def contract(left_side, right_side, left_dim, right_dim):
    return lax.dot_general(left_side, right_side, (((left_dim,), (right_dim,)), ((), ())), preferred_element_type=jnp.float32)

def silu_grad(values):
    sigmoid_v = jax.nn.sigmoid(values)
    return sigmoid_v * (1.0 + values * (1.0 - sigmoid_v))

def decay_table(log_block):
    running = jnp.cumsum(log_block, axis=0)
    length = log_block.shape[0]
    row_ids = lax.broadcasted_iota(jnp.int32, (length, length), 0)
    col_ids = lax.broadcasted_iota(jnp.int32, (length, length), 1)
    log_gap = running.T[:, :, None] - running.T[:, None, :]
    decays = jnp.exp(jnp.where((col_ids <= row_ids)[None], log_gap, -1e+30))
    return (running, decays)

def block_forward(x_block, b_block, c_block, step_block, log_block, start_state, skip_gain):
    per_group = x_block.shape[1] // b_block.shape[1]
    x_wide = x_block.astype(jnp.float32)
    b_wide = b_block.astype(jnp.float32)
    c_wide = c_block.astype(jnp.float32)
    b_heads = jnp.repeat(b_wide, per_group, axis=1)
    c_heads = jnp.repeat(c_wide, per_group, axis=1)
    running, decays = decay_table(log_block)
    scores = jnp.einsum('ign,jgn->gij', c_block, b_block, preferred_element_type=jnp.float32)
    mixing = jnp.repeat(scores, per_group, axis=0) * decays * step_block.T[:, None, :]
    inside = jnp.einsum('hij,jhp->ihp', mixing, x_wide, precision=HIGH_PRECISION)
    from_state = jnp.exp(running)[:, :, None] * jnp.einsum('ihn,hpn->ihp', c_heads, start_state, precision=HIGH_PRECISION)
    output = inside + from_state + skip_gain[None, :, None] * x_wide
    remain = jnp.exp(running[-1][None, :] - running) * step_block
    end_state = jnp.exp(running[-1])[:, None, None] * start_state + jnp.einsum('jh,jhp,jhn->hpn', remain, x_wide, b_heads, precision=HIGH_PRECISION)
    return (output, end_state)

def block_backward(x_block, b_block, c_block, step_block, log_block, start_state, skip_gain, grad_y, ssm_out, after_state):
    group_count = b_block.shape[1]
    per_group = x_block.shape[1] // group_count
    length = x_block.shape[0]
    x_wide = x_block.astype(jnp.float32)
    b_wide = b_block.astype(jnp.float32)
    c_wide = c_block.astype(jnp.float32)
    b_heads = jnp.repeat(b_wide, per_group, axis=1)
    c_heads = jnp.repeat(c_wide, per_group, axis=1)
    running, decays = decay_table(log_block)
    scores = jnp.einsum('ign,jgn->gij', c_block, b_block, preferred_element_type=jnp.float32)
    weighted = jnp.repeat(scores, per_group, axis=0) * decays
    remain = jnp.exp(running[-1][None, :] - running)
    back_b = jnp.einsum('hit,ihp->thp', weighted, grad_y, precision=HIGH_PRECISION)
    back_b = back_b + remain[:, :, None] * jnp.einsum('thn,hpn->thp', b_heads, after_state, precision=HIGH_PRECISION)
    grad_x = skip_gain[None, :, None] * grad_y + step_block[:, :, None] * back_b
    x_back = lax.optimization_barrier(jnp.sum(x_wide * back_b, axis=2))
    grad_cum = lax.optimization_barrier(jnp.sum(grad_y * ssm_out, axis=2)) - step_block * x_back
    pair_terms = decays * jnp.einsum('ihp,jhp->hij', grad_y, x_wide, precision=HIGH_PRECISION) * step_block.T[:, None, :]
    group_terms = pair_terms.reshape(group_count, per_group, length, length).sum(axis=1)
    state_c = jnp.exp(running)[:, :, None] * jnp.einsum('ihp,hpn->ihn', grad_y, start_state, precision=HIGH_PRECISION)
    grad_c = jnp.einsum('gij,jgn->ign', group_terms, b_wide, precision=HIGH_PRECISION) + state_c.reshape(length, group_count, per_group, -1).sum(axis=2)
    state_b = (step_block * remain)[:, :, None] * jnp.einsum('jhp,hpn->jhn', x_wide, after_state, precision=HIGH_PRECISION)
    grad_b = jnp.einsum('gij,ign->jgn', group_terms, c_wide, precision=HIGH_PRECISION) + state_b.reshape(length, group_count, per_group, -1).sum(axis=2)
    before = jnp.exp(running[-1])[:, None, None] * after_state + jnp.einsum('ih,ihp,ihn->hpn', jnp.exp(running), grad_y, c_heads, precision=HIGH_PRECISION)
    return (grad_x, grad_b, grad_c, x_back, grad_cum, before)

def reference(series, in_weight, step_weight, step_bias, log_rate, conv_weight, conv_bias, skip_gain, norm_gain, out_weight, cotangent):
    margin = KW - 1
    block_total = TOKENS // BLOCK
    w_flat = in_weight.reshape(D, 3 * E)
    padded = jnp.concatenate([jnp.zeros((margin, D), jnp.bfloat16), series], axis=0)
    decay_rates = jnp.exp(log_rate)

    def front(block_index, start_state):
        rows_wide = lax.dynamic_slice_in_dim(padded, block_index * BLOCK, BLOCK + margin, 0)
        rows_here = rows_wide[margin:]
        projected = jnp.dot(rows_wide, w_flat, preferred_element_type=jnp.float32).astype(jnp.bfloat16).reshape(BLOCK + margin, 3, E)
        pre_wide = projected[:, 1:, :].astype(jnp.float32)
        conv_out = conv_bias[None] + conv_weight[0][None] * pre_wide[0:BLOCK]
        for offset in range(1, KW):
            conv_out = conv_out + conv_weight[offset][None] * pre_wide[offset:offset + BLOCK]
        activated = jax.nn.silu(conv_out)
        x_heads = activated[:, 0].astype(jnp.bfloat16).reshape(BLOCK, H, P_SIZE)
        bc_values = activated[:, 1].astype(jnp.bfloat16).reshape(BLOCK, GROUPS, 2, N)
        gate_raw = projected[margin:, 0].astype(jnp.float32)
        step_raw = jnp.dot(rows_here, step_weight, preferred_element_type=jnp.float32)
        step_size = jax.nn.softplus(step_raw + step_bias[None])
        log_decay = -step_size * decay_rates[None]
        output, end_state = block_forward(x_heads, bc_values[:, :, 0], bc_values[:, :, 1], step_size, log_decay, start_state, skip_gain)
        y_flat = output.reshape(BLOCK, E)
        gate_act = jax.nn.silu(gate_raw)
        gated_out = y_flat * gate_act
        inv_rms = lax.rsqrt(lax.optimization_barrier(jnp.sum(gated_out * gated_out, axis=1)) / E + NORM_EPSILON)
        normed = (gated_out * inv_rms[:, None] * norm_gain[None]).astype(jnp.bfloat16)
        return (rows_here, conv_out, x_heads, bc_values, gate_raw, step_raw, step_size, log_decay, output, end_state, y_flat, gate_act, gated_out, inv_rms, normed)

    def forward_step(carried, block_index):
        parts = front(block_index, carried)
        layer_block = contract(parts[14], out_weight, 1, 1).astype(jnp.bfloat16)
        return (parts[9], (layer_block, carried))
    block_ids = jnp.arange(block_total, dtype=jnp.int32)
    _, (layer_blocks, starts) = lax.scan(forward_step, jnp.zeros((H, P_SIZE, N), jnp.float32), block_ids)

    def backward_step(carried, inputs):
        block_index, start_state = inputs
        after_state, later_sum, next_rows, in_sum, dt_sum, out_sum = carried
        rows_here, conv_out, x_heads, bc_values, gate_raw, step_raw, step_size, log_decay, output, end_state, y_flat, gate_act, gated_out, inv_rms, normed = front(block_index, start_state)
        grad_here = lax.dynamic_slice_in_dim(cotangent, block_index * BLOCK, BLOCK, 0)
        grad_normed = jnp.dot(grad_here, out_weight, preferred_element_type=jnp.float32)
        out_sum = out_sum + contract(grad_here, normed, 0, 0)
        gain_grad = norm_gain[None] * grad_normed
        inner_sum = lax.optimization_barrier(jnp.sum(gated_out * gain_grad, axis=1))
        grad_gated = inv_rms[:, None] * gain_grad - gated_out * (inv_rms ** 3 * inner_sum / E)[:, None]
        grad_y = (grad_gated * gate_act).reshape(BLOCK, H, P_SIZE)
        grad_gate = grad_gated * y_flat * silu_grad(gate_raw)
        ssm_out = output - skip_gain[None, :, None] * x_heads.astype(jnp.float32)
        grad_x, grad_b, grad_c, x_back, grad_cum, before = block_backward(x_heads, bc_values[:, :, 0], bc_values[:, :, 1], step_size, log_decay, start_state, skip_gain, grad_y, ssm_out, after_state)
        grad_log = lax.cumsum(grad_cum, axis=0, reverse=True) + later_sum[None]
        grad_step = x_back - decay_rates[None] * grad_log
        grad_raw = (grad_step * jax.nn.sigmoid(step_raw + step_bias[None])).astype(jnp.bfloat16)
        grad_bc = jnp.stack([grad_b, grad_c], axis=2).reshape(BLOCK, E)
        grad_act = jnp.stack([grad_x.reshape(BLOCK, E), grad_bc], axis=1)
        grad_conv = grad_act * silu_grad(conv_out)
        grad_wide = jnp.concatenate([grad_conv, next_rows], axis=0)
        grad_pre = conv_weight[0][None] * grad_wide[margin:margin + BLOCK]
        for offset in range(1, KW):
            grad_pre = grad_pre + conv_weight[offset][None] * grad_wide[margin - offset:margin - offset + BLOCK]
        grad_proj = jnp.concatenate([grad_gate[:, None], grad_pre], axis=1).astype(jnp.bfloat16).reshape(BLOCK, 3 * E)
        in_sum = in_sum + contract(rows_here, grad_proj, 0, 0)
        dt_sum = dt_sum + contract(rows_here, grad_raw, 0, 0)
        grad_rows = contract(grad_proj, w_flat, 1, 1) + contract(grad_raw, step_weight, 1, 1)
        carried = (before, later_sum + lax.optimization_barrier(jnp.sum(grad_cum, axis=0)), grad_conv[:margin], in_sum, dt_sum, out_sum)
        return (carried, grad_rows)
    initial = (jnp.zeros((H, P_SIZE, N), jnp.float32), jnp.zeros((H,), jnp.float32), jnp.zeros((margin, 2, E), jnp.float32), jnp.zeros((D, 3 * E), jnp.float32), jnp.zeros((D, H), jnp.float32), jnp.zeros((D, E), jnp.float32))
    finals, grad_blocks = lax.scan(backward_step, initial, (block_ids, starts), reverse=True)
    layer_out = layer_blocks.reshape(TOKENS, D)
    series_grad = grad_blocks.reshape(TOKENS, D)
    return (layer_out, series_grad, finals[3].reshape(D, 3, E), finals[4], finals[5])
```

```python
import jax
import jax.numpy as jnp
from jax import lax
from jax.sharding import PartitionSpec as P

E = 1024
N = 128
KW = 4
BLOCK = 256


NORM_EPSILON = 1e-05
HIGHEST_PRECISION = lax.Precision.HIGHEST
HIGH_PRECISION = lax.Precision.HIGH


def passed_along(block, axis, distance):
    devices = range(lax.axis_size(axis))
    route = [(i - distance, i) for i in devices if i - distance in devices]
    return lax.ppermute(block, axis, route)


def carried_in(x, axis, combine, identity, reverse):
    count, position = (lax.axis_size(axis), lax.axis_index(axis))
    everything = jax.tree.map(lambda part: lax.all_gather(part, axis), x)
    start = jax.tree.map(
        lambda part, zero: jnp.broadcast_to(jnp.asarray(zero, part.dtype), part.shape), x, identity
    )

    def hop(k, before):
        at = count - 1 - k if reverse else k
        reached = at > position if reverse else at < position
        new = combine(before, jax.tree.map(lambda part: part[at], everything))
        return jax.tree.map(lambda a, b: jnp.where(reached, a, b), new, before)

    return lax.fori_loop(0, count, hop, start)


def contract(left_side, right_side, left_dim, right_dim):
    return lax.dot_general(
        left_side,
        right_side,
        (((left_dim,), (right_dim,)), ((), ())),
        preferred_element_type=jnp.float32,
    )


def silu_grad(values):
    sigmoid_v = jax.nn.sigmoid(values)
    return sigmoid_v * (1.0 + values * (1.0 - sigmoid_v))


def decay_table(log_block):
    running = jnp.cumsum(log_block, axis=0)
    length = log_block.shape[0]
    row_ids = lax.broadcasted_iota(jnp.int32, (length, length), 0)
    col_ids = lax.broadcasted_iota(jnp.int32, (length, length), 1)
    log_gap = running.T[:, :, None] - running.T[:, None, :]
    decays = jnp.exp(jnp.where((col_ids <= row_ids)[None], log_gap, -1e30))
    return (running, decays)


def block_forward(x_block, b_block, c_block, step_block, log_block, start_state, skip_gain):
    per_group = x_block.shape[1] // b_block.shape[1]
    x_wide = x_block.astype(jnp.float32)
    b_wide = b_block.astype(jnp.float32)
    c_wide = c_block.astype(jnp.float32)
    b_heads = jnp.repeat(b_wide, per_group, axis=1)
    c_heads = jnp.repeat(c_wide, per_group, axis=1)
    running, decays = decay_table(log_block)
    scores = jnp.einsum("ign,jgn->gij", c_block, b_block, preferred_element_type=jnp.float32)
    mixing = jnp.repeat(scores, per_group, axis=0) * decays * step_block.T[:, None, :]
    inside = jnp.einsum("hij,jhp->ihp", mixing, x_wide, precision=HIGH_PRECISION)
    from_state = jnp.exp(running)[:, :, None] * jnp.einsum(
        "ihn,hpn->ihp", c_heads, start_state, precision=HIGH_PRECISION
    )
    output = inside + from_state + skip_gain[None, :, None] * x_wide
    remain = jnp.exp(running[-1][None, :] - running) * step_block
    end_state = jnp.exp(running[-1])[:, None, None] * start_state + jnp.einsum(
        "jh,jhp,jhn->hpn", remain, x_wide, b_heads, precision=HIGH_PRECISION
    )
    return (output, end_state)


def block_backward(
    x_block,
    b_block,
    c_block,
    step_block,
    log_block,
    start_state,
    skip_gain,
    grad_y,
    ssm_out,
    after_state,
):
    group_count = b_block.shape[1]
    per_group = x_block.shape[1] // group_count
    length = x_block.shape[0]
    x_wide = x_block.astype(jnp.float32)
    b_wide = b_block.astype(jnp.float32)
    c_wide = c_block.astype(jnp.float32)
    b_heads = jnp.repeat(b_wide, per_group, axis=1)
    c_heads = jnp.repeat(c_wide, per_group, axis=1)
    running, decays = decay_table(log_block)
    scores = jnp.einsum("ign,jgn->gij", c_block, b_block, preferred_element_type=jnp.float32)
    weighted = jnp.repeat(scores, per_group, axis=0) * decays
    remain = jnp.exp(running[-1][None, :] - running)
    back_b = jnp.einsum("hit,ihp->thp", weighted, grad_y, precision=HIGH_PRECISION)
    back_b = back_b + remain[:, :, None] * jnp.einsum(
        "thn,hpn->thp", b_heads, after_state, precision=HIGH_PRECISION
    )
    grad_x = skip_gain[None, :, None] * grad_y + step_block[:, :, None] * back_b
    x_back = jnp.sum(x_wide * back_b, axis=2)
    grad_cum = jnp.sum(grad_y * ssm_out, axis=2) - step_block * x_back
    pair_terms = (
        decays
        * jnp.einsum("ihp,jhp->hij", grad_y, x_wide, precision=HIGH_PRECISION)
        * step_block.T[:, None, :]
    )
    group_terms = pair_terms.reshape(group_count, per_group, length, length).sum(axis=1)
    state_c = jnp.exp(running)[:, :, None] * jnp.einsum(
        "ihp,hpn->ihn", grad_y, start_state, precision=HIGH_PRECISION
    )
    grad_c = jnp.einsum(
        "gij,jgn->ign", group_terms, b_wide, precision=HIGH_PRECISION
    ) + state_c.reshape(length, group_count, per_group, -1).sum(axis=2)
    state_b = (step_block * remain)[:, :, None] * jnp.einsum(
        "jhp,hpn->jhn", x_wide, after_state, precision=HIGH_PRECISION
    )
    grad_b = jnp.einsum(
        "gij,ign->jgn", group_terms, c_wide, precision=HIGH_PRECISION
    ) + state_b.reshape(length, group_count, per_group, -1).sum(axis=2)
    before = jnp.exp(running[-1])[:, None, None] * after_state + jnp.einsum(
        "ih,ihp,ihn->hpn", jnp.exp(running), grad_y, c_heads, precision=HIGH_PRECISION
    )
    return (grad_x, grad_b, grad_c, x_back, grad_cum, before)


def conv_rims(values, shift_by):
    return passed_along(values, "tm", shift_by)


def link_states(earlier_part, later_part):
    return (
        earlier_part[0] + later_part[0],
        jnp.exp(later_part[0])[:, None, None] * earlier_part[1] + later_part[1],
    )


def fold(last_logs, states, keep, backward):
    position = lax.axis_index("tm")
    count = states.shape[0]
    before = jnp.zeros(states.shape[1:], jnp.float32)
    out = [None] * count
    order = range(count - 1, -1, -1) if backward else range(count)
    for at in order:
        out[at] = before
        scale = jnp.exp(last_logs[at])
        scale = scale.reshape(scale.shape + (1,) * (states.ndim - 1 - scale.ndim))
        before = scale * before + states[at].astype(jnp.float32)
    every = jnp.stack(out)
    if keep:
        return lax.dynamic_index_in_dim(every, position, 0, keepdims=False)
    return every


def spread(x):
    count = lax.axis_size("tm")
    return lax.all_to_all(jnp.broadcast_to(x[None], (count,) + x.shape), "tm", 0, 0)


def state_pass(summary, backward):
    count = lax.axis_size("tm")
    last_logs, own = summary
    if not backward:
        every = spread(own.astype(jnp.bfloat16))
        return fold(last_logs, every, True, False)
    heads, size, width = own.shape
    cut = own.reshape(heads, count, size // count, width).transpose(1, 0, 2, 3)
    cut = lax.all_to_all(cut, "tm", 0, 0)
    back = lax.all_to_all(fold(last_logs, cut, False, True), "tm", 0, 0)
    return back.transpose(1, 0, 2, 3).reshape(heads, size, width)


def summed(values, axis):
    count = lax.axis_size(axis)
    cut = values.astype(jnp.bfloat16).reshape((count, values.shape[0] // count) + values.shape[1:])
    return jnp.sum(lax.all_to_all(cut, axis, 0, 0).astype(jnp.float32), axis=0)


def channel_total(values):
    return lax.psum(values, "head")


def head_partials(values):
    return summed(values, "head")


def body(
    series,
    in_weight,
    step_weight,
    step_bias,
    log_rate,
    conv_weight,
    conv_bias,
    skip_gain,
    norm_gain,
    out_weight,
    cotangent,
):
    row_count = series.shape[0]
    model_width = series.shape[1]
    inner_width = in_weight.shape[2]
    head_count = step_weight.shape[1]
    head_size = inner_width // head_count
    group_count = inner_width // (2 * N)
    per_group = head_count // group_count
    block_count = row_count // BLOCK
    margin = KW - 1
    w_flat = in_weight.reshape(model_width, 3 * inner_width)
    projected = (
        jnp.dot(series, w_flat, preferred_element_type=jnp.float32)
        .astype(jnp.bfloat16)
        .reshape(row_count, 3, inner_width)
    )
    pre_conv = projected[:, 1:, :]
    upper_rim = conv_rims(pre_conv[row_count - margin :].astype(jnp.float32), 1)
    pre_wide = jnp.concatenate([upper_rim, pre_conv.astype(jnp.float32)], axis=0)
    conv_out = conv_bias[None] + conv_weight[0][None] * pre_wide[0:row_count]
    for offset in range(1, KW):
        conv_out = conv_out + conv_weight[offset][None] * pre_wide[offset : offset + row_count]
    activated = jax.nn.silu(conv_out)
    x_heads = activated[:, 0].astype(jnp.bfloat16).reshape(row_count, head_count, head_size)
    bc_values = activated[:, 1].astype(jnp.bfloat16).reshape(row_count, group_count, 2, N)
    b_values = bc_values[:, :, 0]
    c_values = bc_values[:, :, 1]
    gate_raw = projected[:, 0].astype(jnp.float32)
    step_raw = jnp.dot(series, step_weight, preferred_element_type=jnp.float32)
    step_size = jax.nn.softplus(step_raw + step_bias[None])
    decay_rates = jnp.exp(log_rate)
    log_decay = -step_size * decay_rates[None]
    x_wide = x_heads.astype(jnp.float32)
    running = jnp.cumsum(log_decay, axis=0)
    last_log = running[-1]
    own_state = jnp.einsum(
        "lh,lhp,lhn->hpn",
        jnp.exp(last_log[None] - running) * step_size,
        x_wide,
        jnp.repeat(b_values.astype(jnp.float32), per_group, axis=1),
        precision=HIGHEST_PRECISION,
    )
    last_logs = spread(last_log)
    incoming = state_pass((last_logs, own_state), False)
    blocked = (
        x_heads.reshape(block_count, BLOCK, head_count, head_size),
        b_values.reshape(block_count, BLOCK, group_count, N),
        c_values.reshape(block_count, BLOCK, group_count, N),
        step_size.reshape(block_count, BLOCK, head_count),
        log_decay.reshape(block_count, BLOCK, head_count),
    )

    def forward_step(carried, pieces):
        output, end_state = block_forward(
            pieces[0], pieces[1], pieces[2], pieces[3], pieces[4], carried, skip_gain
        )
        return (end_state, (output, carried))

    final_state, (outputs, starts) = lax.scan(forward_step, incoming, blocked)
    y_flat = outputs.reshape(row_count, inner_width)
    gate_act = jax.nn.silu(gate_raw)
    gated_out = y_flat * gate_act
    grad_normed = jnp.dot(cotangent, out_weight, preferred_element_type=jnp.float32)
    gain_grad = norm_gain[None] * grad_normed
    square_sum, inner_sum = channel_total(
        (jnp.sum(gated_out * gated_out, axis=1), jnp.sum(gated_out * gain_grad, axis=1))
    )
    inv_rms = lax.rsqrt(square_sum / E + NORM_EPSILON)
    normed = (gated_out * inv_rms[:, None] * norm_gain[None]).astype(jnp.bfloat16)
    layer_out = head_partials(contract(normed, out_weight, 1, 1)).astype(jnp.bfloat16)
    grad_out = contract(cotangent, normed, 0, 0)
    grad_gated = inv_rms[:, None] * gain_grad - gated_out * (inv_rms**3 * inner_sum / E)[:, None]
    grad_y = (grad_gated * gate_act).reshape(row_count, head_count, head_size)
    grad_gate = grad_gated * y_flat * silu_grad(gate_raw)
    own_back = jnp.einsum(
        "lh,lhp,lhn->hpn",
        jnp.exp(running),
        grad_y,
        jnp.repeat(c_values.astype(jnp.float32), per_group, axis=1),
        precision=HIGHEST_PRECISION,
    )
    after_in = state_pass((last_logs, own_back), True)
    ssm_out = outputs - skip_gain[None, None, :, None] * x_wide.reshape(
        block_count, BLOCK, head_count, head_size
    )
    back_inputs = blocked + (
        starts,
        grad_y.reshape(block_count, BLOCK, head_count, head_size),
        ssm_out,
    )

    def backward_step(carried, pieces):
        grad_x, grad_b, grad_c, x_back, grad_cum, before = block_backward(
            pieces[0],
            pieces[1],
            pieces[2],
            pieces[3],
            pieces[4],
            pieces[5],
            skip_gain,
            pieces[6],
            pieces[7],
            carried,
        )
        return (before, (grad_x, grad_b, grad_c, x_back, grad_cum))

    _, (grad_x, grad_b, grad_c, x_back, grad_cum) = lax.scan(
        backward_step, after_in, back_inputs, reverse=True
    )
    grad_cum = grad_cum.reshape(row_count, head_count)
    grad_log = (
        lax.cumsum(grad_cum, axis=0, reverse=True)
        + jnp.sum(after_in * final_state, axis=(1, 2))[None]
    )
    grad_step = x_back.reshape(row_count, head_count) - decay_rates[None] * grad_log
    grad_raw = (grad_step * jax.nn.sigmoid(step_raw + step_bias[None])).astype(jnp.bfloat16)
    grad_bc = jnp.stack(
        [grad_b.reshape(row_count, group_count, N), grad_c.reshape(row_count, group_count, N)],
        axis=2,
    ).reshape(row_count, inner_width)
    grad_act = jnp.stack([grad_x.reshape(row_count, inner_width), grad_bc], axis=1)
    grad_conv = grad_act * silu_grad(conv_out)
    lower_rim = conv_rims(grad_conv[:margin], -1)
    grad_wide = jnp.concatenate([grad_conv, lower_rim], axis=0)
    grad_pre = conv_weight[0][None] * grad_wide[margin : margin + row_count]
    for offset in range(1, KW):
        grad_pre = (
            grad_pre
            + conv_weight[offset][None] * grad_wide[margin - offset : margin - offset + row_count]
        )
    grad_proj = (
        jnp.concatenate([grad_gate[:, None], grad_pre], axis=1)
        .astype(jnp.bfloat16)
        .reshape(row_count, 3 * inner_width)
    )
    grad_in = contract(series, grad_proj, 0, 0).reshape(model_width, 3, inner_width)
    grad_dt = contract(series, grad_raw, 0, 0)
    grad_rows = contract(grad_proj, w_flat, 1, 1) + contract(grad_raw, step_weight, 1, 1)
    series_grad = head_partials(grad_rows)
    w_in_grad, w_dt_grad, w_out_grad = (
        summed(grad_in, "tm"),
        summed(grad_dt, "tm"),
        summed(grad_out, "tm"),
    )
    return (layer_out, series_grad, w_in_grad, w_dt_grad, w_out_grad)


def solution(mesh):
    in_specs = (
        P("tm", None),
        P(None, None, "head"),
        P(None, "head"),
        P("head"),
        P("head"),
        P(None, None, "head"),
        P(None, "head"),
        P("head"),
        P("head"),
        P(None, "head"),
        P("tm", None),
    )
    out_specs = (
        P(("tm", "head"), None),
        P(("tm", "head"), None),
        P("tm", None, "head"),
        P("tm", "head"),
        P("tm", "head"),
    )
    return jax.shard_map(body, mesh=mesh, in_specs=in_specs, out_specs=out_specs, check_vma=False)
```

```python
import functools

import jax
import jax.numpy as jnp
from jax import lax
from jax.experimental import pallas as pl
from jax.experimental.pallas import tpu as pltpu
from jax.sharding import PartitionSpec as P

N = 128
KW = 4
RIM = 16
LOGS = 16
NORM_EPSILON = 1e-05

F32 = jnp.float32
BF16 = jnp.bfloat16
NN = (((1,), (0,)), ((), ()))
NT = (((1,), (1,)), ((), ()))
TN = (((0,), (0,)), ((), ()))


def mm(a, b, dims=NN):
    return lax.dot_general(a.astype(BF16), b.astype(BF16), dims, preferred_element_type=F32)


def mm_exact(a, b, dims=NN):
    return lax.dot_general(
        a, b, dims, precision=lax.Precision.HIGHEST, preferred_element_type=F32
    )


def lanes_of(shape):
    return lax.broadcasted_iota(jnp.int32, shape, len(shape) - 1)


def rows_of(shape):
    return lax.broadcasted_iota(jnp.int32, shape, len(shape) - 2)


def per_row(ref, shape):
    rows = rows_of(shape)
    out = jnp.full(shape, ref[0], F32)
    for h in range(1, shape[0]):
        out = jnp.where(rows == h, ref[h], out)
    return out


def per_lane(ref, heads, width):
    head = lanes_of((1, width)) // (width // heads)
    out = jnp.full((1, width), ref[0], F32)
    for h in range(1, heads):
        out = jnp.where(head == h, ref[h], out)
    return out


def widen(cols, heads, width):
    head = lanes_of((cols.shape[0], width)) // (width // heads)
    out = jnp.broadcast_to(cols[:, 0:1], (cols.shape[0], width))
    for h in range(1, heads):
        out = jnp.where(head == h, cols[:, h : h + 1], out)
    return out


def head_mask(heads, width):
    shape = (8, width)
    return jnp.where(lanes_of(shape) // (width // heads) == rows_of(shape), 1.0, 0.0)


def only_head(x, h, heads):
    width = x.shape[1]
    return jnp.where(lanes_of(x.shape) // (width // heads) == h, x, jnp.zeros_like(x))


def columns(rows):
    short = -rows.shape[0] % 8
    if short:
        rows = jnp.concatenate([rows, jnp.zeros((short, rows.shape[1]), F32)], axis=0)
    return jnp.transpose(rows)


def sigmoid(v):
    return 1.0 / (1.0 + jnp.exp(-v))


def running_sum(x):
    width = x.shape[1]
    lanes = lanes_of(x.shape)
    hop = 1
    while hop < width:
        x = x + jnp.where(lanes >= hop, pltpu.roll(x, hop, 1), 0.0)
        hop *= 2
    return x


def running_sum_back(x):
    width = x.shape[1]
    lanes = lanes_of(x.shape)
    hop = 1
    while hop < width:
        x = x + jnp.where(lanes < width - hop, pltpu.roll(x, width - hop, 1), 0.0)
        hop *= 2
    return x


def decay_of(cols, rows, h):
    length = cols.shape[0]
    gap = cols[:, h : h + 1] - rows[h : h + 1, :]
    shape = (length, length)
    return jnp.exp(jnp.where(lanes_of(shape) <= rows_of(shape), gap, -1e30))


def fold(count, position, msg_ref, log_ref, heads, back):
    size = log_ref.shape[1] - LOGS

    def step(at, before):
        logs = log_ref[at, size:, :].astype(F32)
        logs = logs[0:heads] + logs[heads : 2 * heads] + logs[2 * heads : 3 * heads]
        scale = jnp.exp(logs)
        scale = jnp.concatenate(
            [jnp.broadcast_to(scale[h : h + 1], (size // heads, N)) for h in range(heads)], axis=0
        )
        new = scale * before + msg_ref[at, 0:size, :].astype(F32)
        reached = at > position if back else at < position
        return jnp.where(reached, new, before)

    before = jnp.zeros((size, N), F32)
    if count <= 8:
        for k in range(count):
            before = step(count - 1 - k if back else k, before)
        return before
    return lax.fori_loop(0, count, lambda k, b: step(count - 1 - k if back else k, b), before)


def project_kernel(heads, series, w, dtw, bias, rate, gate, pre, scal):
    width = w.shape[2]
    s = series[...]
    gate[...] = mm(s, w[0]).astype(BF16)
    pre[:, 0:width] = mm(s, w[1]).astype(BF16)
    pre[:, width:] = mm(s, w[2]).astype(BF16)
    raw = mm(dtw[...], s, NT)
    shifted = raw + per_row(bias, raw.shape)
    step = jnp.maximum(shifted, 0.0) + jnp.log1p(jnp.exp(-jnp.abs(shifted)))
    running = running_sum(-step * jnp.exp(per_row(rate, raw.shape)))
    scal[0:heads, :] = running
    scal[heads : 2 * heads, :] = step
    scal[2 * heads : 3 * heads, :] = sigmoid(shifted)
    scal[3 * heads :, :] = jnp.zeros_like(running)


def conv_kernel(heads, count, pre, rim, w, cw, cb, scal, x, bc, conv, own, msg, wide):
    length, both = pre.shape
    width = both // 2
    for s in range(2):
        cut = slice(s * width, (s + 1) * width)
        rims = mm(rim[...], w[1 + s]).astype(BF16).astype(F32)
        wide[0:8, cut] = rims[RIM - 8 :, :]
        wide[8:, cut] = pre[:, cut].astype(F32)
        acc = cb[s : s + 1, :] + cw[0, s : s + 1, :] * wide[5 : 5 + length, cut]
        for k in range(1, KW):
            acc = acc + cw[k, s : s + 1, :] * wide[5 + k : 5 + k + length, cut]
        conv[:, cut] = acc
        act = (acc * sigmoid(acc)).astype(BF16)
        if s == 0:
            x[...] = act
        else:
            bc[...] = act
    running = scal[0:heads, :]
    last = running[:, length - 1 : length]
    remain = jnp.exp(last - running) * scal[heads : 2 * heads, :]
    scaled = x[...].astype(F32) * widen(columns(remain), heads, width)
    state = mm(scaled, bc[:, 0:N], TN)
    own[...] = state
    last = jnp.broadcast_to(last, (heads, N))
    high = last.astype(BF16).astype(F32)
    middle = (last - high).astype(BF16).astype(F32)
    low = last - high - middle
    logs = jnp.concatenate([high, middle, low, jnp.zeros_like(low)], axis=0)
    state = state.astype(BF16)
    logs = logs.astype(BF16)
    for at in range(count):
        msg[at, 0:width, :] = state
        msg[at, width:, :] = logs


def inside_kernel(heads, x, bc, scal, skip, cot, ow, gain, y, gg):
    length, width = x.shape
    xv = x[...].astype(F32)
    rows = scal[...]
    cols = columns(rows)
    scores = mm(bc[:, N:], bc[:, 0:N], NT)
    acc = per_lane(skip, heads, width) * xv
    for h in range(heads):
        mixing = scores * decay_of(cols, rows, h) * rows[heads + h : heads + h + 1, :]
        acc = acc + mm(mixing, only_head(xv, h, heads))
    y[...] = acc
    gg[...] = gain[...] * mm(cot[...], ow[...])


def join_kernel(heads, count, pos, msg, yi, gg, gate, bc, scal, y, sin, sums):
    length, width = yi.shape
    start = fold(count, pos[0], msg, msg, heads, False)
    sin[...] = start
    grow = widen(columns(jnp.exp(scal[0:heads, :])), heads, width)
    yv = yi[...] + grow * mm(bc[:, N:], start, NT)
    y[...] = yv
    g = gate[...].astype(F32)
    gated = yv * (g * sigmoid(g))
    ones = jnp.ones((8, width), F32)
    square = mm_exact(ones, gated * gated, NT)
    inner = mm_exact(ones, gated * gg[...], NT)
    sums[...] = jnp.where(rows_of(square.shape) == 0, square, inner)


def norm_columns(total, every):
    inv = lax.rsqrt(total[0:1, :] / every + NORM_EPSILON)
    coef = inv * inv * inv * total[1:2, :] / every
    return columns(jnp.concatenate([inv, coef], axis=0))


def grad_y_kernel(heads, count, every, total, y, gate, gg, bc, scal, gy, msg):
    length, width = y.shape
    cols = norm_columns(total[...], every)
    g = gate[...].astype(F32)
    act = g * sigmoid(g)
    gated = y[...] * act
    grad = (cols[:, 0:1] * gg[...] - gated * cols[:, 1:2]) * act
    gy[...] = grad
    grow = widen(columns(jnp.exp(scal[0:heads, :])), heads, width)
    back = mm(grad * grow, bc[:, N:], TN).astype(BF16)
    for at in range(count):
        msg[at] = back


def beside_kernel(
    heads, count, parts, every,
    total, y, gate, gg, gain, gy, x, bc, scal, sin, cot, ow, series, w,
    lo_msg, wo_msg, sg, bb, gb, gc,
):
    length, width = y.shape
    depth = series.shape[1]
    cols = norm_columns(total[...], every)
    g = gate[...].astype(F32)
    sig = sigmoid(g)
    act = g * sig
    yv = y[...]
    gated = yv * act
    normed = (gated * cols[:, 0:1] * gain[...]).astype(BF16)
    out = mm(normed, ow[...], NT).astype(BF16)
    piece = length // parts
    for at in range(parts):
        lo_msg[at] = out[at * piece : (at + 1) * piece, :]
    grad_gated = cols[:, 0:1] * gg[...] - gated * cols[:, 1:2]
    grad_gate = (grad_gated * yv * (sig * (1.0 + g * (1.0 - sig)))).astype(BF16)
    sg[...] = mm(grad_gate, w[0], NT)
    w_out = mm(cot[...], normed, TN).astype(BF16)
    w_gate = mm(series[...], grad_gate, TN).astype(BF16)
    piece = depth // count
    for at in range(count):
        wo_msg[at, :, 0:width] = w_out[at * piece : (at + 1) * piece, :]
        wo_msg[at, :, width:] = w_gate[at * piece : (at + 1) * piece, :]
    rows = scal[...]
    cols = columns(rows)
    xv = x[...].astype(F32)
    gyv = gy[...]
    b, c = bc[:, 0:N], bc[:, N:]
    scores = mm(c, b, NT)
    back = jnp.zeros((length, width), F32)
    group = jnp.zeros((length, length), F32)
    for h in range(heads):
        decay = decay_of(cols, rows, h)
        gh = only_head(gyv, h, heads)
        back = back + mm(scores * decay, gh, TN)
        group = group + decay * mm(gh, xv, NT) * rows[heads + h : heads + h + 1, :]
    bb[...] = back
    gb[...] = mm(group, c, TN)
    grow = widen(columns(jnp.exp(rows[0:heads])), heads, width)
    gc[...] = mm(group, b) + mm(gyv * grow, sin[...])


def close_kernel(
    heads, count,
    pos, msg, log_msg, x, bc, scal, gy, y, bb, gb, gc, sin, own, conv, series, rim, cw, skip, rate,
    wi_msg, dt_msg, gp, edge, graw, wide,
):
    length, width = y.shape
    depth = series.shape[1]
    after = fold(count, pos[0], msg, log_msg, heads, True)
    rows = scal[...]
    running, step = rows[0:heads], rows[heads : 2 * heads]
    last = running[:, length - 1 : length]
    remain = jnp.exp(last - running)
    cols = columns(jnp.concatenate([remain, step, remain * step], axis=0))
    xv = x[...].astype(F32)
    gyv = gy[...]
    skips = per_lane(skip, heads, width)
    back = bb[...] + widen(cols, heads, width) * mm(bc[:, 0:N], after, NT)
    grad_x = skips * gyv + widen(cols[:, heads:], heads, width) * back
    mask = head_mask(heads, width)
    x_back = mm_exact(mask, xv * back, NT)[0:heads]
    y_back = mm_exact(mask, gyv * (y[...] - skips * xv), NT)[0:heads]
    whole = jnp.concatenate(
        [jnp.broadcast_to(last[h : h + 1], (width // heads, N)) for h in range(heads)], axis=0
    )
    final = jnp.exp(whole) * sin[...] + own[...]
    ends = jnp.sum(mm_exact(mask, after * final), axis=1, keepdims=True)[0:heads]
    grad_log = running_sum_back(y_back - step * x_back) + ends
    grad_step = x_back - jnp.exp(per_row(rate, x_back.shape)) * grad_log
    grad_raw = grad_step * rows[2 * heads : 3 * heads]
    grad_raw = jnp.concatenate([grad_raw, jnp.zeros_like(grad_raw)], axis=0)
    graw[...] = grad_raw
    dt = mm(grad_raw, series[...])
    piece = depth // count
    for at in range(count):
        dt_msg[at] = dt[:, at * piece : (at + 1) * piece]
    grad_b = gb[...] + mm(xv * widen(cols[:, 2 * heads :], heads, width), after)
    zeros = jnp.zeros((RIM, 2 * width), F32)
    wide[0:RIM, :] = zeros
    wide[RIM + length :, :] = zeros[0:8]
    for cut, grad in (
        (slice(0, width), grad_x),
        (slice(width, width + N), grad_b),
        (slice(width + N, 2 * width), gc[...]),
    ):
        v = conv[:, cut]
        sig = sigmoid(v)
        wide[RIM : RIM + length, cut] = grad * (sig * (1.0 + v * (1.0 - sig)))
    for s in range(2):
        cut = slice(s * width, (s + 1) * width)
        acc = cw[0, s : s + 1, :] * wide[KW - 1 : KW - 1 + RIM + length, cut]
        for k in range(1, KW):
            low = KW - 1 - k
            acc = acc + cw[k, s : s + 1, :] * wide[low : low + RIM + length, cut]
        acc = acc.astype(BF16)
        edge[:, cut] = acc[0:RIM]
        gp[:, cut] = acc[RIM:]
        grad_w = (mm(series[...], acc[RIM:], TN) + mm(rim[...], acc[0:RIM], TN)).astype(BF16)
        for at in range(count):
            wi_msg[at, :, cut] = grad_w[at * piece : (at + 1) * piece, :]


def rows_kernel(parts, sg, gp, graw, edge, w, dtw, msg):
    length = gp.shape[0]
    width = w.shape[2]
    heads = dtw.shape[0]
    total = sg[...] + mm(graw[0:heads, :], dtw[...], TN)
    total = total + mm(gp[:, 0:width], w[1], NT) + mm(gp[:, width:], w[2], NT)
    late = mm(edge[:, 0:width], w[1], NT) + mm(edge[:, width:], w[2], NT)
    piece = length // parts
    for at in range(parts - 1):
        msg[at] = total[at * piece : (at + 1) * piece, :].astype(BF16)
    tail = total[(parts - 1) * piece :, :]
    late = jnp.concatenate([jnp.zeros((piece - RIM, late.shape[1]), F32), late], axis=0)
    msg[parts - 1] = (tail + late).astype(BF16)


def total_kernel(count, width, wo, wi, w_in, w_out):
    def sum_of(ref, cut):
        acc = ref[0, :, cut].astype(F32)
        if count <= 8:
            for at in range(1, count):
                acc = acc + ref[at, :, cut].astype(F32)
            return acc
        return lax.fori_loop(1, count, lambda at, a: a + ref[at, :, cut].astype(F32), acc)

    w_out[...] = sum_of(wo, slice(0, width))
    w_in[0] = sum_of(wo, slice(width, 2 * width))
    w_in[1] = sum_of(wi, slice(0, width))
    w_in[2] = sum_of(wi, slice(width, 2 * width))


VMEM = pl.BlockSpec(memory_space=pltpu.VMEM)
SMEM = pl.BlockSpec(memory_space=pltpu.SMEM)


def run(kernel, name, outs, args, scalars=(), scratch=(), flops=10**8):
    moved = sum(a.size * a.dtype.itemsize for a in args)
    return pl.pallas_call(
        kernel,
        name=name,
        out_shape=[jax.ShapeDtypeStruct(shape, kind) for shape, kind in outs],
        in_specs=[SMEM if i in scalars else VMEM for i in range(len(args))],
        out_specs=[VMEM] * len(outs),
        scratch_shapes=list(scratch),
        compiler_params=pltpu.CompilerParams(vmem_limit_bytes=40 * 2**20),
        cost_estimate=pl.CostEstimate(flops=flops, bytes_accessed=2 * moved, transcendentals=0),
    )(*args)


def shifted(block, axis, distance):
    devices = range(lax.axis_size(axis))
    route = [(i - distance, i) for i in devices if i - distance in devices]
    return lax.ppermute(block, axis, route)


def exchange(blocks, axis):
    return lax.all_to_all(blocks, axis, 0, 0)


def body(
    series,
    in_weight,
    step_weight,
    step_bias,
    log_rate,
    conv_weight,
    conv_bias,
    skip_gain,
    norm_gain,
    out_weight,
    cotangent,
):
    length, depth = series.shape
    width = in_weight.shape[2]
    heads = step_weight.shape[1]
    count = lax.axis_size("tm")
    parts = lax.axis_size("head")
    every = width * parts
    assert width == 2 * N and heads == 4
    part = functools.partial
    w = in_weight.transpose(1, 0, 2)
    dtw = step_weight.T
    gain = norm_gain.reshape(1, width)
    position = lax.axis_index("tm").astype(jnp.int32).reshape(1)
    rim = shifted(series[length - RIM :], "tm", 1)

    gate, pre, scal = run(
        part(project_kernel, heads), "project",
        [((length, width), BF16), ((length, 2 * width), BF16), ((4 * heads, length), F32)],
        [series, w, dtw, step_bias, log_rate], (3, 4),
    )
    x, bc, conv, own, msg = run(
        part(conv_kernel, heads, count), "conv",
        [
            ((length, width), BF16),
            ((length, width), BF16),
            ((length, 2 * width), F32),
            ((width, N), F32),
            ((count, width + LOGS, N), BF16),
        ],
        [pre, rim, w, conv_weight, conv_bias, scal],
        scratch=[pltpu.VMEM((length + 8, 2 * width), F32)],
    )
    msg = exchange(msg, "tm")
    inside, gg = run(
        part(inside_kernel, heads), "inside",
        [((length, width), F32), ((length, width), F32)],
        [x, bc, scal, skip_gain, cotangent, out_weight, gain], (3,),
    )
    y, sin, sums = run(
        part(join_kernel, heads, count), "join",
        [((length, width), F32), ((width, N), F32), ((8, length), F32)],
        [position, msg, inside, gg, gate, bc, scal], (0,),
    )
    total = lax.psum(sums, "head")
    gy, back = run(
        part(grad_y_kernel, heads, count, every), "grad_y",
        [((length, width), F32), ((count, width, N), BF16)],
        [total, y, gate, gg, bc, scal],
    )
    back = exchange(back, "tm")
    lo_msg, wo_msg, sg, bb, gb, gc = run(
        part(beside_kernel, heads, count, parts, every), "beside",
        [
            ((parts, length // parts, depth), BF16),
            ((count, depth // count, 2 * width), BF16),
            ((length, depth), F32),
            ((length, width), F32),
            ((length, N), F32),
            ((length, N), F32),
        ],
        [total, y, gate, gg, gain, gy, x, bc, scal, sin, cotangent, out_weight, series, w],
    )
    lo_msg = exchange(lo_msg, "head")
    layer_out = jnp.sum(lo_msg.astype(F32), axis=0).astype(BF16)
    wo_msg = exchange(wo_msg, "tm")
    wi_msg, dt_msg, gp, edge, graw = run(
        part(close_kernel, heads, count), "close",
        [
            ((count, depth // count, 2 * width), BF16),
            ((count, 2 * heads, depth // count), F32),
            ((length, 2 * width), BF16),
            ((RIM, 2 * width), BF16),
            ((2 * heads, length), F32),
        ],
        [
            position, back, msg, x, bc, scal, gy, y, bb, gb, gc, sin, own, conv, series, rim,
            conv_weight, skip_gain, log_rate,
        ],
        (0, 17, 18),
        scratch=[pltpu.VMEM((length + RIM + 8, 2 * width), F32)],
    )
    wi_msg = exchange(wi_msg, "tm")
    edge = shifted(edge, "tm", -1)
    (sg_msg,) = run(
        part(rows_kernel, parts), "rows",
        [((parts, length // parts, depth), BF16)],
        [sg, gp, graw, edge, w, dtw],
    )
    sg_msg = exchange(sg_msg, "head")
    series_grad = jnp.sum(sg_msg.astype(F32), axis=0)
    dt_msg = exchange(dt_msg, "tm")
    w_dt_grad = jnp.sum(dt_msg, axis=0)[0:heads].T
    w_in_grad, w_out_grad = run(
        part(total_kernel, count, width), "total",
        [((3, depth // count, width), F32), ((depth // count, width), F32)],
        [wo_msg, wi_msg],
    )
    return (layer_out, series_grad, w_in_grad.transpose(1, 0, 2), w_dt_grad, w_out_grad)


def solution(mesh):
    in_specs = (
        P("tm", None),
        P(None, None, "head"),
        P(None, "head"),
        P("head"),
        P("head"),
        P(None, None, "head"),
        P(None, "head"),
        P("head"),
        P("head"),
        P(None, "head"),
        P("tm", None),
    )
    out_specs = (
        P(("tm", "head"), None),
        P(("tm", "head"), None),
        P("tm", None, "head"),
        P("tm", "head"),
        P("tm", "head"),
    )
    return jax.shard_map(body, mesh=mesh, in_specs=in_specs, out_specs=out_specs, check_vma=False)
```

```python
import functools

import jax
import jax.numpy as jnp
from jax import lax
from jax.experimental import pallas as pl
from jax.experimental.pallas import tpu as pltpu
from jax.sharding import PartitionSpec as P

N = 128
KW = 4
RIM = 16
LOGS = 16
NORM_EPSILON = 1e-05

F32 = jnp.float32
BF16 = jnp.bfloat16
NN = (((1,), (0,)), ((), ()))
NT = (((1,), (1,)), ((), ()))
TN = (((0,), (0,)), ((), ()))


def mm(a, b, dims=NN):
    return lax.dot_general(a.astype(BF16), b.astype(BF16), dims, preferred_element_type=F32)


def mm_exact(a, b, dims=NN):
    return lax.dot_general(
        a, b, dims, precision=lax.Precision.HIGHEST, preferred_element_type=F32
    )


def lanes_of(shape):
    return lax.broadcasted_iota(jnp.int32, shape, len(shape) - 1)


def rows_of(shape):
    return lax.broadcasted_iota(jnp.int32, shape, len(shape) - 2)


def per_row(ref, shape):
    rows = rows_of(shape)
    out = jnp.full(shape, ref[0], F32)
    for h in range(1, shape[0]):
        out = jnp.where(rows == h, ref[h], out)
    return out


def per_lane(ref, heads, width):
    head = lanes_of((1, width)) // (width // heads)
    out = jnp.full((1, width), ref[0], F32)
    for h in range(1, heads):
        out = jnp.where(head == h, ref[h], out)
    return out


def widen(cols, heads, width):
    head = lanes_of((cols.shape[0], width)) // (width // heads)
    out = jnp.broadcast_to(cols[:, 0:1], (cols.shape[0], width))
    for h in range(1, heads):
        out = jnp.where(head == h, cols[:, h : h + 1], out)
    return out


def head_mask(heads, width):
    shape = (8, width)
    return jnp.where(lanes_of(shape) // (width // heads) == rows_of(shape), 1.0, 0.0)


def only_head(x, h, heads):
    width = x.shape[1]
    return jnp.where(lanes_of(x.shape) // (width // heads) == h, x, jnp.zeros_like(x))


def columns(rows):
    short = -rows.shape[0] % 8
    if short:
        rows = jnp.concatenate([rows, jnp.zeros((short, rows.shape[1]), F32)], axis=0)
    return jnp.transpose(rows)


def sigmoid(v):
    return 1.0 / (1.0 + jnp.exp(-v))


def running_sum(x):
    width = x.shape[1]
    lanes = lanes_of(x.shape)
    hop = 1
    while hop < width:
        x = x + jnp.where(lanes >= hop, pltpu.roll(x, hop, 1), 0.0)
        hop *= 2
    return x


def running_sum_back(x):
    width = x.shape[1]
    lanes = lanes_of(x.shape)
    hop = 1
    while hop < width:
        x = x + jnp.where(lanes < width - hop, pltpu.roll(x, width - hop, 1), 0.0)
        hop *= 2
    return x


def decay_of(cols, rows, h):
    length = cols.shape[0]
    gap = cols[:, h : h + 1] - rows[h : h + 1, :]
    shape = (length, length)
    return jnp.exp(jnp.where(lanes_of(shape) <= rows_of(shape), gap, -1e30))


def logs_of(msg, heads):
    logs = msg[msg.shape[0] - LOGS :].astype(F32)
    return logs[0:heads] + logs[heads : 2 * heads] + logs[2 * heads : 3 * heads]


def spread_rows(logs, heads, size):
    return jnp.concatenate(
        [jnp.broadcast_to(logs[h : h + 1], (size // heads, N)) for h in range(heads)], axis=0
    )


def state_of(msg):
    return msg[0 : msg.shape[0] - LOGS].astype(F32)


def packed(state, logs):
    high = logs.astype(BF16).astype(F32)
    middle = (logs - high).astype(BF16).astype(F32)
    low = logs - high - middle
    logs = jnp.concatenate([high, middle, low, jnp.zeros_like(low)], axis=0)
    return jnp.concatenate([state.astype(BF16), logs.astype(BF16)], axis=0)


def carried(own_turn, partner, others, heads):
    state = jnp.zeros((partner.shape[0] - LOGS, N), F32)
    size = state.shape[0]
    for msg in others:
        state = jnp.exp(spread_rows(logs_of(msg, heads), heads, size)) * state + state_of(msg)
    with_partner = jnp.exp(spread_rows(logs_of(partner, heads), heads, size)) * state
    return jnp.where(own_turn, with_partner + state_of(partner), state)


def project_kernel(heads, series, w, dtw, bias, rate, gate, pre, scal):
    width = w.shape[2]
    s = series[...]
    gate[...] = mm(s, w[0]).astype(BF16)
    pre[:, 0:width] = mm(s, w[1]).astype(BF16)
    pre[:, width:] = mm(s, w[2]).astype(BF16)
    raw = mm(dtw[...], s, NT)
    shifted = raw + per_row(bias, raw.shape)
    step = jnp.maximum(shifted, 0.0) + jnp.log1p(jnp.exp(-jnp.abs(shifted)))
    running = running_sum(-step * jnp.exp(per_row(rate, raw.shape)))
    scal[0:heads, :] = running
    scal[heads : 2 * heads, :] = step
    scal[2 * heads : 3 * heads, :] = sigmoid(shifted)
    scal[3 * heads :, :] = jnp.zeros_like(running)


def conv_kernel(heads, pre, rim, w, cw, cb, scal, x, bc, conv, own, msg, wide):
    length, both = pre.shape
    width = both // 2
    for s in range(2):
        cut = slice(s * width, (s + 1) * width)
        rims = mm(rim[...], w[1 + s]).astype(BF16).astype(F32)
        wide[0:8, cut] = rims[RIM - 8 :, :]
        wide[8:, cut] = pre[:, cut].astype(F32)
        acc = cb[s : s + 1, :] + cw[0, s : s + 1, :] * wide[5 : 5 + length, cut]
        for k in range(1, KW):
            acc = acc + cw[k, s : s + 1, :] * wide[5 + k : 5 + k + length, cut]
        conv[:, cut] = acc
        act = (acc * sigmoid(acc)).astype(BF16)
        if s == 0:
            x[...] = act
        else:
            bc[...] = act
    running = scal[0:heads, :]
    last = running[:, length - 1 : length]
    remain = jnp.exp(last - running) * scal[heads : 2 * heads, :]
    scaled = x[...].astype(F32) * widen(columns(remain), heads, width)
    state = mm(scaled, bc[:, 0:N], TN)
    own[...] = state
    msg[...] = packed(state, jnp.broadcast_to(last, (heads, N)))


def pair_kernel(heads, back, low, mine, other, msg):
    mine, other = mine[...], other[...]
    size = mine.shape[0] - LOGS
    mine_first = low[0] == 0
    mine_logs, other_logs = logs_of(mine, heads), logs_of(other, heads)
    crossed = jnp.logical_not(mine_first) if back else mine_first
    mine_scale = jnp.where(crossed, jnp.exp(other_logs), 1.0)
    other_scale = jnp.where(crossed, 1.0, jnp.exp(mine_logs))
    state = spread_rows(mine_scale, heads, size) * state_of(mine)
    state = state + spread_rows(other_scale, heads, size) * state_of(other)
    msg[...] = packed(state, mine_logs + other_logs)


def inside_kernel(heads, x, bc, scal, skip, cot, ow, gain, conv, y, gg, slope):
    length, width = x.shape
    xv = x[...].astype(F32)
    rows = scal[...]
    cols = columns(rows)
    scores = mm(bc[:, N:], bc[:, 0:N], NT)
    acc = per_lane(skip, heads, width) * xv
    for h in range(heads):
        mixing = scores * decay_of(cols, rows, h) * rows[heads + h : heads + h + 1, :]
        acc = acc + mm(mixing, only_head(xv, h, heads))
    y[...] = acc
    gg[...] = gain[...] * mm(cot[...], ow[...])
    v = conv[...]
    sig = sigmoid(v)
    slope[...] = sig * (1.0 + v * (1.0 - sig))


def join_kernel(heads, low, yi, gg, gate, bc, scal, partner, *rest):
    *others, y, sin, sums = rest
    length, width = yi.shape
    start = carried(low[0] == 1, partner[...], [o[...] for o in others], heads)
    sin[...] = start
    grow = widen(columns(jnp.exp(scal[0:heads, :])), heads, width)
    yv = yi[...] + grow * mm(bc[:, N:], start, NT)
    y[...] = yv
    g = gate[...].astype(F32)
    gated = yv * (g * sigmoid(g))
    ones = jnp.ones((8, width), F32)
    square = mm_exact(ones, gated * gated, NT)
    inner = mm_exact(ones, gated * gg[...], NT)
    sums[...] = jnp.where(rows_of(square.shape) == 0, square, inner)


def norm_columns(total, every):
    inv = lax.rsqrt(total[0:1, :] / every + NORM_EPSILON)
    coef = inv * inv * inv * total[1:2, :] / every
    return columns(jnp.concatenate([inv, coef], axis=0))


def grad_y_kernel(heads, every, total, y, gate, gg, bc, scal, gy, msg):
    length, width = y.shape
    cols = norm_columns(total[...], every)
    g = gate[...].astype(F32)
    act = g * sigmoid(g)
    gated = y[...] * act
    grad = (cols[:, 0:1] * gg[...] - gated * cols[:, 1:2]) * act
    gy[...] = grad
    grow = widen(columns(jnp.exp(scal[0:heads, :])), heads, width)
    last = scal[0:heads, length - 1 : length]
    msg[...] = packed(mm(grad * grow, bc[:, N:], TN), jnp.broadcast_to(last, (heads, N)))


def conv_back(cw, wide, cut, length, slot, slot_cut):
    acc = cw[0, slot : slot + 1, slot_cut] * wide[KW - 1 : KW - 1 + RIM + length, cut]
    for k in range(1, KW):
        at = KW - 1 - k
        acc = acc + cw[k, slot : slot + 1, slot_cut] * wide[at : at + RIM + length, cut]
    return acc.astype(BF16)


def clear_ends(wide, length):
    zeros = jnp.zeros((RIM, wide.shape[1]), F32)
    wide[0:RIM, :] = zeros
    wide[RIM + length :, :] = zeros[0:8]


def stack_columns(msg, grad, at, base, piece):
    for q in range(grad.shape[1] // N):
        msg[at, (base + q) * piece : (base + q + 1) * piece, :] = grad[
            at * piece : (at + 1) * piece, q * N : (q + 1) * N
        ]


def split_pair(low, every, keep, send):
    for at in range(keep.shape[0]):
        keep[at] = every[2 * at + low]
        send[at] = every[2 * at + 1 - low]


def beside_kernel(
    heads, count, every,
    low, total, y, gate, gg, gain, gy, x, bc, scal, sin, cot, ow, series, rim, w, cw, slope, skip,
    out, keep, send, sg, bb, gb, edge, yb, wide, stage,
):
    length, width = y.shape
    depth = series.shape[1]
    cols = norm_columns(total[...], every)
    g = gate[...].astype(F32)
    sig = sigmoid(g)
    act = g * sig
    yv = y[...]
    gated = yv * act
    normed = (gated * cols[:, 0:1] * gain[...]).astype(BF16)
    out[...] = mm(normed, ow[...], NT).astype(BF16)
    grad_gated = cols[:, 0:1] * gg[...] - gated * cols[:, 1:2]
    grad_gate = (grad_gated * yv * (sig * (1.0 + g * (1.0 - sig)))).astype(BF16)
    rows = scal[...]
    cols = columns(rows)
    xv = x[...].astype(F32)
    gyv = gy[...]
    b, c = bc[:, 0:N], bc[:, N:]
    scores = mm(c, b, NT)
    back = jnp.zeros((length, width), F32)
    group = jnp.zeros((length, length), F32)
    for h in range(heads):
        decay = decay_of(cols, rows, h)
        gh = only_head(gyv, h, heads)
        back = back + mm(scores * decay, gh, TN)
        group = group + decay * mm(gh, xv, NT) * rows[heads + h : heads + h + 1, :]
    bb[...] = back
    gb[...] = mm(group, c, TN)
    grow = widen(columns(jnp.exp(rows[0:heads])), heads, width)
    grad_c = mm(group, b) + mm(gyv * grow, sin[...])
    yb[...] = mm_exact(head_mask(heads, width), gyv * (yv - per_lane(skip, heads, width) * xv), NT)
    clear_ends(wide, length)
    wide[RIM : RIM + length, :] = grad_c * slope[:, 2 * width - N :]
    grad_pre = conv_back(cw, wide, slice(0, N), length, 1, slice(width - N, width))
    edge[...] = grad_pre[0:RIM]
    sg[...] = mm(grad_gate, w[0], NT) + mm(grad_pre[RIM:], w[2, :, width - N :], NT)
    w_out = mm(cot[...], normed, TN).astype(BF16)
    w_gate = mm(series[...], grad_gate, TN).astype(BF16)
    w_c = (mm(series[...], grad_pre[RIM:], TN) + mm(rim[...], grad_pre[0:RIM], TN)).astype(BF16)
    piece = depth // count
    for at in range(count):
        stack_columns(stage, w_out, at, 0, piece)
        stack_columns(stage, w_gate, at, 2, piece)
        stack_columns(stage, w_c, at, 4, piece)
    split_pair(low[0], stage, keep, send)


def close_kernel(
    heads, count,
    low, x, bc, scal, gy, bb, gb, yb, sin, own, slope, series, rim, cw, skip, rate, partner, *rest,
):
    *others, keep, send, gp, edge, graw, wide, stage = rest
    length, width = gy.shape
    depth = series.shape[1]
    after = carried(low[0] == 0, partner[...], [o[...] for o in others], heads)
    rows = scal[...]
    running, step = rows[0:heads], rows[heads : 2 * heads]
    last = running[:, length - 1 : length]
    remain = jnp.exp(last - running)
    cols = columns(jnp.concatenate([remain, step, remain * step], axis=0))
    xv = x[...].astype(F32)
    back = bb[...] + widen(cols, heads, width) * mm(bc[:, 0:N], after, NT)
    grad_x = per_lane(skip, heads, width) * gy[...] + widen(cols[:, heads:], heads, width) * back
    grad_b = gb[...] + mm(xv * widen(cols[:, 2 * heads :], heads, width), after)
    clear_ends(wide, length)
    wide[RIM : RIM + length, 0:width] = grad_x * slope[:, 0:width]
    wide[RIM : RIM + length, width:] = grad_b * slope[:, width : width + N]
    grad_x = conv_back(cw, wide, slice(0, width), length, 0, slice(0, width))
    grad_b = conv_back(cw, wide, slice(width, width + N), length, 1, slice(0, N))
    edge[:, 0:width] = grad_x[0:RIM]
    edge[:, width:] = grad_b[0:RIM]
    gp[:, 0:width] = grad_x[RIM:]
    gp[:, width:] = grad_b[RIM:]
    w_x = (mm(series[...], grad_x[RIM:], TN) + mm(rim[...], grad_x[0:RIM], TN)).astype(BF16)
    w_b = (mm(series[...], grad_b[RIM:], TN) + mm(rim[...], grad_b[0:RIM], TN)).astype(BF16)
    mask = head_mask(heads, width)
    x_back = mm_exact(mask, xv * back, NT)[0:heads]
    final = jnp.exp(spread_rows(jnp.broadcast_to(last, (heads, N)), heads, width)) * sin[...]
    ends = jnp.sum(mm_exact(mask, after * (final + own[...])), axis=1, keepdims=True)[0:heads]
    grad_log = running_sum_back(yb[0:heads, :] - step * x_back) + ends
    grad_step = x_back - jnp.exp(per_row(rate, x_back.shape)) * grad_log
    grad_raw = grad_step * rows[2 * heads : 3 * heads]
    grad_raw = jnp.concatenate([grad_raw, jnp.zeros_like(grad_raw)], axis=0)
    graw[...] = grad_raw
    dt = mm(grad_raw, series[...])
    piece = depth // count
    blank = jnp.zeros((LOGS, N), F32)
    for at in range(count):
        stack_columns(stage, w_x, at, 0, piece)
        stack_columns(stage, w_b, at, 2, piece)
        dt_piece = jnp.concatenate(
            [dt[:, at * piece : (at + 1) * piece], blank[0 : 2 * heads, 0 : N - piece]], axis=1
        )
        dt_piece = jnp.concatenate([dt_piece, blank[0 : LOGS - 2 * heads]], axis=0)
        stage[at, 3 * piece :, :] = dt_piece.astype(BF16)
    split_pair(low[0], stage, keep, send)


def halve_kernel(high, keep, other, own, *parts):
    at = high[0]
    own[...] = keep[at].astype(F32) + other[at].astype(F32)
    for k, part in enumerate(parts):
        at = high[0] ^ (k + 1)
        part[...] = (keep[at].astype(F32) + other[at].astype(F32)).astype(BF16)


def rows_kernel(spot, out, sg, gp, graw, edge, edge_c, w, dtw, *rest):
    *parts, stage = rest
    length, depth = sg.shape
    width = w.shape[2]
    heads = dtw.shape[0]
    total = sg[...] + mm(graw[0:heads, :], dtw[...], TN)
    total = total + mm(gp[:, 0:width], w[1], NT) + mm(gp[:, width:], w[2, :, 0:N], NT)
    late = mm(edge[:, 0:width], w[1], NT) + mm(edge[:, width:], w[2, :, 0:N], NT)
    late = late + mm(edge_c[...], w[2, :, N:], NT)
    stage[:, 0:depth] = out[...]
    stage[:, depth:] = total.astype(BF16)
    stage[length - RIM :, depth:] = (total[length - RIM :, :] + late).astype(BF16)
    piece = length // len(parts)
    for k, part in enumerate(parts):
        start = pl.multiple_of((spot[0] ^ k) * piece, piece)
        part[...] = stage[pl.ds(start, piece), :]


def outputs_kernel(*refs):
    *parts, layer, grad = refs
    depth = layer.shape[1]
    total = parts[0][...].astype(F32)
    for part in parts[1:]:
        total = total + part[...].astype(F32)
    layer[...] = total[:, 0:depth].astype(BF16)
    grad[...] = total[:, depth:]


def total_kernel(hops, *refs):
    early, late = refs[0:hops], refs[hops : 2 * hops]
    w_in, w_dt, w_out = refs[2 * hops :]
    piece = w_out.shape[0]

    def sum_of(parts):
        total = parts[0][...]
        for part in parts[1:]:
            total = total + part[...].astype(F32)
        return total

    def laid(total, base):
        return total[base * piece : (base + 1) * piece, :]

    early, late = sum_of(early), sum_of(late)
    for q in range(2):
        cut = slice(q * N, (q + 1) * N)
        w_out[:, cut] = laid(early, q)
        w_in[0, :, cut] = laid(early, 2 + q)
        w_in[1, :, cut] = laid(late, q)
    w_in[2, :, 0:N] = laid(late, 2)
    w_in[2, :, N:] = laid(early, 4)
    w_dt[...] = late[3 * piece : 3 * piece + w_dt.shape[0], 0:piece]


VMEM = pl.BlockSpec(memory_space=pltpu.VMEM)
SMEM = pl.BlockSpec(memory_space=pltpu.SMEM)


def run(kernel, name, outs, args, scalars=(), scratch=(), flops=10**8):
    moved = sum(a.size * a.dtype.itemsize for a in args)
    return pl.pallas_call(
        kernel,
        name=name,
        out_shape=[jax.ShapeDtypeStruct(shape, kind) for shape, kind in outs],
        in_specs=[SMEM if i in scalars else VMEM for i in range(len(args))],
        out_specs=[VMEM] * len(outs),
        scratch_shapes=list(scratch),
        compiler_params=pltpu.CompilerParams(vmem_limit_bytes=16 * 2**20),
        cost_estimate=pl.CostEstimate(flops=flops, bytes_accessed=2 * moved, transcendentals=0),
    )(*args)


def shifted(block, axis, distance):
    devices = range(lax.axis_size(axis))
    route = [(i - distance, i) for i in devices if i - distance in devices]
    return lax.ppermute(block, axis, route)


def swapped(block, axis, flip):
    return lax.ppermute(block, axis, [(i, i ^ flip) for i in range(lax.axis_size(axis))])


def body(
    series,
    in_weight,
    step_weight,
    step_bias,
    log_rate,
    conv_weight,
    conv_bias,
    skip_gain,
    norm_gain,
    out_weight,
    cotangent,
):
    length, depth = series.shape
    width = in_weight.shape[2]
    heads = step_weight.shape[1]
    count = lax.axis_size("tm")
    parts = lax.axis_size("head")
    every = width * parts
    assert width == 2 * N and heads == 4
    part = functools.partial
    w = in_weight.transpose(1, 0, 2)
    dtw = step_weight.T
    gain = norm_gain.reshape(1, width)
    hops = count // 2
    piece = depth // count
    position = lax.axis_index("tm").astype(jnp.int32)
    low, high = (position % 2).reshape(1), (position // 2).reshape(1)
    spot = lax.axis_index("head").astype(jnp.int32).reshape(1)
    rim = shifted(series[length - RIM :], "tm", 1)
    state_msg = ((width + LOGS, N), BF16)

    def passed(msg, back):
        partner = swapped(msg, "tm", 1)
        (both,) = run(part(pair_kernel, heads, back), "pair", [state_msg], [low, msg, partner], (0,))
        sign = -1 if back else 1
        return [partner] + [shifted(both, "tm", sign * 2 * d) for d in range(hops - 1, 0, -1)]

    def summed(keep, send, name):
        rows = keep.shape[1]
        own, *parts = run(
            halve_kernel, name, [((rows, N), F32)] + [((rows, N), BF16)] * (hops - 1),
            [high, keep, swapped(send, "tm", 1)], (0,),
        )
        return [own] + [swapped(block, "tm", 2 * (k + 1)) for k, block in enumerate(parts)]

    gate, pre, scal = run(
        part(project_kernel, heads), "project",
        [((length, width), BF16), ((length, 2 * width), BF16), ((4 * heads, length), F32)],
        [series, w, dtw, step_bias, log_rate], (3, 4),
    )
    x, bc, conv, own, msg = run(
        part(conv_kernel, heads), "conv",
        [
            ((length, width), BF16),
            ((length, width), BF16),
            ((length, 2 * width), F32),
            ((width, N), F32),
            state_msg,
        ],
        [pre, rim, w, conv_weight, conv_bias, scal],
        scratch=[pltpu.VMEM((length + 8, 2 * width), F32)],
    )
    ahead = passed(msg, False)
    inside, gg, slope = run(
        part(inside_kernel, heads), "inside",
        [((length, width), F32), ((length, width), F32), ((length, 2 * width), F32)],
        [x, bc, scal, skip_gain, cotangent, out_weight, gain, conv], (3,),
    )
    y, sin, sums = run(
        part(join_kernel, heads), "join",
        [((length, width), F32), ((width, N), F32), ((8, length), F32)],
        [low, inside, gg, gate, bc, scal] + ahead, (0,),
    )
    total = lax.psum(sums, "head")
    gy, msg = run(
        part(grad_y_kernel, heads, every), "grad_y",
        [((length, width), F32), state_msg],
        [total, y, gate, gg, bc, scal],
    )
    behind = passed(msg, True)
    early, late = 5 * piece, 3 * piece + LOGS
    out, keep, send, sg, bb, gb, edge_c, yb = run(
        part(beside_kernel, heads, count, every), "beside",
        [
            ((length, depth), BF16),
            ((hops, early, N), BF16),
            ((hops, early, N), BF16),
            ((length, depth), F32),
            ((length, width), F32),
            ((length, N), F32),
            ((RIM, N), BF16),
            ((8, length), F32),
        ],
        [
            low, total, y, gate, gg, gain, gy, x, bc, scal, sin, cotangent, out_weight, series,
            rim, w, conv_weight, slope, skip_gain,
        ],
        (0, 18),
        scratch=[
            pltpu.VMEM((length + RIM + 8, N), F32),
            pltpu.VMEM((count, early, N), BF16),
        ],
    )
    early_parts = summed(keep, send, "halve_early")
    keep, send, gp, edge, graw = run(
        part(close_kernel, heads, count), "close",
        [
            ((hops, late, N), BF16),
            ((hops, late, N), BF16),
            ((length, width + N), BF16),
            ((RIM, width + N), BF16),
            ((2 * heads, length), F32),
        ],
        [
            low, x, bc, scal, gy, bb, gb, yb, sin, own, slope, series, rim, conv_weight,
            skip_gain, log_rate,
        ]
        + behind,
        (0, 14, 15),
        scratch=[
            pltpu.VMEM((length + RIM + 8, width + N), F32),
            pltpu.VMEM((count, late, N), BF16),
        ],
    )
    late_parts = summed(keep, send, "halve_late")
    edge, edge_c = shifted(edge, "tm", -1), shifted(edge_c, "tm", -1)
    both = run(
        rows_kernel, "rows",
        [((length // parts, 2 * depth), BF16)] * parts,
        [spot, out, sg, gp, graw, edge, edge_c, w, dtw], (0,),
        scratch=[pltpu.VMEM((length, 2 * depth), BF16)],
    )
    both = [both[0]] + [swapped(both[k], "head", k) for k in range(1, parts)]
    layer_out, series_grad = run(
        outputs_kernel, "outputs",
        [((length // parts, depth), BF16), ((length // parts, depth), F32)], both,
    )
    w_in_grad, w_dt_grad, w_out_grad = run(
        part(total_kernel, hops), "total",
        [((3, piece, width), F32), ((heads, piece), F32), ((piece, width), F32)],
        early_parts + late_parts,
    )
    return (layer_out, series_grad, w_in_grad.transpose(1, 0, 2), w_dt_grad.T, w_out_grad)


def solution(mesh):
    in_specs = (
        P("tm", None),
        P(None, None, "head"),
        P(None, "head"),
        P("head"),
        P("head"),
        P(None, None, "head"),
        P(None, "head"),
        P("head"),
        P("head"),
        P(None, "head"),
        P("tm", None),
    )
    out_specs = (
        P(("tm", "head"), None),
        P(("tm", "head"), None),
        P("tm", None, "head"),
        P("tm", "head"),
        P("tm", "head"),
    )
    return jax.shard_map(body, mesh=mesh, in_specs=in_specs, out_specs=out_specs, check_vma=False)
```

```python
import functools

import jax
import jax.numpy as jnp
from jax import lax
from jax.experimental import pallas as pl
from jax.experimental.pallas import tpu as pltpu
from jax.sharding import PartitionSpec as P

N = 128
KW = 4
RIM = 16
LIMIT = 12 * 2**20
LOGS = 16
NORM_EPSILON = 1e-05

F32 = jnp.float32
BF16 = jnp.bfloat16
NN = (((1,), (0,)), ((), ()))
NT = (((1,), (1,)), ((), ()))
TN = (((0,), (0,)), ((), ()))


def mm(a, b, dims=NN):
    return lax.dot_general(a.astype(BF16), b.astype(BF16), dims, preferred_element_type=F32)


def mm_exact(a, b, dims=NN):
    return lax.dot_general(
        a, b, dims, precision=lax.Precision.HIGHEST, preferred_element_type=F32
    )


def lanes_of(shape):
    return lax.broadcasted_iota(jnp.int32, shape, len(shape) - 1)


def rows_of(shape):
    return lax.broadcasted_iota(jnp.int32, shape, len(shape) - 2)


def per_row(ref, shape):
    rows = rows_of(shape)
    out = jnp.full(shape, ref[0], F32)
    for h in range(1, shape[0]):
        out = jnp.where(rows == h, ref[h], out)
    return out


def per_lane(ref, heads, width):
    head = lanes_of((1, width)) // (width // heads)
    out = jnp.full((1, width), ref[0], F32)
    for h in range(1, heads):
        out = jnp.where(head == h, ref[h], out)
    return out


def widen(cols, heads, width):
    head = lanes_of((cols.shape[0], width)) // (width // heads)
    out = jnp.broadcast_to(cols[:, 0:1], (cols.shape[0], width))
    for h in range(1, heads):
        out = jnp.where(head == h, cols[:, h : h + 1], out)
    return out


def head_mask(heads, width):
    shape = (8, width)
    return jnp.where(lanes_of(shape) // (width // heads) == rows_of(shape), 1.0, 0.0)


def only_head(x, h, heads):
    width = x.shape[1]
    return jnp.where(lanes_of(x.shape) // (width // heads) == h, x, jnp.zeros_like(x))


def columns(rows):
    short = -rows.shape[0] % 8
    if short:
        rows = jnp.concatenate([rows, jnp.zeros((short, rows.shape[1]), F32)], axis=0)
    return jnp.transpose(rows)


def sigmoid(v):
    return 1.0 / (1.0 + jnp.exp(-v))


def running_sum(x):
    width = x.shape[1]
    lanes = lanes_of(x.shape)
    hop = 1
    while hop < width:
        x = x + jnp.where(lanes >= hop, pltpu.roll(x, hop, 1), 0.0)
        hop *= 2
    return x


def running_sum_back(x):
    width = x.shape[1]
    lanes = lanes_of(x.shape)
    hop = 1
    while hop < width:
        x = x + jnp.where(lanes < width - hop, pltpu.roll(x, width - hop, 1), 0.0)
        hop *= 2
    return x


def decay_of(cols, rows, h):
    length = cols.shape[0]
    gap = cols[:, h : h + 1] - rows[h : h + 1, :]
    shape = (length, length)
    return jnp.exp(jnp.where(lanes_of(shape) <= rows_of(shape), gap, -1e30))


def logs_of(msg, heads):
    logs = msg[msg.shape[0] - LOGS :].astype(F32)
    return logs[0:heads] + logs[heads : 2 * heads] + logs[2 * heads : 3 * heads]


def spread_rows(logs, heads, size):
    return jnp.concatenate(
        [jnp.broadcast_to(logs[h : h + 1], (size // heads, N)) for h in range(heads)], axis=0
    )


def state_of(msg):
    return msg[0 : msg.shape[0] - LOGS].astype(F32)


def packed(state, logs):
    high = logs.astype(BF16).astype(F32)
    middle = (logs - high).astype(BF16).astype(F32)
    low = logs - high - middle
    logs = jnp.concatenate([high, middle, low, jnp.zeros_like(low)], axis=0)
    return jnp.concatenate([state.astype(BF16), logs.astype(BF16)], axis=0)


def carried(own_turn, partner, others, heads):
    state = jnp.zeros((partner.shape[0] - LOGS, N), F32)
    size = state.shape[0]
    for msg in others:
        state = jnp.exp(spread_rows(logs_of(msg, heads), heads, size)) * state + state_of(msg)
    with_partner = jnp.exp(spread_rows(logs_of(partner, heads), heads, size)) * state
    return jnp.where(own_turn, with_partner + state_of(partner), state)


def project_kernel(heads, series, w, dtw, bias, rate, gate, pre, scal):
    width = w.shape[2]
    s = series[...]
    gate[...] = mm(s, w[0]).astype(BF16)
    pre[:, 0:width] = mm(s, w[1]).astype(BF16)
    pre[:, width:] = mm(s, w[2]).astype(BF16)
    raw = mm(dtw[...], s, NT)
    shifted = raw + per_row(bias, raw.shape)
    step = jnp.maximum(shifted, 0.0) + jnp.log1p(jnp.exp(-jnp.abs(shifted)))
    running = running_sum(-step * jnp.exp(per_row(rate, raw.shape)))
    scal[0:heads, :] = running
    scal[heads : 2 * heads, :] = step
    scal[2 * heads : 3 * heads, :] = sigmoid(shifted)
    scal[3 * heads :, :] = jnp.zeros_like(running)


def conv_kernel(heads, pre, rim, w, cw, cb, scal, x, bc, conv, own, msg, wide):
    length, both = pre.shape
    width = both // 2
    for s in range(2):
        cut = slice(s * width, (s + 1) * width)
        rims = mm(rim[...], w[1 + s]).astype(BF16).astype(F32)
        wide[0:8, cut] = rims[RIM - 8 :, :]
        wide[8:, cut] = pre[:, cut].astype(F32)
        acc = cb[s : s + 1, :] + cw[0, s : s + 1, :] * wide[5 : 5 + length, cut]
        for k in range(1, KW):
            acc = acc + cw[k, s : s + 1, :] * wide[5 + k : 5 + k + length, cut]
        conv[:, cut] = acc
        act = (acc * sigmoid(acc)).astype(BF16)
        if s == 0:
            x[...] = act
        else:
            bc[...] = act
    running = scal[0:heads, :]
    last = running[:, length - 1 : length]
    remain = jnp.exp(last - running) * scal[heads : 2 * heads, :]
    scaled = x[...].astype(F32) * widen(columns(remain), heads, width)
    state = mm(scaled, bc[:, 0:N], TN)
    own[...] = state
    msg[...] = packed(state, jnp.broadcast_to(last, (heads, N)))


def pair_kernel(heads, back, low, mine, other, msg):
    mine, other = mine[...], other[...]
    size = mine.shape[0] - LOGS
    mine_first = low[0] == 0
    mine_logs, other_logs = logs_of(mine, heads), logs_of(other, heads)
    crossed = jnp.logical_not(mine_first) if back else mine_first
    mine_scale = jnp.where(crossed, jnp.exp(other_logs), 1.0)
    other_scale = jnp.where(crossed, 1.0, jnp.exp(mine_logs))
    state = spread_rows(mine_scale, heads, size) * state_of(mine)
    state = state + spread_rows(other_scale, heads, size) * state_of(other)
    msg[...] = packed(state, mine_logs + other_logs)


def link_kernel(heads, farther, nearer, msg):
    farther, nearer = farther[...], nearer[...]
    size = nearer.shape[0] - LOGS
    logs = logs_of(nearer, heads)
    state = jnp.exp(spread_rows(logs, heads, size)) * state_of(farther) + state_of(nearer)
    msg[...] = packed(state, logs + logs_of(farther, heads))


def inside_kernel(heads, x, bc, scal, skip, cot, ow, gain, conv, y, gg, slope):
    length, width = x.shape
    xv = x[...].astype(F32)
    rows = scal[...]
    cols = columns(rows)
    scores = mm(bc[:, N:], bc[:, 0:N], NT)
    acc = per_lane(skip, heads, width) * xv
    for h in range(heads):
        mixing = scores * decay_of(cols, rows, h) * rows[heads + h : heads + h + 1, :]
        acc = acc + mm(mixing, only_head(xv, h, heads))
    y[...] = acc
    gg[...] = gain[...] * mm(cot[...], ow[...])
    v = conv[...]
    sig = sigmoid(v)
    slope[...] = sig * (1.0 + v * (1.0 - sig))


def join_kernel(heads, low, yi, gg, gate, bc, scal, partner, *rest):
    *others, y, sin, sums = rest
    length, width = yi.shape
    start = carried(low[0] == 1, partner[...], [o[...] for o in others], heads)
    sin[...] = start
    grow = widen(columns(jnp.exp(scal[0:heads, :])), heads, width)
    yv = yi[...] + grow * mm(bc[:, N:], start, NT)
    y[...] = yv
    g = gate[...].astype(F32)
    gated = yv * (g * sigmoid(g))
    ones = jnp.ones((8, width), F32)
    square = mm_exact(ones, gated * gated, NT)
    inner = mm_exact(ones, gated * gg[...], NT)
    sums[...] = jnp.where(rows_of(square.shape) == 0, square, inner)


def norm_columns(total, every):
    inv = lax.rsqrt(total[0:1, :] / every + NORM_EPSILON)
    coef = inv * inv * inv * total[1:2, :] / every
    return columns(jnp.concatenate([inv, coef], axis=0))


def grad_y_kernel(heads, every, sums, other, y, gate, gg, bc, scal, gy, msg, total):
    length, width = y.shape
    total[...] = sums[...] + other[...]
    cols = norm_columns(total[...], every)
    g = gate[...].astype(F32)
    act = g * sigmoid(g)
    gated = y[...] * act
    grad = (cols[:, 0:1] * gg[...] - gated * cols[:, 1:2]) * act
    gy[...] = grad
    grow = widen(columns(jnp.exp(scal[0:heads, :])), heads, width)
    last = scal[0:heads, length - 1 : length]
    msg[...] = packed(mm(grad * grow, bc[:, N:], TN), jnp.broadcast_to(last, (heads, N)))


def conv_back(cw, wide, cut, length, slot, slot_cut):
    acc = cw[0, slot : slot + 1, slot_cut] * wide[KW - 1 : KW - 1 + RIM + length, cut]
    for k in range(1, KW):
        at = KW - 1 - k
        acc = acc + cw[k, slot : slot + 1, slot_cut] * wide[at : at + RIM + length, cut]
    return acc.astype(BF16)


def clear_ends(wide, length):
    zeros = jnp.zeros((RIM, wide.shape[1]), F32)
    wide[0:RIM, :] = zeros
    wide[RIM + length :, :] = zeros[0:8]


def stack_columns(msg, grad, at, base, piece):
    for q in range(grad.shape[1] // N):
        msg[at, (base + q) * piece : (base + q + 1) * piece, :] = grad[
            at * piece : (at + 1) * piece, q * N : (q + 1) * N
        ]


def split_pair(low, every, keep, send):
    for at in range(keep.shape[0]):
        keep[at] = every[2 * at + low]
        send[at] = every[2 * at + 1 - low]


def early_kernel(
    heads, count, every,
    low, total, y, gate, gg, gain, gy, x, bc, scal, sin, cot, series, rim, cw, slope,
    normed, grad_gate, gp, gb, edge, keep, send, wide, stage,
):
    length, width = y.shape
    depth = series.shape[1]
    rows = scal[...]
    cols = columns(rows)
    xv = x[...]
    gyv = gy[...].astype(BF16)
    b, c = bc[:, 0:N], bc[:, N:]
    group = jnp.zeros((length, length), F32)
    for h in range(heads):
        pairs = mm(only_head(gyv, h, heads), xv, NT)
        group = group + decay_of(cols, rows, h) * pairs * rows[heads + h : heads + h + 1, :]
    gb[...] = mm(group, c, TN)
    grow = widen(columns(jnp.exp(rows[0:heads])), heads, width)
    grad_c = mm(group, b) + mm(gy[...] * grow, sin[...])
    clear_ends(wide, length)
    wide[RIM : RIM + length, :] = grad_c * slope[:, 2 * width - N :]
    grad_pre = conv_back(cw, wide, slice(0, N), length, 1, slice(width - N, width))
    edge[...] = grad_pre[0:RIM]
    gp[...] = grad_pre[RIM:]
    cols = norm_columns(total[...], every)
    g = gate[...].astype(F32)
    sig = sigmoid(g)
    yv = y[...]
    gated = yv * (g * sig)
    normed[...] = (gated * cols[:, 0:1] * gain[...]).astype(BF16)
    grad_gated = cols[:, 0:1] * gg[...] - gated * cols[:, 1:2]
    grad_gate[...] = (grad_gated * yv * (sig * (1.0 + g * (1.0 - sig)))).astype(BF16)
    w_out = mm(cot[...], normed[...], TN).astype(BF16)
    w_gate = mm(series[...], grad_gate[...], TN).astype(BF16)
    w_c = (mm(series[...], gp[...], TN) + mm(rim[...], edge[...], TN)).astype(BF16)
    piece = depth // count
    for at in range(count):
        stack_columns(stage, w_out, at, 0, piece)
        stack_columns(stage, w_gate, at, 2, piece)
        stack_columns(stage, w_c, at, 4, piece)
    split_pair(low[0], stage, keep, send)


def beside_kernel(
    heads, normed, grad_gate, gp, y, gy, x, bc, scal, ow, w, skip,
    out, sg, bb, yb,
):
    length, width = y.shape
    rows = scal[...]
    cols = columns(rows)
    xv = x[...].astype(F32)
    gyv = gy[...]
    scores = mm(bc[:, N:], bc[:, 0:N], NT)
    back = jnp.zeros((length, width), F32)
    for h in range(heads):
        back = back + mm(scores * decay_of(cols, rows, h), only_head(gyv, h, heads), TN)
    bb[...] = back
    skips = per_lane(skip, heads, width)
    yb[...] = mm_exact(head_mask(heads, width), gyv * (y[...] - skips * xv), NT)
    out[...] = mm(normed[...], ow[...], NT).astype(BF16)
    sg[...] = mm(grad_gate[...], w[0], NT) + mm(gp[...], w[2, :, width - N :], NT)


def close_kernel(
    heads, count,
    low, x, bc, scal, gy, bb, gb, yb, sin, own, slope, series, rim, cw, edge_c, skip, rate, partner, *rest,
):
    *others, keep, send, gp, edge, graw, wide, stage = rest
    length, width = gy.shape
    depth = series.shape[1]
    after = carried(low[0] == 0, partner[...], [o[...] for o in others], heads)
    rows = scal[...]
    running, step = rows[0:heads], rows[heads : 2 * heads]
    last = running[:, length - 1 : length]
    remain = jnp.exp(last - running)
    cols = columns(jnp.concatenate([remain, step, remain * step], axis=0))
    xv = x[...].astype(F32)
    back = bb[...] + widen(cols, heads, width) * mm(bc[:, 0:N], after, NT)
    grad_x = per_lane(skip, heads, width) * gy[...] + widen(cols[:, heads:], heads, width) * back
    grad_b = gb[...] + mm(xv * widen(cols[:, 2 * heads :], heads, width), after)
    clear_ends(wide, length)
    wide[RIM : RIM + length, 0:width] = grad_x * slope[:, 0:width]
    wide[RIM : RIM + length, width:] = grad_b * slope[:, width : width + N]
    grad_x = conv_back(cw, wide, slice(0, width), length, 0, slice(0, width))
    grad_b = conv_back(cw, wide, slice(width, width + N), length, 1, slice(0, N))
    edge[:, 0:width] = grad_x[0:RIM]
    edge[:, width : width + N] = grad_b[0:RIM]
    edge[:, width + N :] = edge_c[...]
    gp[:, 0:width] = grad_x[RIM:]
    gp[:, width:] = grad_b[RIM:]
    w_x = (mm(series[...], grad_x[RIM:], TN) + mm(rim[...], grad_x[0:RIM], TN)).astype(BF16)
    w_b = (mm(series[...], grad_b[RIM:], TN) + mm(rim[...], grad_b[0:RIM], TN)).astype(BF16)
    mask = head_mask(heads, width)
    x_back = mm_exact(mask, xv * back, NT)[0:heads]
    final = jnp.exp(spread_rows(jnp.broadcast_to(last, (heads, N)), heads, width)) * sin[...]
    ends = jnp.sum(mm_exact(mask, after * (final + own[...])), axis=1, keepdims=True)[0:heads]
    grad_log = running_sum_back(yb[0:heads, :] - step * x_back) + ends
    grad_step = x_back - jnp.exp(per_row(rate, x_back.shape)) * grad_log
    grad_raw = grad_step * rows[2 * heads : 3 * heads]
    grad_raw = jnp.concatenate([grad_raw, jnp.zeros_like(grad_raw)], axis=0)
    graw[...] = grad_raw
    dt = mm(grad_raw, series[...])
    piece = depth // count
    blank = jnp.zeros((LOGS, N), F32)
    for at in range(count):
        stack_columns(stage, w_x, at, 0, piece)
        stack_columns(stage, w_b, at, 2, piece)
        dt_piece = jnp.concatenate(
            [dt[:, at * piece : (at + 1) * piece], blank[0 : 2 * heads, 0 : N - piece]], axis=1
        )
        dt_piece = jnp.concatenate([dt_piece, blank[0 : LOGS - 2 * heads]], axis=0)
        stage[at, 3 * piece :, :] = dt_piece.astype(BF16)
    split_pair(low[0], stage, keep, send)


def halve_kernel(high, keep, other, own, *parts):
    at = high[0]
    own[...] = keep[at].astype(F32) + other[at].astype(F32)
    for k, part in enumerate(parts):
        at = high[0] ^ (k + 1)
        part[...] = (keep[at].astype(F32) + other[at].astype(F32)).astype(BF16)


def rows_kernel(low, out, sg, gp, graw, edge, w, dtw, keep, send, stage):
    length, depth = sg.shape
    width = w.shape[2]
    heads = dtw.shape[0]
    total = sg[...] + mm(graw[0:heads, :], dtw[...], TN)
    total = total + mm(gp[:, 0:width], w[1], NT) + mm(gp[:, width:], w[2, :, 0:N], NT)
    late = mm(edge[:, 0:width], w[1], NT) + mm(edge[:, width:], w[2], NT)
    stage[:, 0:depth] = out[...]
    stage[:, depth:] = total.astype(BF16)
    stage[length - RIM :, depth:] = (total[length - RIM :, :] + late).astype(BF16)
    piece = keep.shape[1]
    for at in range(keep.shape[0]):
        start = pl.multiple_of((2 * at + low[0]) * piece, piece)
        keep[at] = stage[pl.ds(start, piece), :]
        start = pl.multiple_of((2 * at + 1 - low[0]) * piece, piece)
        send[at] = stage[pl.ds(start, piece), :]


def outputs_kernel(*refs):
    *parts, layer, grad = refs
    depth = layer.shape[1]
    total = parts[0][...].astype(F32)
    for part in parts[1:]:
        total = total + part[...].astype(F32)
    layer[...] = total[:, 0:depth].astype(BF16)
    grad[...] = total[:, depth:]


def total_kernel(hops, *refs):
    early, late = refs[0:hops], refs[hops : 2 * hops]
    w_in, w_dt, w_out = refs[2 * hops :]
    piece = w_out.shape[0]

    def sum_of(parts):
        total = parts[0][...]
        for part in parts[1:]:
            total = total + part[...].astype(F32)
        return total

    def laid(total, base):
        return total[base * piece : (base + 1) * piece, :]

    early, late = sum_of(early), sum_of(late)
    for q in range(2):
        cut = slice(q * N, (q + 1) * N)
        w_out[:, cut] = laid(early, q)
        w_in[0, :, cut] = laid(early, 2 + q)
        w_in[1, :, cut] = laid(late, q)
    w_in[2, :, 0:N] = laid(late, 2)
    w_in[2, :, N:] = laid(early, 4)
    w_dt[...] = late[3 * piece : 3 * piece + w_dt.shape[0], 0:piece]


VMEM = pl.BlockSpec(memory_space=pltpu.VMEM)
SMEM = pl.BlockSpec(memory_space=pltpu.SMEM)
HBM = pl.BlockSpec(memory_space=pltpu.HBM)


def run(kernel, name, outs, args, scalars=(), fetched=(), scratch=(), flops=10**8):
    moved = sum(a.size * a.dtype.itemsize for a in args)

    def place(i):
        if i in fetched:
            return HBM
        return SMEM if i in scalars else VMEM

    def whole(*refs):
        held, sems = refs[len(refs) - len(fetched) - 1 : -1], refs[-1]
        refs = list(refs[: len(refs) - len(fetched) - 1])
        copies = []
        for k, i in enumerate(fetched):
            copies.append(pltpu.make_async_copy(refs[i], held[k], sems.at[k]))
            refs[i] = held[k]
        for copy in copies:
            copy.start()
        for copy in copies:
            copy.wait()
        kernel(*refs)

    holders = []
    if fetched:
        for i in fetched:
            kind = pltpu.SMEM if i in scalars else pltpu.VMEM
            holders.append(kind(args[i].shape, args[i].dtype))
        holders.append(pltpu.SemaphoreType.DMA((len(fetched),)))
    return pl.pallas_call(
        whole if fetched else kernel,
        name=name,
        out_shape=[jax.ShapeDtypeStruct(shape, kind) for shape, kind in outs],
        in_specs=[place(i) for i in range(len(args))],
        out_specs=[VMEM] * len(outs),
        scratch_shapes=list(scratch) + holders,
        compiler_params=pltpu.CompilerParams(vmem_limit_bytes=LIMIT),
        cost_estimate=pl.CostEstimate(flops=flops, bytes_accessed=2 * moved, transcendentals=0),
    )(*args)


def shifted(block, axis, distance):
    devices = range(lax.axis_size(axis))
    route = [(i - distance, i) for i in devices if i - distance in devices]
    return lax.ppermute(block, axis, route)


def swapped(block, axis, flip):
    return lax.ppermute(block, axis, [(i, i ^ flip) for i in range(lax.axis_size(axis))])


def body(
    series,
    in_weight,
    step_weight,
    step_bias,
    log_rate,
    conv_weight,
    conv_bias,
    skip_gain,
    norm_gain,
    out_weight,
    cotangent,
):
    length, depth = series.shape
    width = in_weight.shape[2]
    heads = step_weight.shape[1]
    count = lax.axis_size("tm")
    parts = lax.axis_size("head")
    every = width * parts
    assert width == 2 * N and heads == 4
    part = functools.partial
    w = in_weight.transpose(1, 0, 2)
    dtw = step_weight.T
    gain = norm_gain.reshape(1, width)
    hops = count // 2
    piece = depth // count
    position = lax.axis_index("tm").astype(jnp.int32)
    spot = lax.axis_index("head").astype(jnp.int32)
    low, high = (position % 2).reshape(1), (position // 2).reshape(1)
    low_spot, high_spot = (spot % 2).reshape(1), (spot // 2).reshape(1)
    rim = shifted(series[length - RIM :], "tm", 1)
    state_msg = ((width + LOGS, N), BF16)

    def passed(msg, back, during):
        made = []

        def meanwhile(k, block):
            if k < len(during):
                block, extra = lax.optimization_barrier((block, during[k](made)))
                made.append(extra)
            return block

        partner = meanwhile(0, swapped(msg, "tm", 1))
        (msg,) = run(part(pair_kernel, heads, back), "pair", [state_msg], [low, msg, partner], (0,))
        entered = []
        hop = 1
        while hop < hops:
            other = meanwhile(len(made), shifted(msg, "tm", (-2 if back else 2) * hop))
            entered.append(other)
            hop *= 2
            if hop < hops:
                (msg,) = run(part(link_kernel, heads), "link", [state_msg], [other, msg])
        return [partner] + entered[::-1], made

    def halved(keep, send, axis, where, name):
        most, rows, cols = keep.shape
        return run(
            halve_kernel, name, [((rows, cols), F32)] + [((rows, cols), BF16)] * (most - 1),
            [where, keep, swapped(send, axis, 1)], (0,),
        )

    def gathered(blocks, axis):
        return [blocks[0]] + [swapped(block, axis, 2 * k) for k, block in enumerate(blocks) if k]

    gate, pre, scal = run(
        part(project_kernel, heads), "project",
        [((length, width), BF16), ((length, 2 * width), BF16), ((4 * heads, length), F32)],
        [series, w, dtw, step_bias, log_rate], (3, 4), (0, 1, 2, 3, 4),
    )
    x, bc, conv, own, msg = run(
        part(conv_kernel, heads), "conv",
        [
            ((length, width), BF16),
            ((length, width), BF16),
            ((length, 2 * width), F32),
            ((width, N), F32),
            state_msg,
        ],
        [pre, rim, w, conv_weight, conv_bias, scal], (), (2, 3, 4),
        scratch=[pltpu.VMEM((length + 8, 2 * width), F32)],
    )

    def inner(made):
        return run(
            part(inside_kernel, heads), "inside",
            [((length, width), F32), ((length, width), F32), ((length, 2 * width), F32)],
            [x, bc, scal, skip_gain, cotangent, out_weight, gain, conv], (3,), (3, 4, 5, 6),
        )

    ahead, ((inside, gg, slope),) = passed(msg, False, [inner])
    y, sin, sums = run(
        part(join_kernel, heads), "join",
        [((length, width), F32), ((width, N), F32), ((8, length), F32)],
        [low, inside, gg, gate, bc, scal] + ahead, (0,),
    )
    flip = 1
    while 2 * flip < parts:
        sums = sums + swapped(sums, "head", flip)
        flip *= 2
    gy, msg, total = run(
        part(grad_y_kernel, heads, every), "grad_y",
        [((length, width), F32), state_msg, ((8, length), F32)],
        [sums, swapped(sums, "head", flip), y, gate, gg, bc, scal],
    )
    early, late = 5 * piece, 3 * piece + LOGS

    def early_part(made):
        return run(
            part(early_kernel, heads, count, every), "early",
            [
                ((length, width), BF16),
                ((length, width), BF16),
                ((length, N), BF16),
                ((length, N), F32),
                ((RIM, N), BF16),
                ((hops, early, N), BF16),
                ((hops, early, N), BF16),
            ],
            [
                low, total, y, gate, gg, gain, gy, x, bc, scal, sin, cotangent, series, rim,
                conv_weight, slope,
            ],
            (0,), (5, 11, 12, 14),
            scratch=[
                pltpu.VMEM((length + RIM + 8, N), F32),
                pltpu.VMEM((count, early, N), BF16),
            ],
        )

    def beside_part(made):
        normed, grad_gate, gp_c = made[0][0:3]
        return run(
            part(beside_kernel, heads), "beside",
            [
                ((length, depth), BF16),
                ((length, depth), F32),
                ((length, width), F32),
                ((8, length), F32),
            ],
            [normed, grad_gate, gp_c, y, gy, x, bc, scal, out_weight, w, skip_gain],
            (10,), (8, 9, 10),
        )

    behind, (firsts, (out, sg, bb, yb)) = passed(msg, True, [early_part, beside_part])
    gb, edge_c, keep, send = firsts[3:]
    early_parts = halved(keep, send, "tm", high, "halve_early")
    behind, early_parts = lax.optimization_barrier((behind, early_parts))
    early_parts = gathered(early_parts, "tm")
    keep, send, gp, edge, graw = run(
        part(close_kernel, heads, count), "close",
        [
            ((hops, late, N), BF16),
            ((hops, late, N), BF16),
            ((length, width + N), BF16),
            ((RIM, 2 * width), BF16),
            ((2 * heads, length), F32),
        ],
        [
            low, x, bc, scal, gy, bb, gb, yb, sin, own, slope, series, rim, conv_weight, edge_c,
            skip_gain, log_rate,
        ]
        + behind,
        (0, 15, 16), (11, 13, 15, 16),
        scratch=[
            pltpu.VMEM((length + RIM + 8, width + N), F32),
            pltpu.VMEM((count, late, N), BF16),
        ],
    )
    late_parts = halved(keep, send, "tm", high, "halve_late")
    late_parts = gathered(late_parts, "tm")
    edge = shifted(edge, "tm", -1)
    rows = length // parts
    keep, send = run(
        rows_kernel, "rows",
        [((parts // 2, rows, 2 * depth), BF16)] * 2,
        [low_spot, out, sg, gp, graw, edge, w, dtw], (0,), (6, 7),
        scratch=[pltpu.VMEM((length, 2 * depth), BF16)],
    )
    both = gathered(halved(keep, send, "head", high_spot, "halve_rows"), "head")
    layer_out, series_grad = run(
        outputs_kernel, "outputs", [((rows, depth), BF16), ((rows, depth), F32)], both,
    )
    w_in_grad, w_dt_grad, w_out_grad = run(
        part(total_kernel, hops), "total",
        [((3, piece, width), F32), ((heads, piece), F32), ((piece, width), F32)],
        early_parts + late_parts,
    )
    return (layer_out, series_grad, w_in_grad.transpose(1, 0, 2), w_dt_grad.T, w_out_grad)


def solution(mesh):
    in_specs = (
        P("tm", None),
        P(None, None, "head"),
        P(None, "head"),
        P("head"),
        P("head"),
        P(None, None, "head"),
        P(None, "head"),
        P("head"),
        P("head"),
        P(None, "head"),
        P("tm", None),
    )
    out_specs = (
        P(("tm", "head"), None),
        P(("tm", "head"), None),
        P("tm", None, "head"),
        P("tm", "head"),
        P("tm", "head"),
    )
    return jax.shard_map(body, mesh=mesh, in_specs=in_specs, out_specs=out_specs, check_vma=False)
```

```python
import functools

import jax
import jax.numpy as jnp
from jax import lax
from jax.experimental import pallas as pl
from jax.experimental.pallas import tpu as pltpu
from jax.sharding import PartitionSpec as P

N = 128
KW = 4
RIM = 16
LIMIT = 12 * 2**20
LOGS = 16
NORM_EPSILON = 1e-05

F32 = jnp.float32
BF16 = jnp.bfloat16
NN = (((1,), (0,)), ((), ()))
NT = (((1,), (1,)), ((), ()))
TN = (((0,), (0,)), ((), ()))


def mm(a, b, dims=NN):
    return lax.dot_general(a.astype(BF16), b.astype(BF16), dims, preferred_element_type=F32)


def mm_exact(a, b, dims=NN):
    return lax.dot_general(
        a, b, dims, precision=lax.Precision.HIGHEST, preferred_element_type=F32
    )


def lanes_of(shape):
    return lax.broadcasted_iota(jnp.int32, shape, len(shape) - 1)


def rows_of(shape):
    return lax.broadcasted_iota(jnp.int32, shape, len(shape) - 2)


def per_row(ref, shape):
    rows = rows_of(shape)
    out = jnp.full(shape, ref[0], F32)
    for h in range(1, shape[0]):
        out = jnp.where(rows == h, ref[h], out)
    return out


def per_lane(ref, heads, width):
    head = lanes_of((1, width)) // (width // heads)
    out = jnp.full((1, width), ref[0], F32)
    for h in range(1, heads):
        out = jnp.where(head == h, ref[h], out)
    return out


def widen(cols, heads, width):
    head = lanes_of((cols.shape[0], width)) // (width // heads)
    out = jnp.broadcast_to(cols[:, 0:1], (cols.shape[0], width))
    for h in range(1, heads):
        out = jnp.where(head == h, cols[:, h : h + 1], out)
    return out


def head_mask(heads, width):
    shape = (8, width)
    return jnp.where(lanes_of(shape) // (width // heads) == rows_of(shape), 1.0, 0.0)


def only_head(x, h, heads):
    width = x.shape[1]
    return jnp.where(lanes_of(x.shape) // (width // heads) == h, x, jnp.zeros_like(x))


def columns(rows):
    short = -rows.shape[0] % 8
    if short:
        rows = jnp.concatenate([rows, jnp.zeros((short, rows.shape[1]), F32)], axis=0)
    return jnp.transpose(rows)


def sigmoid(v):
    return 1.0 / (1.0 + jnp.exp(-v))


def running_sum(x):
    width = x.shape[1]
    lanes = lanes_of(x.shape)
    hop = 1
    while hop < width:
        x = x + jnp.where(lanes >= hop, pltpu.roll(x, hop, 1), 0.0)
        hop *= 2
    return x


def running_sum_back(x):
    width = x.shape[1]
    lanes = lanes_of(x.shape)
    hop = 1
    while hop < width:
        x = x + jnp.where(lanes < width - hop, pltpu.roll(x, width - hop, 1), 0.0)
        hop *= 2
    return x


def decay_of(cols, rows, h):
    length = cols.shape[0]
    gap = cols[:, h : h + 1] - rows[h : h + 1, :]
    shape = (length, length)
    return jnp.exp(jnp.where(lanes_of(shape) <= rows_of(shape), gap, -1e30))


def logs_of(msg, heads):
    logs = msg[msg.shape[0] - LOGS :].astype(F32)
    return logs[0:heads] + logs[heads : 2 * heads] + logs[2 * heads : 3 * heads]


def spread_rows(logs, heads, size):
    return jnp.concatenate(
        [jnp.broadcast_to(logs[h : h + 1], (size // heads, N)) for h in range(heads)], axis=0
    )


def state_of(msg):
    return msg[0 : msg.shape[0] - LOGS].astype(F32)


def packed(state, logs):
    high = logs.astype(BF16).astype(F32)
    middle = (logs - high).astype(BF16).astype(F32)
    low = logs - high - middle
    logs = jnp.concatenate([high, middle, low, jnp.zeros_like(low)], axis=0)
    return jnp.concatenate([state.astype(BF16), logs.astype(BF16)], axis=0)


def carried(own_turn, partner, others, heads):
    state = jnp.zeros((partner.shape[0] - LOGS, N), F32)
    size = state.shape[0]
    for msg in others:
        state = jnp.exp(spread_rows(logs_of(msg, heads), heads, size)) * state + state_of(msg)
    with_partner = jnp.exp(spread_rows(logs_of(partner, heads), heads, size)) * state
    return jnp.where(own_turn, with_partner + state_of(partner), state)


def project_kernel(heads, series, w, dtw, bias, rate, gate, pre, scal):
    width = w.shape[2]
    s = series[...]
    gate[...] = mm(s, w[0]).astype(BF16)
    pre[:, 0:width] = mm(s, w[1]).astype(BF16)
    pre[:, width:] = mm(s, w[2]).astype(BF16)
    raw = mm(dtw[...], s, NT)
    shifted = raw + per_row(bias, raw.shape)
    step = jnp.maximum(shifted, 0.0) + jnp.log1p(jnp.exp(-jnp.abs(shifted)))
    running = running_sum(-step * jnp.exp(per_row(rate, raw.shape)))
    scal[0:heads, :] = running
    scal[heads : 2 * heads, :] = step
    scal[2 * heads : 3 * heads, :] = sigmoid(shifted)
    scal[3 * heads :, :] = jnp.zeros_like(running)


def conv_kernel(heads, pre, rim, w, cw, cb, scal, x, bc, conv, own, msg, wide):
    length, both = pre.shape
    width = both // 2
    for s in range(2):
        cut = slice(s * width, (s + 1) * width)
        rims = mm(rim[...], w[1 + s]).astype(BF16).astype(F32)
        wide[0:8, cut] = rims[RIM - 8 :, :]
        wide[8:, cut] = pre[:, cut].astype(F32)
        acc = cb[s : s + 1, :] + cw[0, s : s + 1, :] * wide[5 : 5 + length, cut]
        for k in range(1, KW):
            acc = acc + cw[k, s : s + 1, :] * wide[5 + k : 5 + k + length, cut]
        conv[:, cut] = acc
        act = (acc * sigmoid(acc)).astype(BF16)
        if s == 0:
            x[...] = act
        else:
            bc[...] = act
    running = scal[0:heads, :]
    last = running[:, length - 1 : length]
    remain = jnp.exp(last - running) * scal[heads : 2 * heads, :]
    scaled = x[...].astype(F32) * widen(columns(remain), heads, width)
    state = mm(scaled, bc[:, 0:N], TN)
    own[...] = state
    msg[...] = packed(state, jnp.broadcast_to(last, (heads, N)))


def pair_kernel(heads, back, low, mine, other, msg):
    mine, other = mine[...], other[...]
    size = mine.shape[0] - LOGS
    mine_first = low[0] == 0
    mine_logs, other_logs = logs_of(mine, heads), logs_of(other, heads)
    crossed = jnp.logical_not(mine_first) if back else mine_first
    mine_scale = jnp.where(crossed, jnp.exp(other_logs), 1.0)
    other_scale = jnp.where(crossed, 1.0, jnp.exp(mine_logs))
    state = spread_rows(mine_scale, heads, size) * state_of(mine)
    state = state + spread_rows(other_scale, heads, size) * state_of(other)
    msg[...] = packed(state, mine_logs + other_logs)


def link_kernel(heads, farther, nearer, msg):
    farther, nearer = farther[...], nearer[...]
    size = nearer.shape[0] - LOGS
    logs = logs_of(nearer, heads)
    state = jnp.exp(spread_rows(logs, heads, size)) * state_of(farther) + state_of(nearer)
    msg[...] = packed(state, logs + logs_of(farther, heads))


def inside_kernel(heads, x, bc, scal, skip, cot, ow, gain, conv, y, gg, slope):
    length, width = x.shape
    xv = x[...].astype(F32)
    rows = scal[...]
    cols = columns(rows)
    scores = mm(bc[:, N:], bc[:, 0:N], NT)
    acc = per_lane(skip, heads, width) * xv
    for h in range(heads):
        mixing = scores * decay_of(cols, rows, h) * rows[heads + h : heads + h + 1, :]
        acc = acc + mm(mixing, only_head(xv, h, heads))
    y[...] = acc
    gg[...] = gain[...] * mm(cot[...], ow[...])
    v = conv[...]
    sig = sigmoid(v)
    slope[...] = sig * (1.0 + v * (1.0 - sig))


def join_kernel(heads, low, yi, gg, gate, bc, scal, partner, *rest):
    *others, y, sin, sums = rest
    length, width = yi.shape
    start = carried(low[0] == 1, partner[...], [o[...] for o in others], heads)
    sin[...] = start
    grow = widen(columns(jnp.exp(scal[0:heads, :])), heads, width)
    yv = yi[...] + grow * mm(bc[:, N:], start, NT)
    y[...] = yv
    g = gate[...].astype(F32)
    gated = yv * (g * sigmoid(g))
    ones = jnp.ones((8, width), F32)
    square = mm_exact(ones, gated * gated, NT)
    inner = mm_exact(ones, gated * gg[...], NT)
    sums[...] = jnp.where(rows_of(square.shape) == 0, square, inner)


def norm_columns(total, every):
    inv = lax.rsqrt(total[0:1, :] / every + NORM_EPSILON)
    coef = inv * inv * inv * total[1:2, :] / every
    return columns(jnp.concatenate([inv, coef], axis=0))


def grad_y_kernel(heads, every, sums, other, y, gate, gg, bc, scal, gy, msg, total):
    length, width = y.shape
    total[...] = sums[...] + other[...]
    cols = norm_columns(total[...], every)
    g = gate[...].astype(F32)
    act = g * sigmoid(g)
    gated = y[...] * act
    grad = (cols[:, 0:1] * gg[...] - gated * cols[:, 1:2]) * act
    gy[...] = grad
    grow = widen(columns(jnp.exp(scal[0:heads, :])), heads, width)
    last = scal[0:heads, length - 1 : length]
    msg[...] = packed(mm(grad * grow, bc[:, N:], TN), jnp.broadcast_to(last, (heads, N)))


def conv_back(cw, wide, cut, length, slot, slot_cut):
    acc = cw[0, slot : slot + 1, slot_cut] * wide[KW - 1 : KW - 1 + RIM + length, cut]
    for k in range(1, KW):
        at = KW - 1 - k
        acc = acc + cw[k, slot : slot + 1, slot_cut] * wide[at : at + RIM + length, cut]
    return acc.astype(BF16)


def clear_ends(wide, length):
    zeros = jnp.zeros((RIM, wide.shape[1]), F32)
    wide[0:RIM, :] = zeros
    wide[RIM + length :, :] = zeros[0:8]


def stack_columns(msg, grad, at, base, piece):
    for q in range(grad.shape[1] // N):
        msg[at, (base + q) * piece : (base + q + 1) * piece, :] = grad[
            at * piece : (at + 1) * piece, q * N : (q + 1) * N
        ]


def split_pair(low, every, keep, send):
    for at in range(keep.shape[0]):
        keep[at] = every[2 * at + low]
        send[at] = every[2 * at + 1 - low]


def early_kernel(
    heads, count, every,
    low, total, y, gate, gg, gain, gy, x, bc, scal, sin, cot, series, rim, cw, slope,
    normed, grad_gate, gp, gb, edge, keep, send, wide, stage,
):
    length, width = y.shape
    depth = series.shape[1]
    rows = scal[...]
    cols = columns(rows)
    xv = x[...]
    gyv = gy[...].astype(BF16)
    b, c = bc[:, 0:N], bc[:, N:]
    group = jnp.zeros((length, length), F32)
    for h in range(heads):
        pairs = mm(only_head(gyv, h, heads), xv, NT)
        group = group + decay_of(cols, rows, h) * pairs * rows[heads + h : heads + h + 1, :]
    gb[...] = mm(group, c, TN)
    grow = widen(columns(jnp.exp(rows[0:heads])), heads, width)
    grad_c = mm(group, b) + mm(gy[...] * grow, sin[...])
    clear_ends(wide, length)
    wide[RIM : RIM + length, :] = grad_c * slope[:, 2 * width - N :]
    grad_pre = conv_back(cw, wide, slice(0, N), length, 1, slice(width - N, width))
    edge[...] = grad_pre[0:RIM]
    gp[...] = grad_pre[RIM:]
    cols = norm_columns(total[...], every)
    g = gate[...].astype(F32)
    sig = sigmoid(g)
    yv = y[...]
    gated = yv * (g * sig)
    normed[...] = (gated * cols[:, 0:1] * gain[...]).astype(BF16)
    grad_gated = cols[:, 0:1] * gg[...] - gated * cols[:, 1:2]
    grad_gate[...] = (grad_gated * yv * (sig * (1.0 + g * (1.0 - sig)))).astype(BF16)
    w_out = mm(cot[...], normed[...], TN).astype(BF16)
    w_gate = mm(series[...], grad_gate[...], TN).astype(BF16)
    w_c = (mm(series[...], gp[...], TN) + mm(rim[...], edge[...], TN)).astype(BF16)
    piece = depth // count
    for at in range(count):
        stack_columns(stage, w_out, at, 0, piece)
        stack_columns(stage, w_gate, at, 2, piece)
        stack_columns(stage, w_c, at, 4, piece)
    split_pair(low[0], stage, keep, send)


def beside_kernel(
    heads, normed, grad_gate, gp, y, gy, x, bc, scal, ow, w, skip,
    out, sg, bb, yb,
):
    length, width = y.shape
    rows = scal[...]
    cols = columns(rows)
    xv = x[...].astype(F32)
    gyv = gy[...]
    scores = mm(bc[:, N:], bc[:, 0:N], NT)
    back = jnp.zeros((length, width), F32)
    for h in range(heads):
        back = back + mm(scores * decay_of(cols, rows, h), only_head(gyv, h, heads), TN)
    bb[...] = back
    skips = per_lane(skip, heads, width)
    yb[...] = mm_exact(head_mask(heads, width), gyv * (y[...] - skips * xv), NT)
    out[...] = mm(normed[...], ow[...], NT).astype(BF16)
    sg[...] = mm(grad_gate[...], w[0], NT) + mm(gp[...], w[2, :, width - N :], NT)


def close_kernel(
    heads,
    low, x, bc, scal, gy, bb, gb, slope, cw, edge_c, skip, partner, *rest,
):
    *others, after, back, gp, lead, edge, wide = rest
    length, width = gy.shape
    state = carried(low[0] == 0, partner[...], [o[...] for o in others], heads)
    after[...] = state
    rows = scal[...]
    running, step = rows[0:heads], rows[heads : 2 * heads]
    remain = jnp.exp(running[:, length - 1 : length] - running)
    cols = columns(jnp.concatenate([remain, step, remain * step], axis=0))
    grown = bb[...] + widen(cols, heads, width) * mm(bc[:, 0:N], state, NT)
    back[...] = grown
    grad_x = per_lane(skip, heads, width) * gy[...] + widen(cols[:, heads:], heads, width) * grown
    grad_b = gb[...] + mm(x[...].astype(F32) * widen(cols[:, 2 * heads :], heads, width), state)
    clear_ends(wide, length)
    wide[RIM : RIM + length, 0:width] = grad_x * slope[:, 0:width]
    wide[RIM : RIM + length, width:] = grad_b * slope[:, width : width + N]
    grad_x = conv_back(cw, wide, slice(0, width), length, 0, slice(0, width))
    grad_b = conv_back(cw, wide, slice(width, width + N), length, 1, slice(0, N))
    for out, cut in ((lead, slice(0, RIM)), (gp, slice(RIM, RIM + length))):
        out[:, 0:width] = grad_x[cut]
        out[:, width:] = grad_b[cut]
    edge[:, 0 : width + N] = lead[...]
    edge[:, width + N :] = edge_c[...]


def late_kernel(
    heads, count,
    low, x, scal, after, back, gp, lead, yb, sin, own, series, rim, rate,
    keep, send, graw, stage,
):
    length, width = back.shape
    depth = series.shape[1]
    w_xb = (mm(series[...], gp[...], TN) + mm(rim[...], lead[...], TN)).astype(BF16)
    rows = scal[...]
    step = rows[heads : 2 * heads]
    last = jnp.broadcast_to(rows[0:heads, length - 1 : length], (heads, N))
    mask = head_mask(heads, width)
    x_back = mm_exact(mask, x[...].astype(F32) * back[...], NT)[0:heads]
    final = jnp.exp(spread_rows(last, heads, width)) * sin[...] + own[...]
    ends = jnp.sum(mm_exact(mask, after[...] * final), axis=1, keepdims=True)[0:heads]
    grad_log = running_sum_back(yb[0:heads, :] - step * x_back) + ends
    grad_step = x_back - jnp.exp(per_row(rate, x_back.shape)) * grad_log
    grad_raw = grad_step * rows[2 * heads : 3 * heads]
    grad_raw = jnp.concatenate([grad_raw, jnp.zeros_like(grad_raw)], axis=0)
    graw[...] = grad_raw
    dt = mm(grad_raw, series[...])
    piece = depth // count
    blank = jnp.zeros((LOGS, N), F32)
    for at in range(count):
        stack_columns(stage, w_xb, at, 0, piece)
        dt_piece = jnp.concatenate(
            [dt[:, at * piece : (at + 1) * piece], blank[0 : 2 * heads, 0 : N - piece]], axis=1
        )
        dt_piece = jnp.concatenate([dt_piece, blank[0 : LOGS - 2 * heads]], axis=0)
        stage[at, 3 * piece :, :] = dt_piece.astype(BF16)
    split_pair(low[0], stage, keep, send)


def halve_kernel(high, keep, other, own, *parts):
    at = high[0]
    own[...] = keep[at].astype(F32) + other[at].astype(F32)
    for k, part in enumerate(parts):
        at = high[0] ^ (k + 1)
        part[...] = (keep[at].astype(F32) + other[at].astype(F32)).astype(BF16)


def rows_kernel(low, out, sg, gp, graw, edge, w, dtw, keep, send, stage):
    length, depth = sg.shape
    width = w.shape[2]
    heads = dtw.shape[0]
    total = sg[...] + mm(graw[0:heads, :], dtw[...], TN)
    total = total + mm(gp[:, 0:width], w[1], NT) + mm(gp[:, width:], w[2, :, 0:N], NT)
    late = mm(edge[:, 0:width], w[1], NT) + mm(edge[:, width:], w[2], NT)
    stage[:, 0:depth] = out[...]
    stage[:, depth:] = total.astype(BF16)
    stage[length - RIM :, depth:] = (total[length - RIM :, :] + late).astype(BF16)
    piece = keep.shape[1]
    for at in range(keep.shape[0]):
        start = pl.multiple_of((2 * at + low[0]) * piece, piece)
        keep[at] = stage[pl.ds(start, piece), :]
        start = pl.multiple_of((2 * at + 1 - low[0]) * piece, piece)
        send[at] = stage[pl.ds(start, piece), :]


def outputs_kernel(*refs):
    *parts, layer, grad = refs
    depth = layer.shape[1]
    total = parts[0][...].astype(F32)
    for part in parts[1:]:
        total = total + part[...].astype(F32)
    layer[...] = total[:, 0:depth].astype(BF16)
    grad[...] = total[:, depth:]


def total_kernel(hops, *refs):
    early, late = refs[0:hops], refs[hops : 2 * hops]
    w_in, w_dt, w_out = refs[2 * hops :]
    piece = w_out.shape[0]

    def sum_of(parts):
        total = parts[0][...]
        for part in parts[1:]:
            total = total + part[...].astype(F32)
        return total

    def laid(total, base):
        return total[base * piece : (base + 1) * piece, :]

    early, late = sum_of(early), sum_of(late)
    for q in range(2):
        cut = slice(q * N, (q + 1) * N)
        w_out[:, cut] = laid(early, q)
        w_in[0, :, cut] = laid(early, 2 + q)
        w_in[1, :, cut] = laid(late, q)
    w_in[2, :, 0:N] = laid(late, 2)
    w_in[2, :, N:] = laid(early, 4)
    w_dt[...] = late[3 * piece : 3 * piece + w_dt.shape[0], 0:piece]


VMEM = pl.BlockSpec(memory_space=pltpu.VMEM)
SMEM = pl.BlockSpec(memory_space=pltpu.SMEM)
HBM = pl.BlockSpec(memory_space=pltpu.HBM)


def run(kernel, name, outs, args, scalars=(), fetched=(), scratch=()):
    args = [
        pltpu.with_memory_space_constraint(a, pltpu.HBM) if i in fetched else a
        for i, a in enumerate(args)
    ]

    def place(i):
        if i in fetched:
            return HBM
        return SMEM if i in scalars else VMEM

    def whole(*refs):
        held, sems = refs[len(refs) - len(fetched) - 1 : -1], refs[-1]
        refs = list(refs[: len(refs) - len(fetched) - 1])
        copies = []
        for k, i in enumerate(fetched):
            copies.append(pltpu.make_async_copy(refs[i], held[k], sems.at[k]))
            refs[i] = held[k]
        for copy in copies:
            copy.start()
        for copy in copies:
            copy.wait()
        kernel(*refs)

    holders = []
    if fetched:
        for i in fetched:
            kind = pltpu.SMEM if i in scalars else pltpu.VMEM
            holders.append(kind(args[i].shape, args[i].dtype))
        holders.append(pltpu.SemaphoreType.DMA((len(fetched),)))
    return pl.pallas_call(
        whole if fetched else kernel,
        name=name,
        out_shape=[jax.ShapeDtypeStruct(shape, kind) for shape, kind in outs],
        in_specs=[place(i) for i in range(len(args))],
        out_specs=[VMEM] * len(outs),
        scratch_shapes=list(scratch) + holders,
        compiler_params=pltpu.CompilerParams(vmem_limit_bytes=LIMIT),
        cost_estimate=pl.CostEstimate(flops=10**6, bytes_accessed=2**14, transcendentals=0),
    )(*args)


def shifted(block, axis, distance):
    devices = range(lax.axis_size(axis))
    route = [(i - distance, i) for i in devices if i - distance in devices]
    return lax.ppermute(block, axis, route)


def swapped(block, axis, flip):
    return lax.ppermute(block, axis, [(i, i ^ flip) for i in range(lax.axis_size(axis))])


def body(
    series,
    in_weight,
    step_weight,
    step_bias,
    log_rate,
    conv_weight,
    conv_bias,
    skip_gain,
    norm_gain,
    out_weight,
    cotangent,
):
    length, depth = series.shape
    width = in_weight.shape[2]
    heads = step_weight.shape[1]
    count = lax.axis_size("tm")
    parts = lax.axis_size("head")
    every = width * parts
    assert width == 2 * N and heads == 4
    part = functools.partial
    w = in_weight.transpose(1, 0, 2)
    dtw = step_weight.T
    gain = norm_gain.reshape(1, width)
    hops = count // 2
    piece = depth // count
    position = lax.axis_index("tm").astype(jnp.int32)
    spot = lax.axis_index("head").astype(jnp.int32)
    low, high = (position % 2).reshape(1), (position // 2).reshape(1)
    low_spot, high_spot = (spot % 2).reshape(1), (spot // 2).reshape(1)
    rim = shifted(series[length - RIM :], "tm", 1)
    state_msg = ((width + LOGS, N), BF16)

    def passed(msg, back, during):
        made = []

        def meanwhile(k, block):
            if k < len(during):
                block, extra = lax.optimization_barrier((block, during[k](made)))
                made.append(extra)
            return block

        partner = meanwhile(0, swapped(msg, "tm", 1))
        (msg,) = run(part(pair_kernel, heads, back), "pair", [state_msg], [low, msg, partner], (0,))
        entered = []
        hop = 1
        while hop < hops:
            other = meanwhile(len(made), shifted(msg, "tm", (-2 if back else 2) * hop))
            entered.append(other)
            hop *= 2
            if hop < hops:
                (msg,) = run(part(link_kernel, heads), "link", [state_msg], [other, msg])
        return [partner] + entered[::-1], made

    def halved(keep, send, axis, where, name):
        most, rows, cols = keep.shape
        return run(
            halve_kernel, name, [((rows, cols), F32)] + [((rows, cols), BF16)] * (most - 1),
            [where, keep, swapped(send, axis, 1)], (0,),
        )

    def gathered(blocks, axis):
        return [blocks[0]] + [swapped(block, axis, 2 * k) for k, block in enumerate(blocks) if k]

    gate, pre, scal = run(
        part(project_kernel, heads), "project",
        [((length, width), BF16), ((length, 2 * width), BF16), ((4 * heads, length), F32)],
        [series, w, dtw, step_bias, log_rate], (3, 4), (0, 1, 2, 3, 4),
    )
    x, bc, conv, own, msg = run(
        part(conv_kernel, heads), "conv",
        [
            ((length, width), BF16),
            ((length, width), BF16),
            ((length, 2 * width), F32),
            ((width, N), F32),
            state_msg,
        ],
        [pre, rim, w, conv_weight, conv_bias, scal], (), (2, 3, 4),
        scratch=[pltpu.VMEM((length + 8, 2 * width), F32)],
    )

    def inner(made):
        return run(
            part(inside_kernel, heads), "inside",
            [((length, width), F32), ((length, width), F32), ((length, 2 * width), F32)],
            [x, bc, scal, skip_gain, cotangent, out_weight, gain, conv], (3,), (3, 4, 5, 6),
        )

    ahead, ((inside, gg, slope),) = passed(msg, False, [inner])
    y, sin, sums = run(
        part(join_kernel, heads), "join",
        [((length, width), F32), ((width, N), F32), ((8, length), F32)],
        [low, inside, gg, gate, bc, scal] + ahead, (0,),
    )
    flip = 1
    while 2 * flip < parts:
        sums = sums + swapped(sums, "head", flip)
        flip *= 2
    gy, msg, total = run(
        part(grad_y_kernel, heads, every), "grad_y",
        [((length, width), F32), state_msg, ((8, length), F32)],
        [sums, swapped(sums, "head", flip), y, gate, gg, bc, scal],
    )
    early, late = 5 * piece, 3 * piece + LOGS

    def early_part(made):
        return run(
            part(early_kernel, heads, count, every), "early",
            [
                ((length, width), BF16),
                ((length, width), BF16),
                ((length, N), BF16),
                ((length, N), F32),
                ((RIM, N), BF16),
                ((hops, early, N), BF16),
                ((hops, early, N), BF16),
            ],
            [
                low, total, y, gate, gg, gain, gy, x, bc, scal, sin, cotangent, series, rim,
                conv_weight, slope,
            ],
            (0,), (5, 11, 12, 14),
            scratch=[
                pltpu.VMEM((length + RIM + 8, N), F32),
                pltpu.VMEM((count, early, N), BF16),
            ],
        )

    def beside_part(made):
        normed, grad_gate, gp_c = made[0][0:3]
        return run(
            part(beside_kernel, heads), "beside",
            [
                ((length, depth), BF16),
                ((length, depth), F32),
                ((length, width), F32),
                ((8, length), F32),
            ],
            [normed, grad_gate, gp_c, y, gy, x, bc, scal, out_weight, w, skip_gain],
            (10,), (8, 9, 10),
        )

    behind, (firsts, (out, sg, bb, yb)) = passed(msg, True, [early_part, beside_part])
    gb, edge_c, keep, send = firsts[3:]
    early_parts = halved(keep, send, "tm", high, "halve_early")
    behind, early_parts = lax.optimization_barrier((behind, early_parts))
    early_parts = gathered(early_parts, "tm")
    after, back, gp, lead, edge = run(
        part(close_kernel, heads), "close",
        [
            ((width, N), F32),
            ((length, width), F32),
            ((length, width + N), BF16),
            ((RIM, width + N), BF16),
            ((RIM, 2 * width), BF16),
        ],
        [low, x, bc, scal, gy, bb, gb, slope, conv_weight, edge_c, skip_gain] + behind,
        (0, 10), (8, 10),
        scratch=[pltpu.VMEM((length + RIM + 8, width + N), F32)],
    )
    edge = shifted(edge, "tm", -1)
    keep, send, graw = run(
        part(late_kernel, heads, count), "late",
        [((hops, late, N), BF16), ((hops, late, N), BF16), ((2 * heads, length), F32)],
        [low, x, scal, after, back, gp, lead, yb, sin, own, series, rim, log_rate],
        (0, 12), (10, 12),
        scratch=[pltpu.VMEM((count, late, N), BF16)],
    )
    late_parts = halved(keep, send, "tm", high, "halve_late")
    late_parts = gathered(late_parts, "tm")
    rows = length // parts
    keep, send = run(
        rows_kernel, "rows",
        [((parts // 2, rows, 2 * depth), BF16)] * 2,
        [low_spot, out, sg, gp, graw, edge, w, dtw], (0,), (6, 7),
        scratch=[pltpu.VMEM((length, 2 * depth), BF16)],
    )
    both = gathered(halved(keep, send, "head", high_spot, "halve_rows"), "head")
    layer_out, series_grad = run(
        outputs_kernel, "outputs", [((rows, depth), BF16), ((rows, depth), F32)], both,
    )
    w_in_grad, w_dt_grad, w_out_grad = run(
        part(total_kernel, hops), "total",
        [((3, piece, width), F32), ((heads, piece), F32), ((piece, width), F32)],
        early_parts + late_parts,
    )
    return (layer_out, series_grad, w_in_grad.transpose(1, 0, 2), w_dt_grad.T, w_out_grad)


def solution(mesh):
    in_specs = (
        P("tm", None),
        P(None, None, "head"),
        P(None, "head"),
        P("head"),
        P("head"),
        P(None, None, "head"),
        P(None, "head"),
        P("head"),
        P("head"),
        P(None, "head"),
        P("tm", None),
    )
    out_specs = (
        P(("tm", "head"), None),
        P(("tm", "head"), None),
        P("tm", None, "head"),
        P("tm", "head"),
        P("tm", "head"),
    )
    return jax.shard_map(body, mesh=mesh, in_specs=in_specs, out_specs=out_specs, check_vma=False)
```

```python
import functools

import jax
import jax.numpy as jnp
from jax import lax
from jax.experimental import pallas as pl
from jax.experimental.pallas import tpu as pltpu
from jax.sharding import PartitionSpec as P

N = 128
KW = 4
RIM = 16
LIMIT = 12 * 2**20
SKIP, GAIN, BIAS, TAPS, SCALARS = 16, 17, 18, 20, 32
LOGS = 16
NORM_EPSILON = 1e-05

F32 = jnp.float32
BF16 = jnp.bfloat16
NN = (((1,), (0,)), ((), ()))
NT = (((1,), (1,)), ((), ()))
TN = (((0,), (0,)), ((), ()))


def mm(a, b, dims=NN):
    return lax.dot_general(a.astype(BF16), b.astype(BF16), dims, preferred_element_type=F32)


def mm_exact(a, b, dims=NN):
    return lax.dot_general(
        a, b, dims, precision=lax.Precision.HIGHEST, preferred_element_type=F32
    )


def lanes_of(shape):
    return lax.broadcasted_iota(jnp.int32, shape, len(shape) - 1)


def rows_of(shape):
    return lax.broadcasted_iota(jnp.int32, shape, len(shape) - 2)


def per_row(ref, shape):
    rows = rows_of(shape)
    out = jnp.full(shape, ref[0], F32)
    for h in range(1, shape[0]):
        out = jnp.where(rows == h, ref[h], out)
    return out


def per_lane(ref, heads, width):
    head = lanes_of((1, width)) // (width // heads)
    out = jnp.full((1, width), ref[0], F32)
    for h in range(1, heads):
        out = jnp.where(head == h, ref[h], out)
    return out


def widen(cols, heads, width):
    head = lanes_of((cols.shape[0], width)) // (width // heads)
    out = jnp.broadcast_to(cols[:, 0:1], (cols.shape[0], width))
    for h in range(1, heads):
        out = jnp.where(head == h, cols[:, h : h + 1], out)
    return out


def head_mask(heads, width):
    shape = (8, width)
    return jnp.where(lanes_of(shape) // (width // heads) == rows_of(shape), 1.0, 0.0)


def only_head(x, h, heads):
    width = x.shape[1]
    return jnp.where(lanes_of(x.shape) // (width // heads) == h, x, jnp.zeros_like(x))


def tap(scal, k, slot):
    return scal[TAPS + 2 * k + slot : TAPS + 2 * k + slot + 1, :]


def columns(rows):
    short = -rows.shape[0] % 8
    if short:
        rows = jnp.concatenate([rows, jnp.zeros((short, rows.shape[1]), F32)], axis=0)
    return jnp.transpose(rows)


def sigmoid(v):
    return 1.0 / (1.0 + jnp.exp(-v))


def running_sum(x):
    width = x.shape[1]
    lanes = lanes_of(x.shape)
    hop = 1
    while hop < width:
        x = x + jnp.where(lanes >= hop, pltpu.roll(x, hop, 1), 0.0)
        hop *= 2
    return x


def running_sum_back(x):
    width = x.shape[1]
    lanes = lanes_of(x.shape)
    hop = 1
    while hop < width:
        x = x + jnp.where(lanes < width - hop, pltpu.roll(x, width - hop, 1), 0.0)
        hop *= 2
    return x


def decay_of(cols, rows, h):
    length = cols.shape[0]
    gap = cols[:, h : h + 1] - rows[h : h + 1, :]
    shape = (length, length)
    return jnp.exp(jnp.where(lanes_of(shape) <= rows_of(shape), gap, -1e30))


def logs_of(msg, heads):
    logs = msg[msg.shape[0] - LOGS :].astype(F32)
    return logs[0:heads] + logs[heads : 2 * heads] + logs[2 * heads : 3 * heads]


def spread_rows(logs, heads, size):
    return jnp.concatenate(
        [jnp.broadcast_to(logs[h : h + 1], (size // heads, N)) for h in range(heads)], axis=0
    )


def state_of(msg):
    return msg[0 : msg.shape[0] - LOGS].astype(F32)


def packed(state, logs):
    high = logs.astype(BF16).astype(F32)
    middle = (logs - high).astype(BF16).astype(F32)
    low = logs - high - middle
    logs = jnp.concatenate([high, middle, low, jnp.zeros_like(low)], axis=0)
    return jnp.concatenate([state.astype(BF16), logs.astype(BF16)], axis=0)


def carried(own_turn, partner, others, heads):
    state = jnp.zeros((partner.shape[0] - LOGS, N), F32)
    size = state.shape[0]
    for msg in others:
        state = jnp.exp(spread_rows(logs_of(msg, heads), heads, size)) * state + state_of(msg)
    with_partner = jnp.exp(spread_rows(logs_of(partner, heads), heads, size)) * state
    return jnp.where(own_turn, with_partner + state_of(partner), state)


def project_kernel(
    heads, series, w, dtw, bias, rate, skip, gain, cw, cb, gate, pre, scal, w_xbc,
):
    width = w.shape[2]
    s = series[...]
    gate[...] = mm(s, w[0]).astype(BF16)
    pre[:, 0:width] = mm(s, w[1]).astype(BF16)
    pre[:, width:] = mm(s, w[2]).astype(BF16)
    w_xbc[0] = w[1]
    w_xbc[1] = w[2]
    raw = mm(dtw[...], s, NT)
    shifted = raw + per_row(bias, raw.shape)
    step = jnp.maximum(shifted, 0.0) + jnp.log1p(jnp.exp(-jnp.abs(shifted)))
    rates = jnp.exp(per_row(rate, raw.shape))
    scal[0:heads, :] = running_sum(-step * rates)
    scal[heads : 2 * heads, :] = step
    scal[2 * heads : 3 * heads, :] = sigmoid(shifted)
    scal[3 * heads : SKIP, :] = rates
    scal[SKIP : SKIP + 1, :] = per_lane(skip, heads, width)
    scal[GAIN : GAIN + 1, :] = gain[...]
    scal[BIAS : BIAS + 2, :] = cb[...]
    for k in range(KW):
        scal[TAPS + 2 * k : TAPS + 2 * k + 2, :] = cw[k]
    scal[TAPS + 2 * KW :, :] = jnp.zeros((SCALARS - TAPS - 2 * KW, width), F32)


def conv_kernel(heads, pre, rim, w, scal, x, bc, conv, msg, wide):
    length, both = pre.shape
    width = both // 2
    for s in range(2):
        cut = slice(s * width, (s + 1) * width)
        rims = mm(rim[...], w[s]).astype(BF16).astype(F32)
        wide[0:8, cut] = rims[RIM - 8 :, :]
        wide[8:, cut] = pre[:, cut].astype(F32)
        acc = scal[BIAS + s : BIAS + s + 1, :] + tap(scal, 0, s) * wide[5 : 5 + length, cut]
        for k in range(1, KW):
            acc = acc + tap(scal, k, s) * wide[5 + k : 5 + k + length, cut]
        conv[:, cut] = acc
        act = (acc * sigmoid(acc)).astype(BF16)
        if s == 0:
            x[...] = act
        else:
            bc[...] = act
    running = scal[0:heads, :]
    last = running[:, length - 1 : length]
    remain = jnp.exp(last - running) * scal[heads : 2 * heads, :]
    scaled = x[...].astype(F32) * widen(columns(remain), heads, width)
    state = mm(scaled, bc[:, 0:N], TN)
    msg[...] = packed(state, jnp.broadcast_to(last, (heads, N)))


def pair_kernel(heads, back, low, mine, other, msg):
    mine, other = mine[...], other[...]
    size = mine.shape[0] - LOGS
    mine_first = low[0] == 0
    mine_logs, other_logs = logs_of(mine, heads), logs_of(other, heads)
    crossed = jnp.logical_not(mine_first) if back else mine_first
    mine_scale = jnp.where(crossed, jnp.exp(other_logs), 1.0)
    other_scale = jnp.where(crossed, 1.0, jnp.exp(mine_logs))
    state = spread_rows(mine_scale, heads, size) * state_of(mine)
    state = state + spread_rows(other_scale, heads, size) * state_of(other)
    msg[...] = packed(state, mine_logs + other_logs)


def link_kernel(heads, farther, nearer, msg):
    farther, nearer = farther[...], nearer[...]
    size = nearer.shape[0] - LOGS
    logs = logs_of(nearer, heads)
    state = jnp.exp(spread_rows(logs, heads, size)) * state_of(farther) + state_of(nearer)
    msg[...] = packed(state, logs + logs_of(farther, heads))


def inside_kernel(heads, x, bc, scal, cot, ow, conv, y, gg, slope):
    length, width = x.shape
    xv = x[...].astype(F32)
    rows = scal[0 : 2 * heads, :]
    cols = columns(rows)
    scores = mm(bc[:, N:], bc[:, 0:N], NT)
    acc = scal[SKIP : SKIP + 1, :] * xv
    for h in range(heads):
        mixing = scores * decay_of(cols, rows, h) * rows[heads + h : heads + h + 1, :]
        acc = acc + mm(mixing, only_head(xv, h, heads))
    y[...] = acc
    gg[...] = scal[GAIN : GAIN + 1, :] * mm(cot[...], ow[...])
    v = conv[...]
    sig = sigmoid(v)
    slope[...] = sig * (1.0 + v * (1.0 - sig))


def join_kernel(heads, low, yi, gg, gate, bc, scal, partner, *rest):
    *others, y, sin, sums = rest
    length, width = yi.shape
    start = carried(low[0] == 1, partner[...], [o[...] for o in others], heads)
    sin[...] = start
    grow = widen(columns(jnp.exp(scal[0:heads, :])), heads, width)
    yv = yi[...] + grow * mm(bc[:, N:], start, NT)
    y[...] = yv
    g = gate[...].astype(F32)
    gated = yv * (g * sigmoid(g))
    ones = jnp.ones((8, width), F32)
    square = mm_exact(ones, gated * gated, NT)
    inner = mm_exact(ones, gated * gg[...], NT)
    sums[...] = jnp.where(rows_of(square.shape) == 0, square, inner)


def norm_columns(total, every):
    inv = lax.rsqrt(total[0:1, :] / every + NORM_EPSILON)
    coef = inv * inv * inv * total[1:2, :] / every
    return columns(jnp.concatenate([inv, coef], axis=0))


def grad_y_kernel(heads, every, sums, other, y, gate, gg, bc, scal, gy, msg, total):
    length, width = y.shape
    total[...] = sums[...] + other[...]
    cols = norm_columns(total[...], every)
    g = gate[...].astype(F32)
    act = g * sigmoid(g)
    gated = y[...] * act
    grad = (cols[:, 0:1] * gg[...] - gated * cols[:, 1:2]) * act
    gy[...] = grad
    grow = widen(columns(jnp.exp(scal[0:heads, :])), heads, width)
    last = scal[0:heads, length - 1 : length]
    msg[...] = packed(mm(grad * grow, bc[:, N:], TN), jnp.broadcast_to(last, (heads, N)))


def conv_back(scal, wide, cut, length, slot, slot_cut):
    acc = tap(scal, 0, slot)[:, slot_cut] * wide[KW - 1 : KW - 1 + RIM + length, cut]
    for k in range(1, KW):
        at = KW - 1 - k
        acc = acc + tap(scal, k, slot)[:, slot_cut] * wide[at : at + RIM + length, cut]
    return acc.astype(BF16)


def clear_ends(wide, length):
    zeros = jnp.zeros((RIM, wide.shape[1]), F32)
    wide[0:RIM, :] = zeros
    wide[RIM + length :, :] = zeros[0:8]


def stack_columns(msg, grad, at, base, piece):
    for q in range(grad.shape[1] // N):
        msg[at, (base + q) * piece : (base + q + 1) * piece, :] = grad[
            at * piece : (at + 1) * piece, q * N : (q + 1) * N
        ]


def split_pair(low, every, keep, send):
    for at in range(keep.shape[0]):
        keep[at] = every[2 * at + low]
        send[at] = every[2 * at + 1 - low]


def early_kernel(
    heads, count, every,
    low, total, y, gate, gg, gy, x, bc, scal, sin, cot, series, rim, slope,
    normed, grad_gate, gp, gb, edge, keep, send, wide, stage,
):
    length, width = y.shape
    depth = series.shape[1]
    rows = scal[0 : 2 * heads, :]
    cols = columns(rows)
    xv = x[...]
    gyv = gy[...].astype(BF16)
    b, c = bc[:, 0:N], bc[:, N:]
    group = jnp.zeros((length, length), F32)
    for h in range(heads):
        pairs = mm(only_head(gyv, h, heads), xv, NT)
        group = group + decay_of(cols, rows, h) * pairs * rows[heads + h : heads + h + 1, :]
    gb[...] = mm(group, c, TN)
    grow = widen(columns(jnp.exp(rows[0:heads])), heads, width)
    grad_c = mm(group, b) + mm(gy[...] * grow, sin[...])
    clear_ends(wide, length)
    wide[RIM : RIM + length, :] = grad_c * slope[:, 2 * width - N :]
    grad_pre = conv_back(scal, wide, slice(0, N), length, 1, slice(width - N, width))
    edge[...] = grad_pre[0:RIM]
    gp[...] = grad_pre[RIM:]
    cols = norm_columns(total[...], every)
    g = gate[...].astype(F32)
    sig = sigmoid(g)
    yv = y[...]
    gated = yv * (g * sig)
    normed[...] = (gated * cols[:, 0:1] * scal[GAIN : GAIN + 1, :]).astype(BF16)
    grad_gated = cols[:, 0:1] * gg[...] - gated * cols[:, 1:2]
    grad_gate[...] = (grad_gated * yv * (sig * (1.0 + g * (1.0 - sig)))).astype(BF16)
    w_out = mm(cot[...], normed[...], TN).astype(BF16)
    w_gate = mm(series[...], grad_gate[...], TN).astype(BF16)
    w_c = (mm(series[...], gp[...], TN) + mm(rim[...], edge[...], TN)).astype(BF16)
    piece = depth // count
    for at in range(count):
        stack_columns(stage, w_out, at, 0, piece)
        stack_columns(stage, w_gate, at, 2, piece)
        stack_columns(stage, w_c, at, 4, piece)
    split_pair(low[0], stage, keep, send)


def beside_kernel(
    heads, normed, grad_gate, gp, gb, y, gy, x, bc, scal, sin, ow, w, series,
    out, sg, held, yb, turned,
):
    length, width = y.shape
    rows = scal[0 : 2 * heads, :]
    cols = columns(rows)
    xv = x[...].astype(F32)
    gyv = gy[...]
    scores = mm(bc[:, N:], bc[:, 0:N], NT)
    back = jnp.zeros((length, width), F32)
    for h in range(heads):
        back = back + mm(scores * decay_of(cols, rows, h), only_head(gyv, h, heads), TN)
    held[:, 0:width] = back
    held[:, width : width + N] = gb[...]
    last = rows[0:heads, length - 1 : length]
    remain = jnp.exp(last - rows[0:heads]) * rows[heads:]
    own = mm(xv * widen(columns(remain), heads, width), bc[:, 0:N], TN)
    whole = jnp.exp(spread_rows(jnp.broadcast_to(last, (heads, N)), heads, width))
    held[:, width + N :] = whole * sin[...] + own
    turned[...] = jnp.transpose(series[...])
    skips = scal[SKIP : SKIP + 1, :]
    yb[...] = mm_exact(head_mask(heads, width), gyv * (y[...] - skips * xv), NT)
    out[...] = mm(normed[...], ow[...], NT).astype(BF16)
    sg[...] = mm(grad_gate[...], w[0], NT) + mm(gp[...], w[2, :, width - N :], NT)


def close_kernel(
    heads,
    low, x, bc, scal, gy, held, slope, edge_c, partner, *rest,
):
    *others, back, gp, lead, edge, wide = rest
    length, width = gy.shape
    state = carried(low[0] == 0, partner[...], [o[...] for o in others], heads)
    back[:, width:] = state
    running, step = scal[0:heads, :], scal[heads : 2 * heads, :]
    remain = jnp.exp(running[:, length - 1 : length] - running)
    cols = columns(jnp.concatenate([remain, step, remain * step], axis=0))
    grown = held[:, 0:width] + widen(cols, heads, width) * mm(bc[:, 0:N], state, NT)
    back[:, 0:width] = grown
    grad_x = scal[SKIP : SKIP + 1, :] * gy[...] + widen(cols[:, heads:], heads, width) * grown
    grad_b = held[:, width : width + N] + mm(x[...].astype(F32) * widen(cols[:, 2 * heads :], heads, width), state)
    clear_ends(wide, length)
    wide[RIM : RIM + length, 0:width] = grad_x * slope[:, 0:width]
    wide[RIM : RIM + length, width:] = grad_b * slope[:, width : width + N]
    grad_x = conv_back(scal, wide, slice(0, width), length, 0, slice(0, width))
    grad_b = conv_back(scal, wide, slice(width, width + N), length, 1, slice(0, N))
    for out, cut in ((lead, slice(0, RIM)), (gp, slice(RIM, RIM + length))):
        out[:, 0:width] = grad_x[cut]
        out[:, width:] = grad_b[cut]
    edge[:, 0 : width + N] = lead[...]
    edge[:, width + N :] = edge_c[...]


def late_kernel(
    heads, count,
    low, x, scal, back, gp, lead, yb, held, turned, series, rim,
    keep, send, graw, stage,
):
    length, width = x.shape
    depth = series.shape[1]
    w_xb = (mm(turned[...], gp[...]) + mm(rim[...], lead[...], TN)).astype(BF16)
    rows = scal[0 : 4 * heads, :]
    step = rows[heads : 2 * heads]
    mask = head_mask(heads, width)
    x_back = mm_exact(mask, x[...].astype(F32) * back[:, 0:width], NT)[0:heads]
    ends = jnp.sum(mm_exact(mask, back[:, width:] * held[:, width + N :]), axis=1, keepdims=True)[0:heads]
    grad_log = running_sum_back(yb[0:heads, :] - step * x_back) + ends
    grad_step = x_back - rows[3 * heads :] * grad_log
    grad_raw = grad_step * rows[2 * heads : 3 * heads]
    grad_raw = jnp.concatenate([grad_raw, jnp.zeros_like(grad_raw)], axis=0)
    graw[...] = grad_raw
    dt = mm(grad_raw, series[...])
    piece = depth // count
    blank = jnp.zeros((LOGS, N), F32)
    for at in range(count):
        stack_columns(stage, w_xb, at, 0, piece)
        dt_piece = jnp.concatenate(
            [dt[:, at * piece : (at + 1) * piece], blank[0 : 2 * heads, 0 : N - piece]], axis=1
        )
        dt_piece = jnp.concatenate([dt_piece, blank[0 : LOGS - 2 * heads]], axis=0)
        stage[at, 3 * piece :, :] = dt_piece.astype(BF16)
    split_pair(low[0], stage, keep, send)


def halve_kernel(high, keep, other, own, *parts):
    at = high[0]
    own[...] = keep[at].astype(F32) + other[at].astype(F32)
    for k, part in enumerate(parts):
        at = high[0] ^ (k + 1)
        part[...] = (keep[at].astype(F32) + other[at].astype(F32)).astype(BF16)


def rows_kernel(low, out, sg, gp, graw, edge, w, dtw, keep, send, stage):
    length, depth = sg.shape
    width = w.shape[2]
    heads = dtw.shape[0]
    total = sg[...] + mm(graw[0:heads, :], dtw[...], TN)
    total = total + mm(gp[:, 0:width], w[1], NT) + mm(gp[:, width:], w[2, :, 0:N], NT)
    late = mm(edge[:, 0:width], w[1], NT) + mm(edge[:, width:], w[2], NT)
    stage[:, 0:depth] = out[...]
    stage[:, depth:] = total.astype(BF16)
    stage[length - RIM :, depth:] = (total[length - RIM :, :] + late).astype(BF16)
    piece = keep.shape[1]
    for at in range(keep.shape[0]):
        start = pl.multiple_of((2 * at + low[0]) * piece, piece)
        keep[at] = stage[pl.ds(start, piece), :]
        start = pl.multiple_of((2 * at + 1 - low[0]) * piece, piece)
        send[at] = stage[pl.ds(start, piece), :]


def outputs_kernel(*refs):
    *parts, layer, grad = refs
    depth = layer.shape[1]
    total = parts[0][...].astype(F32)
    for part in parts[1:]:
        total = total + part[...].astype(F32)
    layer[...] = total[:, 0:depth].astype(BF16)
    grad[...] = total[:, depth:]


def total_kernel(hops, *refs):
    early, late = refs[0:hops], refs[hops : 2 * hops]
    w_in, w_dt, w_out = refs[2 * hops :]
    piece = w_out.shape[0]

    def sum_of(parts):
        total = parts[0][...]
        for part in parts[1:]:
            total = total + part[...].astype(F32)
        return total

    def laid(total, base):
        return total[base * piece : (base + 1) * piece, :]

    early, late = sum_of(early), sum_of(late)
    for q in range(2):
        cut = slice(q * N, (q + 1) * N)
        w_out[:, cut] = laid(early, q)
        w_in[0, :, cut] = laid(early, 2 + q)
        w_in[1, :, cut] = laid(late, q)
    w_in[2, :, 0:N] = laid(late, 2)
    w_in[2, :, N:] = laid(early, 4)
    w_dt[...] = late[3 * piece : 3 * piece + w_dt.shape[0], 0:piece]


VMEM = pl.BlockSpec(memory_space=pltpu.VMEM)
SMEM = pl.BlockSpec(memory_space=pltpu.SMEM)
HBM = pl.BlockSpec(memory_space=pltpu.HBM)


def run(kernel, name, outs, args, scalars=(), fetched=(), scratch=()):
    args = [
        pltpu.with_memory_space_constraint(a, pltpu.HBM) if i in fetched else a
        for i, a in enumerate(args)
    ]

    def place(i):
        if i in fetched:
            return HBM
        return SMEM if i in scalars else VMEM

    def whole(*refs):
        held, sems = refs[len(refs) - len(fetched) - 1 : -1], refs[-1]
        refs = list(refs[: len(refs) - len(fetched) - 1])
        copies = []
        for k, i in enumerate(fetched):
            copies.append(pltpu.make_async_copy(refs[i], held[k], sems.at[k]))
            refs[i] = held[k]
        for copy in copies:
            copy.start()
        for copy in copies:
            copy.wait()
        kernel(*refs)

    holders = []
    if fetched:
        for i in fetched:
            kind = pltpu.SMEM if i in scalars else pltpu.VMEM
            holders.append(kind(args[i].shape, args[i].dtype))
        holders.append(pltpu.SemaphoreType.DMA((len(fetched),)))
    return pl.pallas_call(
        whole if fetched else kernel,
        name=name,
        out_shape=[jax.ShapeDtypeStruct(shape, kind) for shape, kind in outs],
        in_specs=[place(i) for i in range(len(args))],
        out_specs=[VMEM] * len(outs),
        scratch_shapes=list(scratch) + holders,
        compiler_params=pltpu.CompilerParams(vmem_limit_bytes=LIMIT),
        cost_estimate=pl.CostEstimate(flops=10**6, bytes_accessed=2**14, transcendentals=0),
    )(*args)


def shifted(block, axis, distance):
    devices = range(lax.axis_size(axis))
    route = [(i - distance, i) for i in devices if i - distance in devices]
    return lax.ppermute(block, axis, route)


def swapped(block, axis, flip):
    return lax.ppermute(block, axis, [(i, i ^ flip) for i in range(lax.axis_size(axis))])


def body(
    series,
    in_weight,
    step_weight,
    step_bias,
    log_rate,
    conv_weight,
    conv_bias,
    skip_gain,
    norm_gain,
    out_weight,
    cotangent,
):
    length, depth = series.shape
    width = in_weight.shape[2]
    heads = step_weight.shape[1]
    count = lax.axis_size("tm")
    parts = lax.axis_size("head")
    every = width * parts
    assert width == 2 * N and heads == 4
    part = functools.partial
    w = in_weight.transpose(1, 0, 2)
    dtw = step_weight.T
    gain = norm_gain.reshape(1, width)
    hops = count // 2
    piece = depth // count
    position = lax.axis_index("tm").astype(jnp.int32)
    spot = lax.axis_index("head").astype(jnp.int32)
    low, high = (position % 2).reshape(1), (position // 2).reshape(1)
    low_spot, high_spot = (spot % 2).reshape(1), (spot // 2).reshape(1)
    rim = shifted(series[length - RIM :], "tm", 1)
    state_msg = ((width + LOGS, N), BF16)

    def passed(msg, back, during):
        made = []

        def meanwhile(k, block):
            if k < len(during):
                block, extra = lax.optimization_barrier((block, during[k](made)))
                made.append(extra)
            return block

        partner = meanwhile(0, swapped(msg, "tm", 1))
        (msg,) = run(part(pair_kernel, heads, back), "pair", [state_msg], [low, msg, partner], (0,))
        entered = []
        hop = 1
        while hop < hops:
            other = meanwhile(len(made), shifted(msg, "tm", (-2 if back else 2) * hop))
            entered.append(other)
            hop *= 2
            if hop < hops:
                (msg,) = run(part(link_kernel, heads), "link", [state_msg], [other, msg])
        return [partner] + entered[::-1], made

    def halved(keep, send, axis, where, name):
        most, rows, cols = keep.shape
        return run(
            halve_kernel, name, [((rows, cols), F32)] + [((rows, cols), BF16)] * (most - 1),
            [where, keep, swapped(send, axis, 1)], (0,),
        )

    def gathered(blocks, axis):
        return [blocks[0]] + [swapped(block, axis, 2 * k) for k, block in enumerate(blocks) if k]

    gate, pre, scal, w_xbc = run(
        part(project_kernel, heads), "project",
        [
            ((length, width), BF16),
            ((length, 2 * width), BF16),
            ((SCALARS, length), F32),
            ((2, depth, width), BF16),
        ],
        [series, w, dtw, step_bias, log_rate, skip_gain, gain, conv_weight, conv_bias],
        (3, 4, 5), tuple(range(9)),
    )
    x, bc, conv, msg = run(
        part(conv_kernel, heads), "conv",
        [((length, width), BF16), ((length, width), BF16), ((length, 2 * width), F32), state_msg],
        [pre, rim, w_xbc, scal],
        scratch=[pltpu.VMEM((length + 8, 2 * width), F32)],
    )

    def inner(made):
        return run(
            part(inside_kernel, heads), "inside",
            [((length, width), F32), ((length, width), F32), ((length, 2 * width), F32)],
            [x, bc, scal, cotangent, out_weight, conv],
        )

    ahead, ((inside, gg, slope),) = passed(msg, False, [inner])
    y, sin, sums = run(
        part(join_kernel, heads), "join",
        [((length, width), F32), ((width, N), F32), ((8, length), F32)],
        [low, inside, gg, gate, bc, scal] + ahead, (0,),
    )
    flip = 1
    while 2 * flip < parts:
        sums = sums + swapped(sums, "head", flip)
        flip *= 2
    gy, msg, total = run(
        part(grad_y_kernel, heads, every), "grad_y",
        [((length, width), F32), state_msg, ((8, length), F32)],
        [sums, swapped(sums, "head", flip), y, gate, gg, bc, scal],
    )
    early, late = 5 * piece, 3 * piece + LOGS

    def early_part(made):
        return run(
            part(early_kernel, heads, count, every), "early",
            [
                ((length, width), BF16),
                ((length, width), BF16),
                ((length, N), BF16),
                ((length, N), F32),
                ((RIM, N), BF16),
                ((hops, early, N), BF16),
                ((hops, early, N), BF16),
            ],
            [
                low, total, y, gate, gg, gy, x, bc, scal, sin, cotangent, series, rim, slope,
            ],
            (0,),
            scratch=[
                pltpu.VMEM((length + RIM + 8, N), F32),
                pltpu.VMEM((count, early, N), BF16),
            ],
        )

    def beside_part(made):
        normed, grad_gate, gp_c, gb = made[0][0:4]
        return run(
            part(beside_kernel, heads), "beside",
            [
                ((length, depth), BF16),
                ((length, depth), F32),
                ((length, 2 * width), F32),
                ((8, length), F32),
                ((depth, length), BF16),
            ],
            [normed, grad_gate, gp_c, gb, y, gy, x, bc, scal, sin, out_weight, w, series],
        )

    behind, (firsts, (out, sg, held, yb, turned)) = passed(msg, True, [early_part, beside_part])
    edge_c, keep, send = firsts[4:]
    early_parts = halved(keep, send, "tm", high, "halve_early")
    early_parts = gathered(early_parts, "tm")
    back, gp, lead, edge = run(
        part(close_kernel, heads), "close",
        [
            ((length, width + N), F32),
            ((length, width + N), BF16),
            ((RIM, width + N), BF16),
            ((RIM, 2 * width), BF16),
        ],
        [low, x, bc, scal, gy, held, slope, edge_c] + behind, (0,),
        scratch=[pltpu.VMEM((length + RIM + 8, width + N), F32)],
    )
    edge = shifted(edge, "tm", -1)
    gp, early_parts = lax.optimization_barrier((gp, early_parts))
    keep, send, graw = run(
        part(late_kernel, heads, count), "late",
        [((hops, late, N), BF16), ((hops, late, N), BF16), ((2 * heads, length), F32)],
        [low, x, scal, back, gp, lead, yb, held, turned, series, rim], (0,),
        scratch=[pltpu.VMEM((count, late, N), BF16)],
    )
    late_parts = halved(keep, send, "tm", high, "halve_late")
    late_parts = gathered(late_parts, "tm")
    rows = length // parts
    keep, send = run(
        rows_kernel, "rows",
        [((parts // 2, rows, 2 * depth), BF16)] * 2,
        [low_spot, out, sg, gp, graw, edge, w, dtw], (0,),
        scratch=[pltpu.VMEM((length, 2 * depth), BF16)],
    )
    both = gathered(halved(keep, send, "head", high_spot, "halve_rows"), "head")
    layer_out, series_grad = run(
        outputs_kernel, "outputs", [((rows, depth), BF16), ((rows, depth), F32)], both,
    )
    late_parts, layer_out = lax.optimization_barrier((late_parts, layer_out))
    w_in_grad, w_dt_grad, w_out_grad = run(
        part(total_kernel, hops), "total",
        [((3, piece, width), F32), ((heads, piece), F32), ((piece, width), F32)],
        early_parts + late_parts,
    )
    return (layer_out, series_grad, w_in_grad.transpose(1, 0, 2), w_dt_grad.T, w_out_grad)


def solution(mesh):
    in_specs = (
        P("tm", None),
        P(None, None, "head"),
        P(None, "head"),
        P("head"),
        P("head"),
        P(None, None, "head"),
        P(None, "head"),
        P("head"),
        P("head"),
        P(None, "head"),
        P("tm", None),
    )
    out_specs = (
        P(("tm", "head"), None),
        P(("tm", "head"), None),
        P("tm", None, "head"),
        P("tm", "head"),
        P("tm", "head"),
    )
    return jax.shard_map(body, mesh=mesh, in_specs=in_specs, out_specs=out_specs, check_vma=False)
```

```python
import functools

import jax
import jax.numpy as jnp
from jax import lax
from jax.experimental import pallas as pl
from jax.experimental.pallas import tpu as pltpu
from jax.sharding import PartitionSpec as P

N = 128
KW = 4
RIM = 16
LIMIT = 12 * 2**20
SKIP, GAIN, BIAS, TAPS, SCALARS = 16, 17, 18, 20, 32
LOGS = 16
NORM_EPSILON = 1e-05

F32 = jnp.float32
BF16 = jnp.bfloat16
NN = (((1,), (0,)), ((), ()))
NT = (((1,), (1,)), ((), ()))
TN = (((0,), (0,)), ((), ()))


def mm(a, b, dims=NN):
    return lax.dot_general(a.astype(BF16), b.astype(BF16), dims, preferred_element_type=F32)


def mm_exact(a, b, dims=NN):
    return lax.dot_general(
        a, b, dims, precision=lax.Precision.HIGHEST, preferred_element_type=F32
    )


def lanes_of(shape):
    return lax.broadcasted_iota(jnp.int32, shape, len(shape) - 1)


def rows_of(shape):
    return lax.broadcasted_iota(jnp.int32, shape, len(shape) - 2)


def per_row(ref, shape):
    rows = rows_of(shape)
    out = jnp.full(shape, ref[0], F32)
    for h in range(1, shape[0]):
        out = jnp.where(rows == h, ref[h], out)
    return out


def per_lane(ref, heads, width):
    head = lanes_of((1, width)) // (width // heads)
    out = jnp.full((1, width), ref[0], F32)
    for h in range(1, heads):
        out = jnp.where(head == h, ref[h], out)
    return out


def widen(cols, heads, width):
    head = lanes_of((cols.shape[0], width)) // (width // heads)
    out = jnp.broadcast_to(cols[:, 0:1], (cols.shape[0], width))
    for h in range(1, heads):
        out = jnp.where(head == h, cols[:, h : h + 1], out)
    return out


def head_mask(heads, width):
    shape = (8, width)
    return jnp.where(lanes_of(shape) // (width // heads) == rows_of(shape), 1.0, 0.0)


def only_head(x, h, heads):
    width = x.shape[1]
    return jnp.where(lanes_of(x.shape) // (width // heads) == h, x, jnp.zeros_like(x))


def tap(scal, k, slot):
    return scal[TAPS + 2 * k + slot : TAPS + 2 * k + slot + 1, :]


def columns(rows):
    short = -rows.shape[0] % 8
    if short:
        rows = jnp.concatenate([rows, jnp.zeros((short, rows.shape[1]), F32)], axis=0)
    return jnp.transpose(rows)


def sigmoid(v):
    return 1.0 / (1.0 + jnp.exp(-v))


def running_sum(x):
    width = x.shape[1]
    lanes = lanes_of(x.shape)
    hop = 1
    while hop < width:
        x = x + jnp.where(lanes >= hop, pltpu.roll(x, hop, 1), 0.0)
        hop *= 2
    return x


def running_sum_back(x):
    width = x.shape[1]
    lanes = lanes_of(x.shape)
    hop = 1
    while hop < width:
        x = x + jnp.where(lanes < width - hop, pltpu.roll(x, width - hop, 1), 0.0)
        hop *= 2
    return x


def decay_of(cols, rows, h):
    length = cols.shape[0]
    gap = cols[:, h : h + 1] - rows[h : h + 1, :]
    shape = (length, length)
    return jnp.exp(jnp.where(lanes_of(shape) <= rows_of(shape), gap, -1e30))


def logs_of(msg, heads):
    logs = msg[msg.shape[0] - LOGS :].astype(F32)
    return logs[0:heads] + logs[heads : 2 * heads] + logs[2 * heads : 3 * heads]


def spread_rows(logs, heads, size):
    return jnp.concatenate(
        [jnp.broadcast_to(logs[h : h + 1], (size // heads, N)) for h in range(heads)], axis=0
    )


def state_of(msg):
    return msg[0 : msg.shape[0] - LOGS].astype(F32)


def packed(state, logs):
    high = logs.astype(BF16).astype(F32)
    middle = (logs - high).astype(BF16).astype(F32)
    low = logs - high - middle
    logs = jnp.concatenate([high, middle, low, jnp.zeros_like(low)], axis=0)
    return jnp.concatenate([state.astype(BF16), logs.astype(BF16)], axis=0)


def carried(own_turn, partner, others, heads):
    state = jnp.zeros((partner.shape[0] - LOGS, N), F32)
    size = state.shape[0]
    for msg in others:
        state = jnp.exp(spread_rows(logs_of(msg, heads), heads, size)) * state + state_of(msg)
    with_partner = jnp.exp(spread_rows(logs_of(partner, heads), heads, size)) * state
    return jnp.where(own_turn, with_partner + state_of(partner), state)


def project_kernel(
    heads, series, w, dtw, bias, rate, skip, gain, cw, cb, gate, pre, scal, w_xbc,
):
    width = w.shape[2]
    s = series[...]
    gate[...] = mm(s, w[0]).astype(BF16)
    pre[:, 0:width] = mm(s, w[1]).astype(BF16)
    pre[:, width:] = mm(s, w[2]).astype(BF16)
    w_xbc[0] = w[1]
    w_xbc[1] = w[2]
    raw = mm(dtw[...], s, NT)
    shifted = raw + per_row(bias, raw.shape)
    step = jnp.maximum(shifted, 0.0) + jnp.log1p(jnp.exp(-jnp.abs(shifted)))
    rates = jnp.exp(per_row(rate, raw.shape))
    scal[0:heads, :] = running_sum(-step * rates)
    scal[heads : 2 * heads, :] = step
    scal[2 * heads : 3 * heads, :] = sigmoid(shifted)
    scal[3 * heads : SKIP, :] = rates
    scal[SKIP : SKIP + 1, :] = per_lane(skip, heads, width)
    scal[GAIN : GAIN + 1, :] = gain[...]
    scal[BIAS : BIAS + 2, :] = cb[...]
    for k in range(KW):
        scal[TAPS + 2 * k : TAPS + 2 * k + 2, :] = cw[k]
    scal[TAPS + 2 * KW :, :] = jnp.zeros((SCALARS - TAPS - 2 * KW, width), F32)


def conv_kernel(heads, pre, rim, w, scal, x, bc, conv, msg, wide):
    length, both = pre.shape
    width = both // 2
    for s in range(2):
        cut = slice(s * width, (s + 1) * width)
        rims = mm(rim[...], w[s]).astype(BF16).astype(F32)
        wide[0:8, cut] = rims[RIM - 8 :, :]
        wide[8:, cut] = pre[:, cut].astype(F32)
        acc = scal[BIAS + s : BIAS + s + 1, :] + tap(scal, 0, s) * wide[5 : 5 + length, cut]
        for k in range(1, KW):
            acc = acc + tap(scal, k, s) * wide[5 + k : 5 + k + length, cut]
        conv[:, cut] = acc
        act = (acc * sigmoid(acc)).astype(BF16)
        if s == 0:
            x[...] = act
        else:
            bc[...] = act
    running = scal[0:heads, :]
    last = running[:, length - 1 : length]
    remain = jnp.exp(last - running) * scal[heads : 2 * heads, :]
    scaled = x[...].astype(F32) * widen(columns(remain), heads, width)
    state = mm(scaled, bc[:, 0:N], TN)
    msg[...] = packed(state, jnp.broadcast_to(last, (heads, N)))


def pair_kernel(heads, back, low, mine, other, msg):
    mine, other = mine[...], other[...]
    size = mine.shape[0] - LOGS
    mine_first = low[0] == 0
    mine_logs, other_logs = logs_of(mine, heads), logs_of(other, heads)
    crossed = jnp.logical_not(mine_first) if back else mine_first
    mine_scale = jnp.where(crossed, jnp.exp(other_logs), 1.0)
    other_scale = jnp.where(crossed, 1.0, jnp.exp(mine_logs))
    state = spread_rows(mine_scale, heads, size) * state_of(mine)
    state = state + spread_rows(other_scale, heads, size) * state_of(other)
    msg[...] = packed(state, mine_logs + other_logs)


def link_kernel(heads, farther, nearer, msg):
    farther, nearer = farther[...], nearer[...]
    size = nearer.shape[0] - LOGS
    logs = logs_of(nearer, heads)
    state = jnp.exp(spread_rows(logs, heads, size)) * state_of(farther) + state_of(nearer)
    msg[...] = packed(state, logs + logs_of(farther, heads))


def inside_kernel(heads, x, bc, scal, cot, ow, conv, y, gg, slope):
    length, width = x.shape
    xv = x[...].astype(F32)
    rows = scal[0 : 2 * heads, :]
    cols = columns(rows)
    scores = mm(bc[:, N:], bc[:, 0:N], NT)
    acc = scal[SKIP : SKIP + 1, :] * xv
    for h in range(heads):
        mixing = scores * decay_of(cols, rows, h) * rows[heads + h : heads + h + 1, :]
        acc = acc + mm(mixing, only_head(xv, h, heads))
    y[...] = acc
    gg[...] = scal[GAIN : GAIN + 1, :] * mm(cot[...], ow[...])
    v = conv[...]
    sig = sigmoid(v)
    slope[...] = sig * (1.0 + v * (1.0 - sig))


def join_kernel(heads, low, yi, gg, gate, bc, scal, partner, *rest):
    *others, y, sin, sums = rest
    length, width = yi.shape
    start = carried(low[0] == 1, partner[...], [o[...] for o in others], heads)
    sin[...] = start
    grow = widen(columns(jnp.exp(scal[0:heads, :])), heads, width)
    yv = yi[...] + grow * mm(bc[:, N:], start, NT)
    y[...] = yv
    g = gate[...].astype(F32)
    gated = yv * (g * sigmoid(g))
    ones = jnp.ones((8, width), F32)
    square = mm_exact(ones, gated * gated, NT)
    inner = mm_exact(ones, gated * gg[...], NT)
    sums[...] = jnp.where(rows_of(square.shape) == 0, square, inner)


def norm_columns(total, every):
    inv = lax.rsqrt(total[0:1, :] / every + NORM_EPSILON)
    coef = inv * inv * inv * total[1:2, :] / every
    return columns(jnp.concatenate([inv, coef], axis=0))


def grad_y_kernel(heads, every, sums, other, y, gate, gg, bc, scal, gy, msg, total):
    length, width = y.shape
    total[...] = sums[...] + other[...]
    cols = norm_columns(total[...], every)
    g = gate[...].astype(F32)
    act = g * sigmoid(g)
    gated = y[...] * act
    grad = (cols[:, 0:1] * gg[...] - gated * cols[:, 1:2]) * act
    gy[...] = grad
    grow = widen(columns(jnp.exp(scal[0:heads, :])), heads, width)
    last = scal[0:heads, length - 1 : length]
    msg[...] = packed(mm(grad * grow, bc[:, N:], TN), jnp.broadcast_to(last, (heads, N)))


def conv_back(scal, wide, cut, length, slot, slot_cut):
    acc = tap(scal, 0, slot)[:, slot_cut] * wide[KW - 1 : KW - 1 + RIM + length, cut]
    for k in range(1, KW):
        at = KW - 1 - k
        acc = acc + tap(scal, k, slot)[:, slot_cut] * wide[at : at + RIM + length, cut]
    return acc.astype(BF16)


def clear_ends(wide, length):
    zeros = jnp.zeros((RIM, wide.shape[1]), F32)
    wide[0:RIM, :] = zeros
    wide[RIM + length :, :] = zeros[0:8]


def stack_columns(msg, grad, at, base, piece):
    for q in range(grad.shape[1] // N):
        msg[at, (base + q) * piece : (base + q + 1) * piece, :] = grad[
            at * piece : (at + 1) * piece, q * N : (q + 1) * N
        ]


def split_pair(low, every, keep, send):
    for at in range(keep.shape[0]):
        keep[at] = every[2 * at + low]
        send[at] = every[2 * at + 1 - low]


def early_kernel(
    heads, count, every,
    low, total, y, gate, gg, gy, x, bc, scal, sin, cot, series, rim, slope,
    normed, grad_gate, gp, gb, edge, keep, send, wide, stage,
):
    length, width = y.shape
    depth = series.shape[1]
    rows = scal[0 : 2 * heads, :]
    cols = columns(rows)
    xv = x[...]
    gyv = gy[...].astype(BF16)
    b, c = bc[:, 0:N], bc[:, N:]
    group = jnp.zeros((length, length), F32)
    for h in range(heads):
        pairs = mm(only_head(gyv, h, heads), xv, NT)
        group = group + decay_of(cols, rows, h) * pairs * rows[heads + h : heads + h + 1, :]
    gb[...] = mm(group, c, TN)
    grow = widen(columns(jnp.exp(rows[0:heads])), heads, width)
    grad_c = mm(group, b) + mm(gy[...] * grow, sin[...])
    clear_ends(wide, length)
    wide[RIM : RIM + length, :] = grad_c * slope[:, 2 * width - N :]
    grad_pre = conv_back(scal, wide, slice(0, N), length, 1, slice(width - N, width))
    edge[...] = grad_pre[0:RIM]
    gp[...] = grad_pre[RIM:]
    cols = norm_columns(total[...], every)
    g = gate[...].astype(F32)
    sig = sigmoid(g)
    yv = y[...]
    gated = yv * (g * sig)
    normed[...] = (gated * cols[:, 0:1] * scal[GAIN : GAIN + 1, :]).astype(BF16)
    grad_gated = cols[:, 0:1] * gg[...] - gated * cols[:, 1:2]
    grad_gate[...] = (grad_gated * yv * (sig * (1.0 + g * (1.0 - sig)))).astype(BF16)
    w_out = mm(cot[...], normed[...], TN).astype(BF16)
    w_gate = mm(series[...], grad_gate[...], TN).astype(BF16)
    w_c = (mm(series[...], gp[...], TN) + mm(rim[...], edge[...], TN)).astype(BF16)
    piece = depth // count
    for at in range(count):
        stack_columns(stage, w_out, at, 0, piece)
        stack_columns(stage, w_gate, at, 2, piece)
        stack_columns(stage, w_c, at, 4, piece)
    split_pair(low[0], stage, keep, send)


def beside_kernel(
    heads, normed, grad_gate, gp, gb, y, gy, x, bc, scal, sin, ow, w, series,
    out, sg, held, yb, turned,
):
    length, width = y.shape
    rows = scal[0 : 2 * heads, :]
    cols = columns(rows)
    xv = x[...].astype(F32)
    gyv = gy[...]
    scores = mm(bc[:, N:], bc[:, 0:N], NT)
    back = jnp.zeros((length, width), F32)
    for h in range(heads):
        back = back + mm(scores * decay_of(cols, rows, h), only_head(gyv, h, heads), TN)
    held[:, 0:width] = back
    held[:, width : width + N] = gb[...]
    last = rows[0:heads, length - 1 : length]
    remain = jnp.exp(last - rows[0:heads]) * rows[heads:]
    own = mm(xv * widen(columns(remain), heads, width), bc[:, 0:N], TN)
    whole = jnp.exp(spread_rows(jnp.broadcast_to(last, (heads, N)), heads, width))
    held[:, width + N :] = whole * sin[...] + own
    turned[...] = jnp.transpose(series[...])
    skips = scal[SKIP : SKIP + 1, :]
    yb[...] = mm_exact(head_mask(heads, width), gyv * (y[...] - skips * xv), NT)
    out[...] = mm(normed[...], ow[...], NT).astype(BF16)
    sg[...] = mm(grad_gate[...], w[0], NT) + mm(gp[...], w[2, :, width - N :], NT)


def close_kernel(
    heads,
    low, x, bc, scal, gy, held, slope, edge_c, partner, *rest,
):
    *others, back, gp, lead, edge, wide = rest
    length, width = gy.shape
    state = carried(low[0] == 0, partner[...], [o[...] for o in others], heads)
    back[:, width:] = state
    running, step = scal[0:heads, :], scal[heads : 2 * heads, :]
    remain = jnp.exp(running[:, length - 1 : length] - running)
    cols = columns(jnp.concatenate([remain, step, remain * step], axis=0))
    grown = held[:, 0:width] + widen(cols, heads, width) * mm(bc[:, 0:N], state, NT)
    back[:, 0:width] = grown
    grad_x = scal[SKIP : SKIP + 1, :] * gy[...] + widen(cols[:, heads:], heads, width) * grown
    grad_b = held[:, width : width + N] + mm(x[...].astype(F32) * widen(cols[:, 2 * heads :], heads, width), state)
    clear_ends(wide, length)
    wide[RIM : RIM + length, 0:width] = grad_x * slope[:, 0:width]
    wide[RIM : RIM + length, width:] = grad_b * slope[:, width : width + N]
    grad_x = conv_back(scal, wide, slice(0, width), length, 0, slice(0, width))
    grad_b = conv_back(scal, wide, slice(width, width + N), length, 1, slice(0, N))
    for out, cut in ((lead, slice(0, RIM)), (gp, slice(RIM, RIM + length))):
        out[:, 0:width] = grad_x[cut]
        out[:, width:] = grad_b[cut]
    edge[:, 0 : width + N] = lead[...]
    edge[:, width + N :] = edge_c[...]


def late_kernel(
    heads, count,
    low, x, scal, back, gp, lead, yb, held, turned, series, rim,
    keep, send, graw, stage,
):
    length, width = x.shape
    depth = series.shape[1]
    w_xb = (mm(turned[...], gp[...]) + mm(rim[...], lead[...], TN)).astype(BF16)
    rows = scal[0 : 4 * heads, :]
    step = rows[heads : 2 * heads]
    mask = head_mask(heads, width)
    x_back = mm_exact(mask, x[...].astype(F32) * back[:, 0:width], NT)[0:heads]
    ends = jnp.sum(mm_exact(mask, back[:, width:] * held[:, width + N :]), axis=1, keepdims=True)[0:heads]
    grad_log = running_sum_back(yb[0:heads, :] - step * x_back) + ends
    grad_step = x_back - rows[3 * heads :] * grad_log
    grad_raw = grad_step * rows[2 * heads : 3 * heads]
    grad_raw = jnp.concatenate([grad_raw, jnp.zeros_like(grad_raw)], axis=0)
    graw[...] = grad_raw
    dt = mm(grad_raw, series[...])
    piece = depth // count
    blank = jnp.zeros((LOGS, N), F32)
    for at in range(count):
        stack_columns(stage, w_xb, at, 0, piece)
        dt_piece = jnp.concatenate(
            [dt[:, at * piece : (at + 1) * piece], blank[0 : 2 * heads, 0 : N - piece]], axis=1
        )
        dt_piece = jnp.concatenate([dt_piece, blank[0 : LOGS - 2 * heads]], axis=0)
        stage[at, 3 * piece :, :] = dt_piece.astype(BF16)
    split_pair(low[0], stage, keep, send)


def halve_kernel(high, keep, other, own, *parts):
    at = high[0]
    own[...] = keep[at].astype(F32) + other[at].astype(F32)
    for k, part in enumerate(parts):
        at = high[0] ^ (k + 1)
        part[...] = (keep[at].astype(F32) + other[at].astype(F32)).astype(BF16)


def rows_kernel(low, out, sg, gp, graw, edge, w, dtw, keep, send, stage):
    length, depth = sg.shape
    width = w.shape[2]
    heads = dtw.shape[0]
    total = sg[...] + mm(graw[0:heads, :], dtw[...], TN)
    total = total + mm(gp[:, 0:width], w[1], NT) + mm(gp[:, width:], w[2, :, 0:N], NT)
    late = mm(edge[:, 0:width], w[1], NT) + mm(edge[:, width:], w[2], NT)
    stage[:, 0:depth] = out[...]
    stage[:, depth:] = total.astype(BF16)
    stage[length - RIM :, depth:] = (total[length - RIM :, :] + late).astype(BF16)
    piece = keep.shape[1]
    for at in range(keep.shape[0]):
        start = pl.multiple_of((2 * at + low[0]) * piece, piece)
        keep[at] = stage[pl.ds(start, piece), :]
        start = pl.multiple_of((2 * at + 1 - low[0]) * piece, piece)
        send[at] = stage[pl.ds(start, piece), :]


def outputs_kernel(*refs):
    *parts, layer, grad = refs
    depth = layer.shape[1]
    total = parts[0][...].astype(F32)
    for part in parts[1:]:
        total = total + part[...].astype(F32)
    layer[...] = total[:, 0:depth].astype(BF16)
    grad[...] = total[:, depth:]


def total_kernel(hops, *refs):
    early, late = refs[0:hops], refs[hops : 2 * hops]
    w_in, w_dt, w_out = refs[2 * hops :]
    piece = w_out.shape[0]

    def sum_of(parts):
        total = parts[0][...]
        for part in parts[1:]:
            total = total + part[...].astype(F32)
        return total

    def laid(total, base):
        return total[base * piece : (base + 1) * piece, :]

    early, late = sum_of(early), sum_of(late)
    for q in range(2):
        cut = slice(q * N, (q + 1) * N)
        w_out[:, cut] = laid(early, q)
        w_in[0, :, cut] = laid(early, 2 + q)
        w_in[1, :, cut] = laid(late, q)
    w_in[2, :, 0:N] = laid(late, 2)
    w_in[2, :, N:] = laid(early, 4)
    w_dt[...] = late[3 * piece : 3 * piece + w_dt.shape[0], 0:piece]


VMEM = pl.BlockSpec(memory_space=pltpu.VMEM)
SMEM = pl.BlockSpec(memory_space=pltpu.SMEM)
HBM = pl.BlockSpec(memory_space=pltpu.HBM)


def run(given, kernel, name, outs, args, scalars=(), fetched=(), scratch=()):
    kept = [i not in scalars and not any(a is g for g in given) for i, a in enumerate(args)]
    args = [
        pltpu.with_memory_space_constraint(a, pltpu.HBM if i in fetched else pltpu.VMEM)
        if i in fetched or kept[i]
        else a
        for i, a in enumerate(args)
    ]

    def place(i):
        if i in fetched:
            return HBM
        return SMEM if i in scalars else VMEM

    def whole(*refs):
        held, sems = refs[len(refs) - len(fetched) - 1 : -1], refs[-1]
        refs = list(refs[: len(refs) - len(fetched) - 1])
        copies = []
        for k, i in enumerate(fetched):
            copies.append(pltpu.make_async_copy(refs[i], held[k], sems.at[k]))
            refs[i] = held[k]
        for copy in copies:
            copy.start()
        for copy in copies:
            copy.wait()
        kernel(*refs)

    holders = []
    if fetched:
        for i in fetched:
            kind = pltpu.SMEM if i in scalars else pltpu.VMEM
            holders.append(kind(args[i].shape, args[i].dtype))
        holders.append(pltpu.SemaphoreType.DMA((len(fetched),)))
    return pl.pallas_call(
        whole if fetched else kernel,
        name=name,
        out_shape=[jax.ShapeDtypeStruct(shape, kind) for shape, kind in outs],
        in_specs=[place(i) for i in range(len(args))],
        out_specs=[VMEM] * len(outs),
        scratch_shapes=list(scratch) + holders,
        compiler_params=pltpu.CompilerParams(vmem_limit_bytes=LIMIT),
        cost_estimate=pl.CostEstimate(flops=10**6, bytes_accessed=2**14, transcendentals=0),
    )(*args)


def shifted(block, axis, distance):
    devices = range(lax.axis_size(axis))
    route = [(i - distance, i) for i in devices if i - distance in devices]
    return lax.ppermute(block, axis, route)


def swapped(block, axis, flip):
    return lax.ppermute(block, axis, [(i, i ^ flip) for i in range(lax.axis_size(axis))])


def body(
    series,
    in_weight,
    step_weight,
    step_bias,
    log_rate,
    conv_weight,
    conv_bias,
    skip_gain,
    norm_gain,
    out_weight,
    cotangent,
):
    length, depth = series.shape
    width = in_weight.shape[2]
    heads = step_weight.shape[1]
    count = lax.axis_size("tm")
    parts = lax.axis_size("head")
    every = width * parts
    assert width == 2 * N and heads == 4
    part = functools.partial
    w = in_weight.transpose(1, 0, 2)
    dtw = step_weight.T
    gain = norm_gain.reshape(1, width)
    call = part(run, (series, w, dtw, cotangent, out_weight, gain, conv_weight, conv_bias))
    hops = count // 2
    piece = depth // count
    position = lax.axis_index("tm").astype(jnp.int32)
    spot = lax.axis_index("head").astype(jnp.int32)
    low, high = (position % 2).reshape(1), (position // 2).reshape(1)
    low_spot, high_spot = (spot % 2).reshape(1), (spot // 2).reshape(1)
    rim = shifted(series[length - RIM :], "tm", 1)
    state_msg = ((width + LOGS, N), BF16)

    def passed(msg, back, during):
        made = []

        def meanwhile(k, block):
            if k < len(during):
                block, extra = lax.optimization_barrier((block, during[k](made)))
                made.append(extra)
            return block

        partner = meanwhile(0, swapped(msg, "tm", 1))
        (msg,) = call(part(pair_kernel, heads, back), "pair", [state_msg], [low, msg, partner], (0,))
        entered = []
        hop = 1
        while hop < hops:
            other = meanwhile(len(made), shifted(msg, "tm", (-2 if back else 2) * hop))
            entered.append(other)
            hop *= 2
            if hop < hops:
                (msg,) = call(part(link_kernel, heads), "link", [state_msg], [other, msg])
        return [partner] + entered[::-1], made

    def halved(keep, send, axis, where, name):
        most, rows, cols = keep.shape
        return call(
            halve_kernel, name, [((rows, cols), F32)] + [((rows, cols), BF16)] * (most - 1),
            [where, keep, swapped(send, axis, 1)], (0,),
        )

    def gathered(blocks, axis):
        return [blocks[0]] + [swapped(block, axis, 2 * k) for k, block in enumerate(blocks) if k]

    gate, pre, scal, w_xbc = call(
        part(project_kernel, heads), "project",
        [
            ((length, width), BF16),
            ((length, 2 * width), BF16),
            ((SCALARS, length), F32),
            ((2, depth, width), BF16),
        ],
        [series, w, dtw, step_bias, log_rate, skip_gain, gain, conv_weight, conv_bias],
        (3, 4, 5), tuple(range(9)),
    )
    x, bc, conv, msg = call(
        part(conv_kernel, heads), "conv",
        [((length, width), BF16), ((length, width), BF16), ((length, 2 * width), F32), state_msg],
        [pre, rim, w_xbc, scal],
        scratch=[pltpu.VMEM((length + 8, 2 * width), F32)],
    )

    def inner(made):
        return call(
            part(inside_kernel, heads), "inside",
            [((length, width), F32), ((length, width), F32), ((length, 2 * width), F32)],
            [x, bc, scal, cotangent, out_weight, conv],
        )

    ahead, ((inside, gg, slope),) = passed(msg, False, [inner])
    y, sin, sums = call(
        part(join_kernel, heads), "join",
        [((length, width), F32), ((width, N), F32), ((8, length), F32)],
        [low, inside, gg, gate, bc, scal] + ahead, (0,),
    )
    flip = 1
    while 2 * flip < parts:
        sums = sums + swapped(sums, "head", flip)
        flip *= 2
    gy, msg, total = call(
        part(grad_y_kernel, heads, every), "grad_y",
        [((length, width), F32), state_msg, ((8, length), F32)],
        [sums, swapped(sums, "head", flip), y, gate, gg, bc, scal],
    )
    early, late = 5 * piece, 3 * piece + LOGS

    def early_part(made):
        return call(
            part(early_kernel, heads, count, every), "early",
            [
                ((length, width), BF16),
                ((length, width), BF16),
                ((length, N), BF16),
                ((length, N), F32),
                ((RIM, N), BF16),
                ((hops, early, N), BF16),
                ((hops, early, N), BF16),
            ],
            [
                low, total, y, gate, gg, gy, x, bc, scal, sin, cotangent, series, rim, slope,
            ],
            (0,),
            scratch=[
                pltpu.VMEM((length + RIM + 8, N), F32),
                pltpu.VMEM((count, early, N), BF16),
            ],
        )

    def beside_part(made):
        normed, grad_gate, gp_c, gb = made[0][0:4]
        return call(
            part(beside_kernel, heads), "beside",
            [
                ((length, depth), BF16),
                ((length, depth), F32),
                ((length, 2 * width), F32),
                ((8, length), F32),
                ((depth, length), BF16),
            ],
            [normed, grad_gate, gp_c, gb, y, gy, x, bc, scal, sin, out_weight, w, series],
        )

    behind, (firsts, (out, sg, held, yb, turned)) = passed(msg, True, [early_part, beside_part])
    edge_c, keep, send = firsts[4:]
    early_parts = halved(keep, send, "tm", high, "halve_early")
    early_parts = gathered(early_parts, "tm")
    back, gp, lead, edge = call(
        part(close_kernel, heads), "close",
        [
            ((length, width + N), F32),
            ((length, width + N), BF16),
            ((RIM, width + N), BF16),
            ((RIM, 2 * width), BF16),
        ],
        [low, x, bc, scal, gy, held, slope, edge_c] + behind, (0,),
        scratch=[pltpu.VMEM((length + RIM + 8, width + N), F32)],
    )
    edge = shifted(edge, "tm", -1)
    gp, early_parts = lax.optimization_barrier((gp, early_parts))
    keep, send, graw = call(
        part(late_kernel, heads, count), "late",
        [((hops, late, N), BF16), ((hops, late, N), BF16), ((2 * heads, length), F32)],
        [low, x, scal, back, gp, lead, yb, held, turned, series, rim], (0,),
        scratch=[pltpu.VMEM((count, late, N), BF16)],
    )
    late_parts = halved(keep, send, "tm", high, "halve_late")
    late_parts = gathered(late_parts, "tm")
    rows = length // parts
    keep, send = call(
        rows_kernel, "rows",
        [((parts // 2, rows, 2 * depth), BF16)] * 2,
        [low_spot, out, sg, gp, graw, edge, w, dtw], (0,),
        scratch=[pltpu.VMEM((length, 2 * depth), BF16)],
    )
    both = gathered(halved(keep, send, "head", high_spot, "halve_rows"), "head")
    layer_out, series_grad = call(
        outputs_kernel, "outputs", [((rows, depth), BF16), ((rows, depth), F32)], both,
    )
    late_parts, layer_out = lax.optimization_barrier((late_parts, layer_out))
    w_in_grad, w_dt_grad, w_out_grad = call(
        part(total_kernel, hops), "total",
        [((3, piece, width), F32), ((heads, piece), F32), ((piece, width), F32)],
        early_parts + late_parts,
    )
    return (layer_out, series_grad, w_in_grad.transpose(1, 0, 2), w_dt_grad.T, w_out_grad)


def solution(mesh):
    in_specs = (
        P("tm", None),
        P(None, None, "head"),
        P(None, "head"),
        P("head"),
        P("head"),
        P(None, None, "head"),
        P(None, "head"),
        P("head"),
        P("head"),
        P(None, "head"),
        P("tm", None),
    )
    out_specs = (
        P(("tm", "head"), None),
        P(("tm", "head"), None),
        P("tm", None, "head"),
        P("tm", "head"),
        P("tm", "head"),
    )
    return jax.shard_map(body, mesh=mesh, in_specs=in_specs, out_specs=out_specs, check_vma=False)
```

```python
import functools

import jax
import jax.numpy as jnp
from jax import lax
from jax.experimental import pallas as pl
from jax.experimental.pallas import tpu as pltpu
from jax.sharding import PartitionSpec as P

N = 128
KW = 4
RIM = 16
LIMIT = 12 * 2**20
SPARE = 4
SKIP, GAIN, BIAS, TAPS, SCALARS = 16, 17, 18, 20, 32
LOGS = 16
NORM_EPSILON = 1e-05

F32 = jnp.float32
BF16 = jnp.bfloat16
NN = (((1,), (0,)), ((), ()))
NT = (((1,), (1,)), ((), ()))
TN = (((0,), (0,)), ((), ()))


def mm(a, b, dims=NN):
    return lax.dot_general(a.astype(BF16), b.astype(BF16), dims, preferred_element_type=F32)


def mm_exact(a, b, dims=NN):
    return lax.dot_general(
        a, b, dims, precision=lax.Precision.HIGHEST, preferred_element_type=F32
    )


def lanes_of(shape):
    return lax.broadcasted_iota(jnp.int32, shape, len(shape) - 1)


def rows_of(shape):
    return lax.broadcasted_iota(jnp.int32, shape, len(shape) - 2)


def per_row(ref, shape):
    rows = rows_of(shape)
    out = jnp.full(shape, ref[0], F32)
    for h in range(1, shape[0]):
        out = jnp.where(rows == h, ref[h], out)
    return out


def per_lane(ref, heads, width):
    head = lanes_of((1, width)) // (width // heads)
    out = jnp.full((1, width), ref[0], F32)
    for h in range(1, heads):
        out = jnp.where(head == h, ref[h], out)
    return out


def widen(cols, heads, width):
    head = lanes_of((cols.shape[0], width)) // (width // heads)
    out = jnp.broadcast_to(cols[:, 0:1], (cols.shape[0], width))
    for h in range(1, heads):
        out = jnp.where(head == h, cols[:, h : h + 1], out)
    return out


def head_mask(heads, width):
    shape = (8, width)
    return jnp.where(lanes_of(shape) // (width // heads) == rows_of(shape), 1.0, 0.0)


def only_head(x, h, heads):
    width = x.shape[1]
    return jnp.where(lanes_of(x.shape) // (width // heads) == h, x, jnp.zeros_like(x))


def tap(scal, k, slot):
    return scal[TAPS + 2 * k + slot : TAPS + 2 * k + slot + 1, :]


def columns(rows):
    short = -rows.shape[0] % 8
    if short:
        rows = jnp.concatenate([rows, jnp.zeros((short, rows.shape[1]), F32)], axis=0)
    return jnp.transpose(rows)


def sigmoid(v):
    return 1.0 / (1.0 + jnp.exp(-v))


def running_sum(x):
    width = x.shape[1]
    lanes = lanes_of(x.shape)
    hop = 1
    while hop < width:
        x = x + jnp.where(lanes >= hop, pltpu.roll(x, hop, 1), 0.0)
        hop *= 2
    return x


def running_sum_back(x):
    width = x.shape[1]
    lanes = lanes_of(x.shape)
    hop = 1
    while hop < width:
        x = x + jnp.where(lanes < width - hop, pltpu.roll(x, width - hop, 1), 0.0)
        hop *= 2
    return x


def decay_of(cols, rows, h):
    length = cols.shape[0]
    gap = cols[:, h : h + 1] - rows[h : h + 1, :]
    shape = (length, length)
    return jnp.exp(jnp.where(lanes_of(shape) <= rows_of(shape), gap, -1e30))


def logs_of(msg, heads):
    logs = msg[msg.shape[0] - LOGS :].astype(F32)
    return logs[0:heads] + logs[heads : 2 * heads] + logs[2 * heads : 3 * heads]


def spread_rows(logs, heads, size):
    return jnp.concatenate(
        [jnp.broadcast_to(logs[h : h + 1], (size // heads, N)) for h in range(heads)], axis=0
    )


def state_of(msg):
    return msg[0 : msg.shape[0] - LOGS].astype(F32)


def packed(state, logs):
    high = logs.astype(BF16).astype(F32)
    middle = (logs - high).astype(BF16).astype(F32)
    low = logs - high - middle
    logs = jnp.concatenate([high, middle, low, jnp.zeros_like(low)], axis=0)
    return jnp.concatenate([state.astype(BF16), logs.astype(BF16)], axis=0)


def carried(own_turn, partner, far, near, heads):
    state = state_of(far)
    size = state.shape[0]
    if near is not None:
        state = near[0:size, 0:N] + near[0:size, N:] * state
    with_partner = jnp.exp(spread_rows(logs_of(partner, heads), heads, size)) * state
    return jnp.where(own_turn, with_partner + state_of(partner), state)


def project_kernel(
    heads, series, w, dtw, bias, rate, skip, gain, cw, cb, gate, pre, scal, w_xbc,
):
    width = w.shape[2]
    s = series[...]
    gate[...] = mm(s, w[0]).astype(BF16)
    pre[:, 0:width] = mm(s, w[1]).astype(BF16)
    pre[:, width:] = mm(s, w[2]).astype(BF16)
    w_xbc[0] = w[1]
    w_xbc[1] = w[2]
    raw = mm(dtw[...], s, NT)
    shifted = raw + per_row(bias, raw.shape)
    step = jnp.maximum(shifted, 0.0) + jnp.log1p(jnp.exp(-jnp.abs(shifted)))
    rates = jnp.exp(per_row(rate, raw.shape))
    scal[0:heads, :] = running_sum(-step * rates)
    scal[heads : 2 * heads, :] = step
    scal[2 * heads : 3 * heads, :] = sigmoid(shifted)
    scal[3 * heads : SKIP, :] = rates
    scal[SKIP : SKIP + 1, :] = per_lane(skip, heads, width)
    scal[GAIN : GAIN + 1, :] = gain[...]
    scal[BIAS : BIAS + 2, :] = cb[...]
    for k in range(KW):
        scal[TAPS + 2 * k : TAPS + 2 * k + 2, :] = cw[k]
    scal[TAPS + 2 * KW :, :] = jnp.zeros((SCALARS - TAPS - 2 * KW, width), F32)


def conv_kernel(heads, pre, rim, w, scal, x, bc, conv, msg, wide):
    length, both = pre.shape
    width = both // 2
    for s in range(2):
        cut = slice(s * width, (s + 1) * width)
        rims = mm(rim[...], w[s]).astype(BF16).astype(F32)
        wide[0:8, cut] = rims[RIM - 8 :, :]
        wide[8:, cut] = pre[:, cut].astype(F32)
        acc = scal[BIAS + s : BIAS + s + 1, :] + tap(scal, 0, s) * wide[5 : 5 + length, cut]
        for k in range(1, KW):
            acc = acc + tap(scal, k, s) * wide[5 + k : 5 + k + length, cut]
        conv[:, cut] = acc
        act = (acc * sigmoid(acc)).astype(BF16)
        if s == 0:
            x[...] = act
        else:
            bc[...] = act
    running = scal[0:heads, :]
    last = running[:, length - 1 : length]
    remain = jnp.exp(last - running) * scal[heads : 2 * heads, :]
    scaled = x[...].astype(F32) * widen(columns(remain), heads, width)
    state = mm(scaled, bc[:, 0:N], TN)
    msg[...] = packed(state, jnp.broadcast_to(last, (heads, N)))


def pair_kernel(heads, back, low, mine, other, msg):
    mine, other = mine[...], other[...]
    size = mine.shape[0] - LOGS
    mine_first = low[0] == 0
    mine_logs, other_logs = logs_of(mine, heads), logs_of(other, heads)
    crossed = jnp.logical_not(mine_first) if back else mine_first
    mine_scale = jnp.where(crossed, jnp.exp(other_logs), 1.0)
    other_scale = jnp.where(crossed, 1.0, jnp.exp(mine_logs))
    state = spread_rows(mine_scale, heads, size) * state_of(mine)
    state = state + spread_rows(other_scale, heads, size) * state_of(other)
    msg[...] = packed(state, mine_logs + other_logs)


def link_kernel(heads, farther, nearer, *rest):
    *before, msg, near = rest
    farther, nearer = farther[...], nearer[...]
    size = nearer.shape[0] - LOGS
    logs, more = logs_of(nearer, heads), logs_of(farther, heads)
    state = state_of(farther)
    msg[...] = packed(
        jnp.exp(spread_rows(logs, heads, size)) * state + state_of(nearer), logs + more
    )
    scale = jnp.exp(spread_rows(more, heads, size))
    if before:
        state = before[0][0:size, 0:N] + before[0][0:size, N:] * state
        scale = before[0][0:size, N:] * scale
    near[0:size, 0:N] = state
    near[0:size, N:] = scale


def inside_kernel(heads, x, bc, scal, cot, ow, conv, y, gg, slope):
    length, width = x.shape
    xv = x[...].astype(F32)
    rows = scal[0 : 2 * heads, :]
    cols = columns(rows)
    scores = mm(bc[:, N:], bc[:, 0:N], NT)
    acc = scal[SKIP : SKIP + 1, :] * xv
    for h in range(heads):
        mixing = scores * decay_of(cols, rows, h) * rows[heads + h : heads + h + 1, :]
        acc = acc + mm(mixing, only_head(xv, h, heads))
    y[...] = acc
    gg[...] = scal[GAIN : GAIN + 1, :] * mm(cot[...], ow[...])
    v = conv[...]
    sig = sigmoid(v)
    slope[...] = sig * (1.0 + v * (1.0 - sig))


def join_kernel(heads, low, yi, gg, gate, bc, scal, partner, *rest):
    far, *near, y, sin, sums = rest
    length, width = yi.shape
    start = carried(low[0] == 1, partner[...], far[...], near[0] if near else None, heads)
    sin[...] = start
    grow = widen(columns(jnp.exp(scal[0:heads, :])), heads, width)
    yv = yi[...] + grow * mm(bc[:, N:], start, NT)
    y[...] = yv
    g = gate[...].astype(F32)
    gated = yv * (g * sigmoid(g))
    ones = jnp.ones((8, width), F32)
    square = mm_exact(ones, gated * gated, NT)
    inner = mm_exact(ones, gated * gg[...], NT)
    sums[...] = jnp.where(rows_of(square.shape) == 0, square, inner)


def norm_columns(total, every):
    inv = lax.rsqrt(total[0:1, :] / every + NORM_EPSILON)
    coef = inv * inv * inv * total[1:2, :] / every
    return columns(jnp.concatenate([inv, coef], axis=0))


def grad_y_kernel(heads, every, sums, other, y, gate, gg, bc, scal, gy, msg, total):
    length, width = y.shape
    total[...] = sums[...] + other[...]
    cols = norm_columns(total[...], every)
    g = gate[...].astype(F32)
    act = g * sigmoid(g)
    gated = y[...] * act
    grad = (cols[:, 0:1] * gg[...] - gated * cols[:, 1:2]) * act
    gy[...] = grad
    grow = widen(columns(jnp.exp(scal[0:heads, :])), heads, width)
    last = scal[0:heads, length - 1 : length]
    msg[...] = packed(mm(grad * grow, bc[:, N:], TN), jnp.broadcast_to(last, (heads, N)))


def conv_back(scal, wide, cut, length, slot, slot_cut):
    acc = tap(scal, 0, slot)[:, slot_cut] * wide[KW - 1 : KW - 1 + RIM + length, cut]
    for k in range(1, KW):
        at = KW - 1 - k
        acc = acc + tap(scal, k, slot)[:, slot_cut] * wide[at : at + RIM + length, cut]
    return acc.astype(BF16)


def clear_ends(wide, length):
    zeros = jnp.zeros((RIM, wide.shape[1]), F32)
    wide[0:RIM, :] = zeros
    wide[RIM + length :, :] = zeros[0:8]


def stack_columns(msg, grad, at, base, piece):
    for q in range(grad.shape[1] // N):
        msg[at, (base + q) * piece : (base + q + 1) * piece, :] = grad[
            at * piece : (at + 1) * piece, q * N : (q + 1) * N
        ]


def split_pair(low, every, keep, send):
    for at in range(send.shape[0]):
        keep[at] = every[2 * at + low]
        send[at] = every[2 * at + 1 - low]


def early_kernel(
    heads, count, every,
    low, total, y, gate, gg, gy, x, bc, scal, sin, cot, series, rim, slope,
    normed, grad_gate, gp, gb, edge, keep, send, wide, stage,
):
    length, width = y.shape
    depth = series.shape[1]
    rows = scal[0 : 2 * heads, :]
    cols = columns(rows)
    xv = x[...]
    gyv = gy[...].astype(BF16)
    b, c = bc[:, 0:N], bc[:, N:]
    group = jnp.zeros((length, length), F32)
    for h in range(heads):
        pairs = mm(only_head(gyv, h, heads), xv, NT)
        group = group + decay_of(cols, rows, h) * pairs * rows[heads + h : heads + h + 1, :]
    gb[...] = mm(group, c, TN)
    grow = widen(columns(jnp.exp(rows[0:heads])), heads, width)
    grad_c = mm(group, b) + mm(gy[...] * grow, sin[...])
    clear_ends(wide, length)
    wide[RIM : RIM + length, :] = grad_c * slope[:, 2 * width - N :]
    grad_pre = conv_back(scal, wide, slice(0, N), length, 1, slice(width - N, width))
    edge[...] = grad_pre[0:RIM]
    gp[...] = grad_pre[RIM:]
    cols = norm_columns(total[...], every)
    g = gate[...].astype(F32)
    sig = sigmoid(g)
    yv = y[...]
    gated = yv * (g * sig)
    normed[...] = (gated * cols[:, 0:1] * scal[GAIN : GAIN + 1, :]).astype(BF16)
    grad_gated = cols[:, 0:1] * gg[...] - gated * cols[:, 1:2]
    grad_gate[...] = (grad_gated * yv * (sig * (1.0 + g * (1.0 - sig)))).astype(BF16)
    w_out = mm(cot[...], normed[...], TN).astype(BF16)
    w_gate = mm(series[...], grad_gate[...], TN).astype(BF16)
    w_c = (mm(series[...], gp[...], TN) + mm(rim[...], edge[...], TN)).astype(BF16)
    piece = depth // count
    for at in range(count):
        stack_columns(stage, w_out, at, 0, piece)
        stack_columns(stage, w_gate, at, 2, piece)
        stack_columns(stage, w_c, at, 4, piece)
    split_pair(low[0], stage, keep, send)


def beside_kernel(
    heads, normed, grad_gate, gp, gb, y, gy, x, bc, scal, sin, ow, w, series,
    sg, held, yb, turned,
):
    length, width = y.shape
    rows = scal[0 : 2 * heads, :]
    cols = columns(rows)
    xv = x[...].astype(F32)
    gyv = gy[...]
    scores = mm(bc[:, N:], bc[:, 0:N], NT)
    back = jnp.zeros((length, width), F32)
    for h in range(heads):
        back = back + mm(scores * decay_of(cols, rows, h), only_head(gyv, h, heads), TN)
    held[:, 0:width] = back
    held[:, width : width + N] = gb[...]
    last = rows[0:heads, length - 1 : length]
    remain = jnp.exp(last - rows[0:heads]) * rows[heads:]
    own = mm(xv * widen(columns(remain), heads, width), bc[:, 0:N], TN)
    whole = jnp.exp(spread_rows(jnp.broadcast_to(last, (heads, N)), heads, width))
    held[:, width + N :] = whole * sin[...] + own
    turned[0 : series.shape[1], :] = jnp.transpose(series[...])
    skips = scal[SKIP : SKIP + 1, :]
    yb[...] = mm_exact(head_mask(heads, width), gyv * (y[...] - skips * xv), NT)
    depth = series.shape[1]
    sg[:, 0:depth] = mm(normed[...], ow[...], NT)
    sg[:, depth:] = mm(grad_gate[...], w[0], NT) + mm(gp[...], w[2, :, width - N :], NT)


def close_kernel(
    heads,
    low, x, bc, scal, gy, held, slope, edge_c, partner, *rest,
):
    far, *near, back, gp, lead, edge, wide = rest
    length, width = gy.shape
    state = carried(low[0] == 0, partner[...], far[...], near[0] if near else None, heads)
    back[0:width, width:] = state
    running, step = scal[0:heads, :], scal[heads : 2 * heads, :]
    remain = jnp.exp(running[:, length - 1 : length] - running)
    cols = columns(jnp.concatenate([remain, step, remain * step], axis=0))
    grown = held[:, 0:width] + widen(cols, heads, width) * mm(bc[:, 0:N], state, NT)
    back[0:length, 0:width] = grown
    grad_x = scal[SKIP : SKIP + 1, :] * gy[...] + widen(cols[:, heads:], heads, width) * grown
    grad_b = held[:, width : width + N] + mm(x[...].astype(F32) * widen(cols[:, 2 * heads :], heads, width), state)
    clear_ends(wide, length)
    wide[RIM : RIM + length, 0:width] = grad_x * slope[:, 0:width]
    wide[RIM : RIM + length, width:] = grad_b * slope[:, width : width + N]
    grad_x = conv_back(scal, wide, slice(0, width), length, 0, slice(0, width))
    grad_b = conv_back(scal, wide, slice(width, width + N), length, 1, slice(0, N))
    for out, cut in ((lead, slice(0, RIM)), (gp, slice(RIM, RIM + length))):
        out[:, 0:width] = grad_x[cut]
        out[:, width:] = grad_b[cut]
    edge[:, 0 : width + N] = lead[...]
    edge[:, width + N :] = edge_c[...]


def late_kernel(
    heads, count,
    low, x, scal, back, gp, lead, yb, held, turned, series, rim,
    keep, send, graw, stage,
):
    length, width = x.shape
    depth = series.shape[1]
    w_xb = (mm(turned[0:depth, :], gp[...]) + mm(rim[...], lead[...], TN)).astype(BF16)
    rows = scal[0 : 4 * heads, :]
    step = rows[heads : 2 * heads]
    mask = head_mask(heads, width)
    x_back = mm_exact(mask, x[...].astype(F32) * back[0:length, 0:width], NT)[0:heads]
    ends = jnp.sum(mm_exact(mask, back[0:width, width:] * held[:, width + N :]), axis=1, keepdims=True)[0:heads]
    grad_log = running_sum_back(yb[0:heads, :] - step * x_back) + ends
    grad_step = x_back - rows[3 * heads :] * grad_log
    grad_raw = grad_step * rows[2 * heads : 3 * heads]
    grad_raw = jnp.concatenate([grad_raw, jnp.zeros_like(grad_raw)], axis=0)
    graw[...] = grad_raw
    dt = mm(grad_raw, series[...])
    piece = depth // count
    blank = jnp.zeros((LOGS, N), F32)
    for at in range(count):
        stack_columns(stage, w_xb, at, 0, piece)
        dt_piece = jnp.concatenate(
            [dt[:, at * piece : (at + 1) * piece], blank[0 : 2 * heads, 0 : N - piece]], axis=1
        )
        dt_piece = jnp.concatenate([dt_piece, blank[0 : LOGS - 2 * heads]], axis=0)
        stage[at, 3 * piece :, :] = dt_piece.astype(BF16)
    split_pair(low[0], stage, keep, send)


def halve_kernel(high, keep, other, own, *parts):
    at = high[0]
    own[0 : other.shape[1], :] = keep[at].astype(F32) + other[at].astype(F32)
    for k, part in enumerate(parts):
        at = high[0] ^ (k + 1)
        part[...] = (keep[at].astype(F32) + other[at].astype(F32)).astype(BF16)


def rows_kernel(low, sg, gp, graw, edge, w, dtw, keep, send, stage):
    length, depth = sg.shape[0], sg.shape[1] // 2
    width = w.shape[2]
    heads = dtw.shape[0]
    total = sg[:, depth:] + mm(graw[0:heads, :], dtw[...], TN)
    total = total + mm(gp[:, 0:width], w[1], NT) + mm(gp[:, width:], w[2, :, 0:N], NT)
    late = mm(edge[:, 0:width], w[1], NT) + mm(edge[:, width:], w[2], NT)
    stage[:, 0:depth] = sg[:, 0:depth].astype(BF16)
    stage[:, depth:] = total.astype(BF16)
    stage[length - RIM :, depth:] = (total[length - RIM :, :] + late).astype(BF16)
    piece = keep.shape[1]
    for at in range(send.shape[0]):
        start = pl.multiple_of((2 * at + low[0]) * piece, piece)
        keep[at] = stage[pl.ds(start, piece), :]
        start = pl.multiple_of((2 * at + 1 - low[0]) * piece, piece)
        send[at] = stage[pl.ds(start, piece), :]


def sum_of(parts):
    rows = parts[-1].shape[0]
    total = parts[0][0:rows, :]
    for part in parts[1:]:
        total = total + part[...].astype(F32)
    return total


def outputs_kernel(*refs):
    *parts, layer, grad = refs
    depth = layer.shape[1]
    total = sum_of(parts)
    layer[...] = total[:, 0:depth].astype(BF16)
    grad[...] = total[:, depth:]


def early_sum_kernel(*refs):
    *parts, w_out, others = refs
    piece = w_out.shape[0]
    total = sum_of(parts)
    for q in range(2):
        w_out[:, q * N : (q + 1) * N] = total[q * piece : (q + 1) * piece, :]
    others[0 : 3 * piece, :] = total[2 * piece :, :]


def total_kernel(early, *refs):
    *parts, w_in, w_dt = refs
    piece = w_in.shape[1]
    late = sum_of(parts)
    for q in range(2):
        cut = slice(q * N, (q + 1) * N)
        w_in[0, :, cut] = early[q * piece : (q + 1) * piece, :]
        w_in[1, :, cut] = late[q * piece : (q + 1) * piece, :]
    w_in[2, :, 0:N] = late[2 * piece : 3 * piece, :]
    w_in[2, :, N:] = early[2 * piece : 3 * piece, :]
    w_dt[...] = late[3 * piece : 3 * piece + w_dt.shape[0], 0:piece]


VMEM = pl.BlockSpec(memory_space=pltpu.VMEM)
SMEM = pl.BlockSpec(memory_space=pltpu.SMEM)
HBM = pl.BlockSpec(memory_space=pltpu.HBM)


def run(kernel, name, outs, args, scalars=(), fetched=(), scratch=()):
    args = [
        pltpu.with_memory_space_constraint(a, pltpu.HBM) if i in fetched else a
        for i, a in enumerate(args)
    ]

    def place(i):
        if i in fetched:
            return HBM
        return SMEM if i in scalars else VMEM

    def whole(*refs):
        held, sems = refs[len(refs) - len(fetched) - 1 : -1], refs[-1]
        refs = list(refs[: len(refs) - len(fetched) - 1])
        copies = []
        for k, i in enumerate(fetched):
            copies.append(pltpu.make_async_copy(refs[i], held[k], sems.at[k]))
            refs[i] = held[k]
        for copy in copies:
            copy.start()
        for copy in copies:
            copy.wait()
        kernel(*refs)

    holders = []
    if fetched:
        for i in fetched:
            kind = pltpu.SMEM if i in scalars else pltpu.VMEM
            holders.append(kind(args[i].shape, args[i].dtype))
        holders.append(pltpu.SemaphoreType.DMA((len(fetched),)))
    return pl.pallas_call(
        whole if fetched else kernel,
        name=name,
        out_shape=[jax.ShapeDtypeStruct(shape, kind) for shape, kind in outs],
        in_specs=[place(i) for i in range(len(args))],
        out_specs=[VMEM] * len(outs),
        scratch_shapes=list(scratch) + holders,
        compiler_params=pltpu.CompilerParams(vmem_limit_bytes=LIMIT),
        cost_estimate=pl.CostEstimate(flops=10**6, bytes_accessed=2**14, transcendentals=0),
    )(*args)


def shifted(block, axis, distance):
    devices = range(lax.axis_size(axis))
    route = [(i - distance, i) for i in devices if i - distance in devices]
    return lax.ppermute(block, axis, route)


def swapped(block, axis, flip):
    return lax.ppermute(block, axis, [(i, i ^ flip) for i in range(lax.axis_size(axis))])


def body(
    series,
    in_weight,
    step_weight,
    step_bias,
    log_rate,
    conv_weight,
    conv_bias,
    skip_gain,
    norm_gain,
    out_weight,
    cotangent,
):
    length, depth = series.shape
    width = in_weight.shape[2]
    heads = step_weight.shape[1]
    count = lax.axis_size("tm")
    parts = lax.axis_size("head")
    every = width * parts
    assert width == 2 * N and heads == 4
    part = functools.partial
    w = in_weight.transpose(1, 0, 2)
    dtw = step_weight.T
    gain = norm_gain.reshape(1, width)
    hops = count // 2
    piece = depth // count
    position = lax.axis_index("tm").astype(jnp.int32)
    spot = lax.axis_index("head").astype(jnp.int32)
    low, high = (position % 2).reshape(1), (position // 2).reshape(1)
    low_spot, high_spot = (spot % 2).reshape(1), (spot // 2).reshape(1)
    rim = shifted(series[length - RIM :], "tm", 1)
    state_msg = ((width + LOGS, N), BF16)

    def passed(msg, back, during):
        made = []

        def meanwhile(k, block):
            if k < len(during):
                block, extra = lax.optimization_barrier((block, during[k](made)))
                made.append(extra)
            return block

        partner = meanwhile(0, swapped(msg, "tm", 1))
        (msg,) = run(part(pair_kernel, heads, back), "pair", [state_msg], [low, msg, partner], (0,))
        near = []
        hop = 1
        while hop < hops:
            far = meanwhile(len(made), shifted(msg, "tm", (-2 if back else 2) * hop))
            hop *= 2
            if hop < hops:
                msg, *near = run(
                    part(link_kernel, heads), "link",
                    [state_msg, ((SPARE * width, 2 * N), F32)], [far, msg] + near,
                )
        return [partner, far] + near, made

    def halved(keep, send, axis, where, name):
        most, rows, cols = send.shape
        return run(
            halve_kernel, name, [((SPARE * rows, cols), F32)] + [((rows, cols), BF16)] * (most - 1),
            [where, keep, swapped(send, axis, 1)], (0,),
        )

    def gathered(blocks, axis):
        return [blocks[0]] + [swapped(block, axis, 2 * k) for k, block in enumerate(blocks) if k]

    gate, pre, scal, w_xbc = run(
        part(project_kernel, heads), "project",
        [
            ((length, width), BF16),
            ((length, 2 * width), BF16),
            ((SCALARS, length), F32),
            ((2, depth, width), BF16),
        ],
        [series, w, dtw, step_bias, log_rate, skip_gain, gain, conv_weight, conv_bias],
        (3, 4, 5), tuple(range(9)),
    )
    x, bc, conv, msg = run(
        part(conv_kernel, heads), "conv",
        [((length, width), BF16), ((length, width), BF16), ((length, 2 * width), F32), state_msg],
        [pre, rim, w_xbc, scal],
        scratch=[pltpu.VMEM((length + 8, 2 * width), F32)],
    )

    def inner(made):
        return run(
            part(inside_kernel, heads), "inside",
            [((length, width), F32), ((length, width), F32), ((length, 2 * width), F32)],
            [x, bc, scal, cotangent, out_weight, conv],
        )

    ahead, ((inside, gg, slope),) = passed(msg, False, [inner])
    y, sin, sums = run(
        part(join_kernel, heads), "join",
        [((length, width), F32), ((width, N), F32), ((8, length), F32)],
        [low, inside, gg, gate, bc, scal] + ahead, (0,),
    )
    flip = 1
    while 2 * flip < parts:
        sums = sums + swapped(sums, "head", flip)
        flip *= 2
    gy, msg, total = run(
        part(grad_y_kernel, heads, every), "grad_y",
        [((length, width), F32), state_msg, ((8, length), F32)],
        [sums, swapped(sums, "head", flip), y, gate, gg, bc, scal],
    )
    early, late = 5 * piece, 3 * piece + LOGS

    def early_part(made):
        return run(
            part(early_kernel, heads, count, every), "early",
            [
                ((length, width), BF16),
                ((length, width), BF16),
                ((length, N), BF16),
                ((length, N), F32),
                ((RIM, N), BF16),
                ((SPARE * hops, early, N), BF16),
                ((hops, early, N), BF16),
            ],
            [
                low, total, y, gate, gg, gy, x, bc, scal, sin, cotangent, series, rim, slope,
            ],
            (0,),
            scratch=[
                pltpu.VMEM((length + RIM + 8, N), F32),
                pltpu.VMEM((count, early, N), BF16),
            ],
        )

    def beside_part(made):
        normed, grad_gate, gp_c, gb = made[0][0:4]
        return run(
            part(beside_kernel, heads), "beside",
            [
                ((length, 2 * depth), F32),
                ((length, 2 * width), F32),
                ((8, length), F32),
                ((SPARE * depth, length), BF16),
            ],
            [normed, grad_gate, gp_c, gb, y, gy, x, bc, scal, sin, out_weight, w, series],
        )

    behind, (firsts, (sg, held, yb, turned)) = passed(msg, True, [early_part, beside_part])
    edge_c, keep, send = firsts[4:]
    early_parts = halved(keep, send, "tm", high, "halve_early")
    early_parts = gathered(early_parts, "tm")
    back, gp, lead, edge = run(
        part(close_kernel, heads), "close",
        [
            ((SPARE * length, width + N), F32),
            ((length, width + N), BF16),
            ((RIM, width + N), BF16),
            ((RIM, 2 * width), BF16),
        ],
        [low, x, bc, scal, gy, held, slope, edge_c] + behind, (0,),
        scratch=[pltpu.VMEM((length + RIM + 8, width + N), F32)],
    )
    edge = shifted(edge, "tm", -1)
    keep, send, graw = run(
        part(late_kernel, heads, count), "late",
        [((SPARE * hops, late, N), BF16), ((hops, late, N), BF16), ((2 * heads, length), F32)],
        [low, x, scal, back, gp, lead, yb, held, turned, series, rim], (0,),
        scratch=[pltpu.VMEM((count, late, N), BF16)],
    )
    late_parts = halved(keep, send, "tm", high, "halve_late")
    late_parts = gathered(late_parts, "tm")
    rows = length // parts
    edge, early_parts = lax.optimization_barrier((edge, early_parts))
    w_out_grad, early_total = run(
        early_sum_kernel, "early_sum",
        [((piece, width), F32), ((SPARE * 3 * piece, N), F32)], early_parts,
    )
    keep, send = run(
        rows_kernel, "rows",
        [((SPARE * parts // 2, rows, 2 * depth), BF16), ((parts // 2, rows, 2 * depth), BF16)],
        [low_spot, sg, gp, graw, edge, w, dtw], (0,),
        scratch=[pltpu.VMEM((length, 2 * depth), BF16)],
    )
    both = gathered(halved(keep, send, "head", high_spot, "halve_rows"), "head")
    layer_out, series_grad = run(
        outputs_kernel, "outputs", [((rows, depth), BF16), ((rows, depth), F32)], both,
    )
    late_parts, layer_out = lax.optimization_barrier((late_parts, layer_out))
    w_in_grad, w_dt_grad = run(
        total_kernel, "total",
        [((3, piece, width), F32), ((heads, piece), F32)], [early_total] + late_parts,
    )
    return (layer_out, series_grad, w_in_grad.transpose(1, 0, 2), w_dt_grad.T, w_out_grad)


def solution(mesh):
    in_specs = (
        P("tm", None),
        P(None, None, "head"),
        P(None, "head"),
        P("head"),
        P("head"),
        P(None, None, "head"),
        P(None, "head"),
        P("head"),
        P("head"),
        P(None, "head"),
        P("tm", None),
    )
    out_specs = (
        P(("tm", "head"), None),
        P(("tm", "head"), None),
        P("tm", None, "head"),
        P("tm", "head"),
        P("tm", "head"),
    )
    return jax.shard_map(body, mesh=mesh, in_specs=in_specs, out_specs=out_specs, check_vma=False)
```

```python
import functools

import jax
import jax.numpy as jnp
from jax import lax
from jax.experimental import pallas as pl
from jax.experimental.pallas import tpu as pltpu
from jax.sharding import PartitionSpec as P

N = 128
KW = 4
RIM = 16
LIMIT = 6 * 2**20
SKIP, GAIN, BIAS, TAPS, SCALARS = 16, 17, 18, 20, 32
LOGS = 16
NORM_EPSILON = 1e-05

F32 = jnp.float32
BF16 = jnp.bfloat16
NN = (((1,), (0,)), ((), ()))
NT = (((1,), (1,)), ((), ()))
TN = (((0,), (0,)), ((), ()))


def mm(a, b, dims=NN):
    return lax.dot_general(a.astype(BF16), b.astype(BF16), dims, preferred_element_type=F32)


def mm_exact(a, b, dims=NN):
    return lax.dot_general(
        a, b, dims, precision=lax.Precision.HIGHEST, preferred_element_type=F32
    )


def lanes_of(shape):
    return lax.broadcasted_iota(jnp.int32, shape, len(shape) - 1)


def rows_of(shape):
    return lax.broadcasted_iota(jnp.int32, shape, len(shape) - 2)


def per_row(ref, shape):
    rows = rows_of(shape)
    out = jnp.full(shape, ref[0], F32)
    for h in range(1, shape[0]):
        out = jnp.where(rows == h, ref[h], out)
    return out


def per_lane(ref, heads, width):
    head = lanes_of((1, width)) // (width // heads)
    out = jnp.full((1, width), ref[0], F32)
    for h in range(1, heads):
        out = jnp.where(head == h, ref[h], out)
    return out


def widen(cols, heads, width):
    head = lanes_of((cols.shape[0], width)) // (width // heads)
    out = jnp.broadcast_to(cols[:, 0:1], (cols.shape[0], width))
    for h in range(1, heads):
        out = jnp.where(head == h, cols[:, h : h + 1], out)
    return out


def head_mask(heads, width):
    shape = (8, width)
    return jnp.where(lanes_of(shape) // (width // heads) == rows_of(shape), 1.0, 0.0)


def only_head(x, h, heads):
    width = x.shape[1]
    return jnp.where(lanes_of(x.shape) // (width // heads) == h, x, jnp.zeros_like(x))


def tap(scal, k, slot):
    return scal[TAPS + 2 * k + slot : TAPS + 2 * k + slot + 1, :]


def columns(rows):
    short = -rows.shape[0] % 8
    if short:
        rows = jnp.concatenate([rows, jnp.zeros((short, rows.shape[1]), F32)], axis=0)
    return jnp.transpose(rows)


def sigmoid(v):
    return 1.0 / (1.0 + jnp.exp(-v))


def running_sum(x):
    width = x.shape[1]
    lanes = lanes_of(x.shape)
    hop = 1
    while hop < width:
        x = x + jnp.where(lanes >= hop, pltpu.roll(x, hop, 1), 0.0)
        hop *= 2
    return x


def running_sum_back(x):
    width = x.shape[1]
    lanes = lanes_of(x.shape)
    hop = 1
    while hop < width:
        x = x + jnp.where(lanes < width - hop, pltpu.roll(x, width - hop, 1), 0.0)
        hop *= 2
    return x


def decay_of(cols, rows, h):
    length = cols.shape[0]
    gap = cols[:, h : h + 1] - rows[h : h + 1, :]
    shape = (length, length)
    return jnp.exp(jnp.where(lanes_of(shape) <= rows_of(shape), gap, -1e30))


def logs_of(msg, heads):
    logs = msg[msg.shape[0] - LOGS :].astype(F32)
    return logs[0:heads] + logs[heads : 2 * heads] + logs[2 * heads : 3 * heads]


def spread_rows(logs, heads, size):
    return jnp.concatenate(
        [jnp.broadcast_to(logs[h : h + 1], (size // heads, N)) for h in range(heads)], axis=0
    )


def state_of(msg):
    return msg[0 : msg.shape[0] - LOGS].astype(F32)


def packed(state, logs):
    high = logs.astype(BF16).astype(F32)
    middle = (logs - high).astype(BF16).astype(F32)
    low = logs - high - middle
    logs = jnp.concatenate([high, middle, low, jnp.zeros_like(low)], axis=0)
    return jnp.concatenate([state.astype(BF16), logs.astype(BF16)], axis=0)


def carried(own_turn, partner, far, near, heads):
    state = state_of(far)
    size = state.shape[0]
    if near is not None:
        state = near[0:size, 0:N] + near[0:size, N:] * state
    with_partner = jnp.exp(spread_rows(logs_of(partner, heads), heads, size)) * state
    return jnp.where(own_turn, with_partner + state_of(partner), state)


def project_kernel(
    heads, series, w, dtw, bias, rate, skip, gain, cw, cb, gate, pre, scal, w_xbc,
):
    width = w.shape[2]
    s = series[...]
    gate[...] = mm(s, w[0]).astype(BF16)
    pre[:, 0:width] = mm(s, w[1]).astype(BF16)
    pre[:, width:] = mm(s, w[2]).astype(BF16)
    w_xbc[0] = w[1]
    w_xbc[1] = w[2]
    raw = mm(dtw[...], s, NT)
    shifted = raw + per_row(bias, raw.shape)
    step = jnp.maximum(shifted, 0.0) + jnp.log1p(jnp.exp(-jnp.abs(shifted)))
    rates = jnp.exp(per_row(rate, raw.shape))
    scal[0:heads, :] = running_sum(-step * rates)
    scal[heads : 2 * heads, :] = step
    scal[2 * heads : 3 * heads, :] = sigmoid(shifted)
    scal[3 * heads : SKIP, :] = rates
    scal[SKIP : SKIP + 1, :] = per_lane(skip, heads, width)
    scal[GAIN : GAIN + 1, :] = gain[...]
    scal[BIAS : BIAS + 2, :] = cb[...]
    for k in range(KW):
        scal[TAPS + 2 * k : TAPS + 2 * k + 2, :] = cw[k]
    scal[TAPS + 2 * KW :, :] = jnp.zeros((SCALARS - TAPS - 2 * KW, width), F32)


def conv_kernel(heads, pre, rim, w, scal, x, bc, conv, msg, wide):
    length, both = pre.shape
    width = both // 2
    for s in range(2):
        cut = slice(s * width, (s + 1) * width)
        rims = mm(rim[...], w[s]).astype(BF16).astype(F32)
        wide[0:8, cut] = rims[RIM - 8 :, :]
        wide[8:, cut] = pre[:, cut].astype(F32)
        acc = scal[BIAS + s : BIAS + s + 1, :] + tap(scal, 0, s) * wide[5 : 5 + length, cut]
        for k in range(1, KW):
            acc = acc + tap(scal, k, s) * wide[5 + k : 5 + k + length, cut]
        conv[:, cut] = acc
        act = (acc * sigmoid(acc)).astype(BF16)
        if s == 0:
            x[...] = act
        else:
            bc[...] = act
    running = scal[0:heads, :]
    last = running[:, length - 1 : length]
    remain = jnp.exp(last - running) * scal[heads : 2 * heads, :]
    scaled = x[...].astype(F32) * widen(columns(remain), heads, width)
    state = mm(scaled, bc[:, 0:N], TN)
    msg[...] = packed(state, jnp.broadcast_to(last, (heads, N)))


def pair_kernel(heads, back, low, mine, other, msg):
    mine, other = mine[...], other[...]
    size = mine.shape[0] - LOGS
    mine_first = low[0] == 0
    mine_logs, other_logs = logs_of(mine, heads), logs_of(other, heads)
    crossed = jnp.logical_not(mine_first) if back else mine_first
    mine_scale = jnp.where(crossed, jnp.exp(other_logs), 1.0)
    other_scale = jnp.where(crossed, 1.0, jnp.exp(mine_logs))
    state = spread_rows(mine_scale, heads, size) * state_of(mine)
    state = state + spread_rows(other_scale, heads, size) * state_of(other)
    msg[...] = packed(state, mine_logs + other_logs)


def link_kernel(heads, farther, nearer, *rest):
    *before, msg, near = rest
    farther, nearer = farther[...], nearer[...]
    size = nearer.shape[0] - LOGS
    logs, more = logs_of(nearer, heads), logs_of(farther, heads)
    state = state_of(farther)
    msg[...] = packed(
        jnp.exp(spread_rows(logs, heads, size)) * state + state_of(nearer), logs + more
    )
    scale = jnp.exp(spread_rows(more, heads, size))
    if before:
        state = before[0][0:size, 0:N] + before[0][0:size, N:] * state
        scale = before[0][0:size, N:] * scale
    near[0:size, 0:N] = state
    near[0:size, N:] = scale


def inside_kernel(heads, x, bc, scal, cot, ow, conv, y, gg, slope):
    length, width = x.shape
    xv = x[...].astype(F32)
    rows = scal[0 : 2 * heads, :]
    cols = columns(rows)
    scores = mm(bc[:, N:], bc[:, 0:N], NT)
    acc = scal[SKIP : SKIP + 1, :] * xv
    for h in range(heads):
        mixing = scores * decay_of(cols, rows, h) * rows[heads + h : heads + h + 1, :]
        acc = acc + mm(mixing, only_head(xv, h, heads))
    y[...] = acc
    gg[...] = scal[GAIN : GAIN + 1, :] * mm(cot[...], ow[...])
    v = conv[...]
    sig = sigmoid(v)
    slope[...] = (sig * (1.0 + v * (1.0 - sig))).astype(BF16)


def join_kernel(heads, low, yi, gg, gate, bc, scal, partner, *rest):
    far, *near, y, sin, sums = rest
    length, width = yi.shape
    start = carried(low[0] == 1, partner[...], far[...], near[0] if near else None, heads)
    sin[...] = start
    grow = widen(columns(jnp.exp(scal[0:heads, :])), heads, width)
    yv = yi[...] + grow * mm(bc[:, N:], start, NT)
    y[...] = yv
    g = gate[...].astype(F32)
    gated = yv * (g * sigmoid(g))
    ones = jnp.ones((8, width), F32)
    square = mm_exact(ones, gated * gated, NT)
    inner = mm_exact(ones, gated * gg[...], NT)
    sums[...] = jnp.where(rows_of(square.shape) == 0, square, inner)


def norm_columns(total, every):
    inv = lax.rsqrt(total[0:1, :] / every + NORM_EPSILON)
    coef = inv * inv * inv * total[1:2, :] / every
    return columns(jnp.concatenate([inv, coef], axis=0))


def grad_y_kernel(heads, every, sums, other, y, gate, gg, bc, scal, gy, msg, total):
    length, width = y.shape
    total[...] = sums[...] + other[...]
    cols = norm_columns(total[...], every)
    g = gate[...].astype(F32)
    act = g * sigmoid(g)
    gated = y[...] * act
    grad = (cols[:, 0:1] * gg[...] - gated * cols[:, 1:2]) * act
    gy[...] = grad
    grow = widen(columns(jnp.exp(scal[0:heads, :])), heads, width)
    last = scal[0:heads, length - 1 : length]
    msg[...] = packed(mm(grad * grow, bc[:, N:], TN), jnp.broadcast_to(last, (heads, N)))


def conv_back(scal, wide, cut, length, slot, slot_cut):
    acc = tap(scal, 0, slot)[:, slot_cut] * wide[KW - 1 : KW - 1 + RIM + length, cut]
    for k in range(1, KW):
        at = KW - 1 - k
        acc = acc + tap(scal, k, slot)[:, slot_cut] * wide[at : at + RIM + length, cut]
    return acc.astype(BF16)


def clear_ends(wide, length):
    zeros = jnp.zeros((RIM, wide.shape[1]), F32)
    wide[0:RIM, :] = zeros
    wide[RIM + length :, :] = zeros[0:8]


def stack_columns(msg, grad, at, base, piece):
    for q in range(grad.shape[1] // N):
        msg[at, (base + q) * piece : (base + q + 1) * piece, :] = grad[
            at * piece : (at + 1) * piece, q * N : (q + 1) * N
        ]


def split_pair(low, every, keep, send):
    for at in range(send.shape[0]):
        keep[at] = every[2 * at + low]
        send[at] = every[2 * at + 1 - low]


def early_kernel(
    heads, count, every,
    low, total, y, gate, gg, gy, x, bc, scal, sin, cot, series, rim, slope,
    normed, grad_gate, gp, gb, edge, keep, send, wide, stage,
):
    length, width = y.shape
    depth = series.shape[1]
    rows = scal[0 : 2 * heads, :]
    cols = columns(rows)
    xv = x[...]
    gyv = gy[...].astype(BF16)
    b, c = bc[:, 0:N], bc[:, N:]
    group = jnp.zeros((length, length), F32)
    for h in range(heads):
        pairs = mm(only_head(gyv, h, heads), xv, NT)
        group = group + decay_of(cols, rows, h) * pairs * rows[heads + h : heads + h + 1, :]
    gb[...] = mm(group, c, TN)
    grow = widen(columns(jnp.exp(rows[0:heads])), heads, width)
    grad_c = mm(group, b) + mm(gy[...] * grow, sin[...])
    clear_ends(wide, length)
    wide[RIM : RIM + length, :] = grad_c * slope[:, 2 * width - N :].astype(F32)
    grad_pre = conv_back(scal, wide, slice(0, N), length, 1, slice(width - N, width))
    edge[...] = grad_pre[0:RIM]
    gp[...] = grad_pre[RIM:]
    cols = norm_columns(total[...], every)
    g = gate[...].astype(F32)
    sig = sigmoid(g)
    yv = y[...]
    gated = yv * (g * sig)
    normed[...] = (gated * cols[:, 0:1] * scal[GAIN : GAIN + 1, :]).astype(BF16)
    grad_gated = cols[:, 0:1] * gg[...] - gated * cols[:, 1:2]
    grad_gate[...] = (grad_gated * yv * (sig * (1.0 + g * (1.0 - sig)))).astype(BF16)
    w_out = mm(cot[...], normed[...], TN).astype(BF16)
    w_gate = mm(series[...], grad_gate[...], TN).astype(BF16)
    w_c = (mm(series[...], gp[...], TN) + mm(rim[...], edge[...], TN)).astype(BF16)
    piece = depth // count
    for at in range(count):
        stack_columns(stage, w_out, at, 0, piece)
        stack_columns(stage, w_gate, at, 2, piece)
        stack_columns(stage, w_c, at, 4, piece)
    split_pair(low[0], stage, keep, send)


def beside_kernel(
    heads, normed, grad_gate, gp, gb, y, gy, x, bc, scal, sin, ow, w,
    sg, held, yb,
):
    length, width = y.shape
    rows = scal[0 : 2 * heads, :]
    cols = columns(rows)
    xv = x[...].astype(F32)
    gyv = gy[...]
    scores = mm(bc[:, N:], bc[:, 0:N], NT)
    back = jnp.zeros((length, width), F32)
    for h in range(heads):
        back = back + mm(scores * decay_of(cols, rows, h), only_head(gyv, h, heads), TN)
    held[:, 0:width] = back
    held[:, width : width + N] = gb[...]
    last = rows[0:heads, length - 1 : length]
    remain = jnp.exp(last - rows[0:heads]) * rows[heads:]
    own = mm(xv * widen(columns(remain), heads, width), bc[:, 0:N], TN)
    whole = jnp.exp(spread_rows(jnp.broadcast_to(last, (heads, N)), heads, width))
    held[:, width + N :] = whole * sin[...] + own
    skips = scal[SKIP : SKIP + 1, :]
    yb[...] = mm_exact(head_mask(heads, width), gyv * (y[...] - skips * xv), NT)
    depth = ow.shape[0]
    sg[:, 0:depth] = mm(normed[...], ow[...], NT).astype(BF16)
    late = mm(grad_gate[...], w[0], NT) + mm(gp[...], w[2, :, width - N :], NT)
    sg[:, depth:] = late.astype(BF16)


def close_kernel(
    heads,
    low, x, bc, scal, gy, held, slope, edge_c, partner, *rest,
):
    far, *near, back, gp, lead, edge, wide = rest
    length, width = gy.shape
    state = carried(low[0] == 0, partner[...], far[...], near[0] if near else None, heads)
    back[0:width, width:] = state
    running, step = scal[0:heads, :], scal[heads : 2 * heads, :]
    remain = jnp.exp(running[:, length - 1 : length] - running)
    cols = columns(jnp.concatenate([remain, step, remain * step], axis=0))
    grown = held[:, 0:width] + widen(cols, heads, width) * mm(bc[:, 0:N], state, NT)
    back[0:length, 0:width] = grown
    grad_x = scal[SKIP : SKIP + 1, :] * gy[...] + widen(cols[:, heads:], heads, width) * grown
    grad_b = held[:, width : width + N] + mm(x[...].astype(F32) * widen(cols[:, 2 * heads :], heads, width), state)
    clear_ends(wide, length)
    wide[RIM : RIM + length, 0:width] = grad_x * slope[:, 0:width].astype(F32)
    wide[RIM : RIM + length, width:] = grad_b * slope[:, width : width + N].astype(F32)
    grad_x = conv_back(scal, wide, slice(0, width), length, 0, slice(0, width))
    grad_b = conv_back(scal, wide, slice(width, width + N), length, 1, slice(0, N))
    for out, cut in ((lead, slice(0, RIM)), (gp, slice(RIM, RIM + length))):
        out[:, 0:width] = grad_x[cut]
        out[:, width:] = grad_b[cut]
    edge[:, 0 : width + N] = lead[...]
    edge[:, width + N :] = edge_c[...]


def late_kernel(
    heads, count,
    low, x, scal, back, gp, lead, yb, held, series, rim,
    keep, send, graw, stage,
):
    length, width = x.shape
    depth = series.shape[1]
    w_xb = (mm(series[...], gp[...], TN) + mm(rim[...], lead[...], TN)).astype(BF16)
    rows = scal[0 : 4 * heads, :]
    step = rows[heads : 2 * heads]
    mask = head_mask(heads, width)
    x_back = mm_exact(mask, x[...].astype(F32) * back[0:length, 0:width], NT)[0:heads]
    ends = jnp.sum(mm_exact(mask, back[0:width, width:] * held[:, width + N :]), axis=1, keepdims=True)[0:heads]
    grad_log = running_sum_back(yb[0:heads, :] - step * x_back) + ends
    grad_step = x_back - rows[3 * heads :] * grad_log
    grad_raw = grad_step * rows[2 * heads : 3 * heads]
    grad_raw = jnp.concatenate([grad_raw, jnp.zeros_like(grad_raw)], axis=0)
    graw[...] = grad_raw
    dt = mm(grad_raw, series[...])
    piece = depth // count
    blank = jnp.zeros((LOGS, N), F32)
    for at in range(count):
        stack_columns(stage, w_xb, at, 0, piece)
        dt_piece = jnp.concatenate(
            [dt[:, at * piece : (at + 1) * piece], blank[0 : 2 * heads, 0 : N - piece]], axis=1
        )
        dt_piece = jnp.concatenate([dt_piece, blank[0 : LOGS - 2 * heads]], axis=0)
        stage[at, 3 * piece :, :] = dt_piece.astype(BF16)
    split_pair(low[0], stage, keep, send)


def halve_kernel(high, keep, other, own, *parts):
    at = high[0]
    own[0 : other.shape[1], :] = keep[at].astype(F32) + other[at].astype(F32)
    for k, part in enumerate(parts):
        at = high[0] ^ (k + 1)
        part[...] = (keep[at].astype(F32) + other[at].astype(F32)).astype(BF16)


def rows_kernel(low, sg, gp, graw, edge, w, dtw, keep, send, stage):
    length, depth = sg.shape[0], sg.shape[1] // 2
    width = w.shape[2]
    heads = dtw.shape[0]
    total = sg[:, depth:].astype(F32) + mm(graw[0:heads, :], dtw[...], TN)
    total = total + mm(gp[:, 0:width], w[1], NT) + mm(gp[:, width:], w[2, :, 0:N], NT)
    late = mm(edge[:, 0:width], w[1], NT) + mm(edge[:, width:], w[2], NT)
    stage[:, 0:depth] = sg[:, 0:depth]
    stage[:, depth:] = total.astype(BF16)
    stage[length - RIM :, depth:] = (total[length - RIM :, :] + late).astype(BF16)
    piece = keep.shape[1]
    for at in range(send.shape[0]):
        start = pl.multiple_of((2 * at + low[0]) * piece, piece)
        keep[at] = stage[pl.ds(start, piece), :]
        start = pl.multiple_of((2 * at + 1 - low[0]) * piece, piece)
        send[at] = stage[pl.ds(start, piece), :]


def sum_of(parts):
    rows = parts[-1].shape[0]
    total = parts[0][0:rows, :]
    for part in parts[1:]:
        total = total + part[...].astype(F32)
    return total


def outputs_kernel(*refs):
    *parts, layer, grad = refs
    depth = layer.shape[1]
    total = sum_of(parts)
    layer[...] = total[:, 0:depth].astype(BF16)
    grad[...] = total[:, depth:]


def early_sum_kernel(*refs):
    *parts, w_out, others = refs
    piece = w_out.shape[0]
    total = sum_of(parts)
    for q in range(2):
        w_out[:, q * N : (q + 1) * N] = total[q * piece : (q + 1) * piece, :]
    others[0 : 3 * piece, :] = total[2 * piece :, :]


def total_kernel(early, *refs):
    *parts, w_in, w_dt = refs
    piece = w_in.shape[1]
    late = sum_of(parts)
    for q in range(2):
        cut = slice(q * N, (q + 1) * N)
        w_in[0, :, cut] = early[q * piece : (q + 1) * piece, :]
        w_in[1, :, cut] = late[q * piece : (q + 1) * piece, :]
    w_in[2, :, 0:N] = late[2 * piece : 3 * piece, :]
    w_in[2, :, N:] = early[2 * piece : 3 * piece, :]
    w_dt[...] = late[3 * piece : 3 * piece + w_dt.shape[0], 0:piece]


VMEM = pl.BlockSpec(memory_space=pltpu.VMEM)
SMEM = pl.BlockSpec(memory_space=pltpu.SMEM)
HBM = pl.BlockSpec(memory_space=pltpu.HBM)


def run(kernel, name, outs, args, scalars=(), fetched=(), scratch=()):
    args = [
        pltpu.with_memory_space_constraint(a, pltpu.HBM) if i in fetched else a
        for i, a in enumerate(args)
    ]

    def place(i):
        if i in fetched:
            return HBM
        return SMEM if i in scalars else VMEM

    def whole(*refs):
        held, sems = refs[len(refs) - len(fetched) - 1 : -1], refs[-1]
        refs = list(refs[: len(refs) - len(fetched) - 1])
        copies = []
        for k, i in enumerate(fetched):
            copies.append(pltpu.make_async_copy(refs[i], held[k], sems.at[k]))
            refs[i] = held[k]
        for copy in copies:
            copy.start()
        for copy in copies:
            copy.wait()
        kernel(*refs)

    holders = []
    if fetched:
        for i in fetched:
            kind = pltpu.SMEM if i in scalars else pltpu.VMEM
            holders.append(kind(args[i].shape, args[i].dtype))
        holders.append(pltpu.SemaphoreType.DMA((len(fetched),)))
    return pl.pallas_call(
        whole if fetched else kernel,
        name=name,
        out_shape=[jax.ShapeDtypeStruct(shape, kind) for shape, kind in outs],
        in_specs=[place(i) for i in range(len(args))],
        out_specs=[VMEM] * len(outs),
        scratch_shapes=list(scratch) + holders,
        compiler_params=pltpu.CompilerParams(vmem_limit_bytes=LIMIT),
        cost_estimate=pl.CostEstimate(flops=10**6, bytes_accessed=2**14, transcendentals=0),
    )(*args)


def shifted(block, axis, distance):
    devices = range(lax.axis_size(axis))
    route = [(i - distance, i) for i in devices if i - distance in devices]
    return lax.ppermute(block, axis, route)


def swapped(block, axis, flip):
    return lax.ppermute(block, axis, [(i, i ^ flip) for i in range(lax.axis_size(axis))])


def body(
    series,
    in_weight,
    step_weight,
    step_bias,
    log_rate,
    conv_weight,
    conv_bias,
    skip_gain,
    norm_gain,
    out_weight,
    cotangent,
):
    length, depth = series.shape
    width = in_weight.shape[2]
    heads = step_weight.shape[1]
    count = lax.axis_size("tm")
    parts = lax.axis_size("head")
    every = width * parts
    assert width == 2 * N and heads == 4
    part = functools.partial
    w = in_weight.transpose(1, 0, 2)
    dtw = step_weight.T
    gain = norm_gain.reshape(1, width)
    hops = count // 2
    piece = depth // count
    position = lax.axis_index("tm").astype(jnp.int32)
    spot = lax.axis_index("head").astype(jnp.int32)
    low, high = (position % 2).reshape(1), (position // 2).reshape(1)
    low_spot, high_spot = (spot % 2).reshape(1), (spot // 2).reshape(1)
    rim = shifted(series[length - RIM :], "tm", 1)
    state_msg = ((width + LOGS, N), BF16)

    def passed(msg, back, during):
        made = []

        def meanwhile(k, block):
            if k < len(during):
                block, extra = lax.optimization_barrier((block, during[k](made)))
                made.append(extra)
            return block

        partner = meanwhile(0, swapped(msg, "tm", 1))
        (msg,) = run(part(pair_kernel, heads, back), "pair", [state_msg], [low, msg, partner], (0,))
        near = []
        hop = 1
        while hop < hops:
            far = meanwhile(len(made), shifted(msg, "tm", (-2 if back else 2) * hop))
            hop *= 2
            if hop < hops:
                msg, *near = run(
                    part(link_kernel, heads), "link",
                    [state_msg, ((width, 2 * N), F32)], [far, msg] + near,
                )
        return [partner, far] + near, made

    def halved(keep, send, axis, where, name):
        most, rows, cols = send.shape
        return run(
            halve_kernel, name, [((rows, cols), F32)] + [((rows, cols), BF16)] * (most - 1),
            [where, keep, swapped(send, axis, 1)], (0,),
        )

    def gathered(blocks, axis):
        return [blocks[0]] + [swapped(block, axis, 2 * k) for k, block in enumerate(blocks) if k]

    gate, pre, scal, w_xbc = run(
        part(project_kernel, heads), "project",
        [
            ((length, width), BF16),
            ((length, 2 * width), BF16),
            ((SCALARS, length), F32),
            ((2, depth, width), BF16),
        ],
        [series, w, dtw, step_bias, log_rate, skip_gain, gain, conv_weight, conv_bias],
        (3, 4, 5), tuple(range(9)),
    )
    x, bc, conv, msg = run(
        part(conv_kernel, heads), "conv",
        [((length, width), BF16), ((length, width), BF16), ((length, 2 * width), F32), state_msg],
        [pre, rim, w_xbc, scal],
        scratch=[pltpu.VMEM((length + 8, 2 * width), F32)],
    )

    def inner(made):
        return run(
            part(inside_kernel, heads), "inside",
            [((length, width), F32), ((length, width), F32), ((length, 2 * width), BF16)],
            [x, bc, scal, cotangent, out_weight, conv],
        )

    ahead, ((inside, gg, slope),) = passed(msg, False, [inner])
    y, sin, sums = run(
        part(join_kernel, heads), "join",
        [((length, width), F32), ((width, N), F32), ((8, length), F32)],
        [low, inside, gg, gate, bc, scal] + ahead, (0,),
    )
    flip = 1
    while 2 * flip < parts:
        sums = sums + swapped(sums, "head", flip)
        flip *= 2
    gy, msg, total = run(
        part(grad_y_kernel, heads, every), "grad_y",
        [((length, width), F32), state_msg, ((8, length), F32)],
        [sums, swapped(sums, "head", flip), y, gate, gg, bc, scal],
    )
    early, late = 5 * piece, 3 * piece + LOGS

    def early_part(made):
        return run(
            part(early_kernel, heads, count, every), "early",
            [
                ((length, width), BF16),
                ((length, width), BF16),
                ((length, N), BF16),
                ((length, N), F32),
                ((RIM, N), BF16),
                ((hops, early, N), BF16),
                ((hops, early, N), BF16),
            ],
            [
                low, total, y, gate, gg, gy, x, bc, scal, sin, cotangent, series, rim, slope,
            ],
            (0,),
            scratch=[
                pltpu.VMEM((length + RIM + 8, N), F32),
                pltpu.VMEM((count, early, N), BF16),
            ],
        )

    def beside_part(made):
        normed, grad_gate, gp_c, gb = made[0][0:4]
        return run(
            part(beside_kernel, heads), "beside",
            [
                ((length, 2 * depth), BF16),
                ((length, 2 * width), F32),
                ((8, length), F32),
            ],
            [normed, grad_gate, gp_c, gb, y, gy, x, bc, scal, sin, out_weight, w],
        )

    behind, (firsts, (sg, held, yb)) = passed(msg, True, [early_part, beside_part])
    edge_c, keep, send = firsts[4:]
    early_parts = halved(keep, send, "tm", high, "halve_early")
    early_parts = gathered(early_parts, "tm")
    back, gp, lead, edge = run(
        part(close_kernel, heads), "close",
        [
            ((length, width + N), F32),
            ((length, width + N), BF16),
            ((RIM, width + N), BF16),
            ((RIM, 2 * width), BF16),
        ],
        [low, x, bc, scal, gy, held, slope, edge_c] + behind, (0,),
        scratch=[pltpu.VMEM((length + RIM + 8, width + N), F32)],
    )
    edge = shifted(edge, "tm", -1)
    keep, send, graw = run(
        part(late_kernel, heads, count), "late",
        [((hops, late, N), BF16), ((hops, late, N), BF16), ((2 * heads, length), F32)],
        [low, x, scal, back, gp, lead, yb, held, series, rim], (0,),
        scratch=[pltpu.VMEM((count, late, N), BF16)],
    )
    late_parts = halved(keep, send, "tm", high, "halve_late")
    late_parts = gathered(late_parts, "tm")
    rows = length // parts
    edge, early_parts = lax.optimization_barrier((edge, early_parts))
    w_out_grad, early_total = run(
        early_sum_kernel, "early_sum",
        [((piece, width), F32), ((3 * piece, N), F32)], early_parts,
    )
    keep, send = run(
        rows_kernel, "rows",
        [((parts // 2, rows, 2 * depth), BF16), ((parts // 2, rows, 2 * depth), BF16)],
        [low_spot, sg, gp, graw, edge, w, dtw], (0,),
        scratch=[pltpu.VMEM((length, 2 * depth), BF16)],
    )
    both = gathered(halved(keep, send, "head", high_spot, "halve_rows"), "head")
    layer_out, series_grad = run(
        outputs_kernel, "outputs", [((rows, depth), BF16), ((rows, depth), F32)], both,
    )
    late_parts, layer_out = lax.optimization_barrier((late_parts, layer_out))
    w_in_grad, w_dt_grad = run(
        total_kernel, "total",
        [((3, piece, width), F32), ((heads, piece), F32)], [early_total] + late_parts,
    )
    return (layer_out, series_grad, w_in_grad.transpose(1, 0, 2), w_dt_grad.T, w_out_grad)


def solution(mesh):
    in_specs = (
        P("tm", None),
        P(None, None, "head"),
        P(None, "head"),
        P("head"),
        P("head"),
        P(None, None, "head"),
        P(None, "head"),
        P("head"),
        P("head"),
        P(None, "head"),
        P("tm", None),
    )
    out_specs = (
        P(("tm", "head"), None),
        P(("tm", "head"), None),
        P("tm", None, "head"),
        P("tm", "head"),
        P("tm", "head"),
    )
    return jax.shard_map(body, mesh=mesh, in_specs=in_specs, out_specs=out_specs, check_vma=False)
```

```python
import functools

import jax
import jax.numpy as jnp
from jax import lax
from jax.experimental import pallas as pl
from jax.experimental.pallas import tpu as pltpu
from jax.sharding import PartitionSpec as P

N = 128
KW = 4
RIM = 16
LIMIT = 6 * 2**20
SKIP, GAIN, BIAS, TAPS, SCALARS = 16, 17, 18, 20, 32
LOGS = 16
NORM_EPSILON = 1e-05

F32 = jnp.float32
BF16 = jnp.bfloat16
NN = (((1,), (0,)), ((), ()))
NT = (((1,), (1,)), ((), ()))
TN = (((0,), (0,)), ((), ()))


def mm(a, b, dims=NN):
    return lax.dot_general(a.astype(BF16), b.astype(BF16), dims, preferred_element_type=F32)


def mm_exact(a, b, dims=NN):
    return lax.dot_general(
        a, b, dims, precision=lax.Precision.HIGHEST, preferred_element_type=F32
    )


def lanes_of(shape):
    return lax.broadcasted_iota(jnp.int32, shape, len(shape) - 1)


def rows_of(shape):
    return lax.broadcasted_iota(jnp.int32, shape, len(shape) - 2)


def per_row(ref, shape):
    rows = rows_of(shape)
    out = jnp.full(shape, ref[0], F32)
    for h in range(1, shape[0]):
        out = jnp.where(rows == h, ref[h], out)
    return out


def per_lane(ref, heads, width):
    head = lanes_of((1, width)) // (width // heads)
    out = jnp.full((1, width), ref[0], F32)
    for h in range(1, heads):
        out = jnp.where(head == h, ref[h], out)
    return out


def widen(cols, heads, width):
    head = lanes_of((cols.shape[0], width)) // (width // heads)
    out = jnp.broadcast_to(cols[:, 0:1], (cols.shape[0], width))
    for h in range(1, heads):
        out = jnp.where(head == h, cols[:, h : h + 1], out)
    return out


def head_mask(heads, width):
    shape = (8, width)
    return jnp.where(lanes_of(shape) // (width // heads) == rows_of(shape), 1.0, 0.0)


def only_head(x, h, heads):
    width = x.shape[1]
    return jnp.where(lanes_of(x.shape) // (width // heads) == h, x, jnp.zeros_like(x))


def tap(scal, k, slot):
    return scal[TAPS + 2 * k + slot : TAPS + 2 * k + slot + 1, :]


def columns(rows):
    short = -rows.shape[0] % 8
    if short:
        rows = jnp.concatenate([rows, jnp.zeros((short, rows.shape[1]), F32)], axis=0)
    return jnp.transpose(rows)


def sigmoid(v):
    return 1.0 / (1.0 + jnp.exp(-v))


def running_sum(x):
    width = x.shape[1]
    lanes = lanes_of(x.shape)
    hop = 1
    while hop < width:
        x = x + jnp.where(lanes >= hop, pltpu.roll(x, hop, 1), 0.0)
        hop *= 2
    return x


def running_sum_back(x):
    width = x.shape[1]
    lanes = lanes_of(x.shape)
    hop = 1
    while hop < width:
        x = x + jnp.where(lanes < width - hop, pltpu.roll(x, width - hop, 1), 0.0)
        hop *= 2
    return x


def decay_of(cols, rows, h):
    length = cols.shape[0]
    gap = cols[:, h : h + 1] - rows[h : h + 1, :]
    shape = (length, length)
    return jnp.exp(jnp.where(lanes_of(shape) <= rows_of(shape), gap, -1e30))


def logs_of(msg, heads):
    logs = msg[msg.shape[0] - LOGS :].astype(F32)
    return logs[0:heads] + logs[heads : 2 * heads] + logs[2 * heads : 3 * heads]


def spread_rows(logs, heads, size):
    return jnp.concatenate(
        [jnp.broadcast_to(logs[h : h + 1], (size // heads, N)) for h in range(heads)], axis=0
    )


def state_of(msg):
    return msg[0 : msg.shape[0] - LOGS].astype(F32)


def packed(state, logs):
    high = logs.astype(BF16).astype(F32)
    middle = (logs - high).astype(BF16).astype(F32)
    low = logs - high - middle
    logs = jnp.concatenate([high, middle, low, jnp.zeros_like(low)], axis=0)
    return jnp.concatenate([state.astype(BF16), logs.astype(BF16)], axis=0)


def carried(own_turn, partner, far, near, heads):
    state = state_of(far)
    size = state.shape[0]
    if near is not None:
        state = near[0:size, 0:N] + near[0:size, N:] * state
    with_partner = jnp.exp(spread_rows(logs_of(partner, heads), heads, size)) * state
    return jnp.where(own_turn, with_partner + state_of(partner), state)


def project_kernel(
    heads, series, w, dtw, bias, rate, skip, gain, cw, cb, gate, pre, scal, w_xbc,
):
    width = w.shape[2]
    s = series[...]
    gate[...] = mm(s, w[0]).astype(BF16)
    pre[:, 0:width] = mm(s, w[1]).astype(BF16)
    pre[:, width:] = mm(s, w[2]).astype(BF16)
    w_xbc[0] = w[1]
    w_xbc[1] = w[2]
    raw = mm(dtw[...], s, NT)
    shifted = raw + per_row(bias, raw.shape)
    step = jnp.maximum(shifted, 0.0) + jnp.log1p(jnp.exp(-jnp.abs(shifted)))
    rates = jnp.exp(per_row(rate, raw.shape))
    scal[0:heads, :] = running_sum(-step * rates)
    scal[heads : 2 * heads, :] = step
    scal[2 * heads : 3 * heads, :] = sigmoid(shifted)
    scal[3 * heads : SKIP, :] = rates
    scal[SKIP : SKIP + 1, :] = per_lane(skip, heads, width)
    scal[GAIN : GAIN + 1, :] = gain[...]
    scal[BIAS : BIAS + 2, :] = cb[...]
    for k in range(KW):
        scal[TAPS + 2 * k : TAPS + 2 * k + 2, :] = cw[k]
    scal[TAPS + 2 * KW :, :] = jnp.zeros((SCALARS - TAPS - 2 * KW, width), F32)


def conv_kernel(heads, pre, rim, w, scal, x, bc, conv, msg, wide):
    length, both = pre.shape
    width = both // 2
    for s in range(2):
        cut = slice(s * width, (s + 1) * width)
        rims = mm(rim[...], w[s]).astype(BF16).astype(F32)
        wide[0:8, cut] = rims[RIM - 8 :, :]
        wide[8:, cut] = pre[:, cut].astype(F32)
        acc = scal[BIAS + s : BIAS + s + 1, :] + tap(scal, 0, s) * wide[5 : 5 + length, cut]
        for k in range(1, KW):
            acc = acc + tap(scal, k, s) * wide[5 + k : 5 + k + length, cut]
        conv[:, cut] = acc
        act = (acc * sigmoid(acc)).astype(BF16)
        if s == 0:
            x[...] = act
        else:
            bc[...] = act
    running = scal[0:heads, :]
    last = running[:, length - 1 : length]
    remain = jnp.exp(last - running) * scal[heads : 2 * heads, :]
    scaled = x[...].astype(F32) * widen(columns(remain), heads, width)
    state = mm(scaled, bc[:, 0:N], TN)
    msg[...] = packed(state, jnp.broadcast_to(last, (heads, N)))


def pair_kernel(heads, back, low, mine, other, msg):
    mine, other = mine[...], other[...]
    size = mine.shape[0] - LOGS
    mine_first = low[0] == 0
    mine_logs, other_logs = logs_of(mine, heads), logs_of(other, heads)
    crossed = jnp.logical_not(mine_first) if back else mine_first
    mine_scale = jnp.where(crossed, jnp.exp(other_logs), 1.0)
    other_scale = jnp.where(crossed, 1.0, jnp.exp(mine_logs))
    state = spread_rows(mine_scale, heads, size) * state_of(mine)
    state = state + spread_rows(other_scale, heads, size) * state_of(other)
    msg[...] = packed(state, mine_logs + other_logs)


def link_kernel(heads, farther, nearer, *rest):
    *before, msg, near = rest
    farther, nearer = farther[...], nearer[...]
    size = nearer.shape[0] - LOGS
    logs, more = logs_of(nearer, heads), logs_of(farther, heads)
    state = state_of(farther)
    msg[...] = packed(
        jnp.exp(spread_rows(logs, heads, size)) * state + state_of(nearer), logs + more
    )
    scale = jnp.exp(spread_rows(more, heads, size))
    if before:
        state = before[0][0:size, 0:N] + before[0][0:size, N:] * state
        scale = before[0][0:size, N:] * scale
    near[0:size, 0:N] = state
    near[0:size, N:] = scale


def inside_kernel(heads, x, bc, scal, cot, ow, conv, y, gg, slope):
    length, width = x.shape
    xv = x[...].astype(F32)
    rows = scal[0 : 2 * heads, :]
    cols = columns(rows)
    scores = mm(bc[:, N:], bc[:, 0:N], NT)
    acc = scal[SKIP : SKIP + 1, :] * xv
    for h in range(heads):
        mixing = scores * decay_of(cols, rows, h) * rows[heads + h : heads + h + 1, :]
        acc = acc + mm(mixing, only_head(xv, h, heads))
    y[...] = acc
    gg[...] = scal[GAIN : GAIN + 1, :] * mm(cot[...], ow[...])
    v = conv[...]
    sig = sigmoid(v)
    slope[...] = (sig * (1.0 + v * (1.0 - sig))).astype(BF16)


def join_kernel(heads, low, yi, gg, gate, bc, scal, partner, *rest):
    far, *near, y, sin, sums = rest
    length, width = yi.shape
    start = carried(low[0] == 1, partner[...], far[...], near[0] if near else None, heads)
    sin[...] = start
    grow = widen(columns(jnp.exp(scal[0:heads, :])), heads, width)
    yv = yi[...] + grow * mm(bc[:, N:], start, NT)
    y[...] = yv
    g = gate[...].astype(F32)
    gated = yv * (g * sigmoid(g))
    ones = jnp.ones((8, width), F32)
    square = mm_exact(ones, gated * gated, NT)
    inner = mm_exact(ones, gated * gg[...], NT)
    sums[...] = jnp.where(rows_of(square.shape) == 0, square, inner)


def norm_columns(total, every):
    inv = lax.rsqrt(total[0:1, :] / every + NORM_EPSILON)
    coef = inv * inv * inv * total[1:2, :] / every
    return columns(jnp.concatenate([inv, coef], axis=0))


def grad_y_kernel(heads, every, sums, other, y, gate, gg, bc, scal, gy, msg, total):
    length, width = y.shape
    total[...] = sums[...] + other[...]
    cols = norm_columns(total[...], every)
    g = gate[...].astype(F32)
    act = g * sigmoid(g)
    gated = y[...] * act
    grad = (cols[:, 0:1] * gg[...] - gated * cols[:, 1:2]) * act
    gy[...] = grad
    grow = widen(columns(jnp.exp(scal[0:heads, :])), heads, width)
    last = scal[0:heads, length - 1 : length]
    msg[...] = packed(mm(grad * grow, bc[:, N:], TN), jnp.broadcast_to(last, (heads, N)))


def conv_back(scal, wide, cut, length, slot, slot_cut):
    acc = tap(scal, 0, slot)[:, slot_cut] * wide[KW - 1 : KW - 1 + RIM + length, cut]
    for k in range(1, KW):
        at = KW - 1 - k
        acc = acc + tap(scal, k, slot)[:, slot_cut] * wide[at : at + RIM + length, cut]
    return acc.astype(BF16)


def clear_ends(wide, length):
    zeros = jnp.zeros((RIM, wide.shape[1]), F32)
    wide[0:RIM, :] = zeros
    wide[RIM + length :, :] = zeros[0:8]


def stack_columns(msg, grad, at, base, piece):
    for q in range(grad.shape[1] // N):
        msg[at, (base + q) * piece : (base + q + 1) * piece, :] = grad[
            at * piece : (at + 1) * piece, q * N : (q + 1) * N
        ]


def split_pair(low, every, keep, send):
    for at in range(send.shape[0]):
        keep[at] = every[2 * at + low]
        send[at] = every[2 * at + 1 - low]


def early_kernel(
    heads, every,
    low, total, y, gate, gg, gy, x, bc, scal, sin, cot, series, rim, slope,
    normed, grad_gate, gp, gb, edge, sums, wide,
):
    length, width = y.shape
    depth = series.shape[1]
    rows = scal[0 : 2 * heads, :]
    cols = columns(rows)
    xv = x[...]
    gyv = gy[...].astype(BF16)
    b, c = bc[:, 0:N], bc[:, N:]
    group = jnp.zeros((length, length), F32)
    for h in range(heads):
        pairs = mm(only_head(gyv, h, heads), xv, NT)
        group = group + decay_of(cols, rows, h) * pairs * rows[heads + h : heads + h + 1, :]
    gb[...] = mm(group, c, TN)
    grow = widen(columns(jnp.exp(rows[0:heads])), heads, width)
    grad_c = mm(group, b) + mm(gy[...] * grow, sin[...])
    clear_ends(wide, length)
    wide[RIM : RIM + length, :] = grad_c * slope[:, 2 * width - N :].astype(F32)
    grad_pre = conv_back(scal, wide, slice(0, N), length, 1, slice(width - N, width))
    edge[...] = grad_pre[0:RIM]
    gp[...] = grad_pre[RIM:]
    cols = norm_columns(total[...], every)
    g = gate[...].astype(F32)
    sig = sigmoid(g)
    yv = y[...]
    gated = yv * (g * sig)
    normed[...] = (gated * cols[:, 0:1] * scal[GAIN : GAIN + 1, :]).astype(BF16)
    grad_gated = cols[:, 0:1] * gg[...] - gated * cols[:, 1:2]
    grad_gate[...] = (grad_gated * yv * (sig * (1.0 + g * (1.0 - sig)))).astype(BF16)
    sums[:, 0:width] = mm(cot[...], normed[...], TN).astype(BF16)
    sums[:, width : 2 * width] = mm(series[...], grad_gate[...], TN).astype(BF16)
    w_c = mm(series[...], gp[...], TN) + mm(rim[...], edge[...], TN)
    sums[:, 2 * width :] = w_c.astype(BF16)


def beside_kernel(
    heads, normed, grad_gate, gp, gb, y, gy, x, bc, scal, sin, ow, w,
    sg, held, yb,
):
    length, width = y.shape
    rows = scal[0 : 2 * heads, :]
    cols = columns(rows)
    xv = x[...].astype(F32)
    gyv = gy[...]
    scores = mm(bc[:, N:], bc[:, 0:N], NT)
    back = jnp.zeros((length, width), F32)
    for h in range(heads):
        back = back + mm(scores * decay_of(cols, rows, h), only_head(gyv, h, heads), TN)
    held[:, 0:width] = back
    held[:, width : width + N] = gb[...]
    last = rows[0:heads, length - 1 : length]
    remain = jnp.exp(last - rows[0:heads]) * rows[heads:]
    own = mm(xv * widen(columns(remain), heads, width), bc[:, 0:N], TN)
    whole = jnp.exp(spread_rows(jnp.broadcast_to(last, (heads, N)), heads, width))
    held[:, width + N :] = whole * sin[...] + own
    skips = scal[SKIP : SKIP + 1, :]
    yb[...] = mm_exact(head_mask(heads, width), gyv * (y[...] - skips * xv), NT)
    depth = ow.shape[0]
    sg[:, 0:depth] = mm(normed[...], ow[...], NT).astype(BF16)
    late = mm(grad_gate[...], w[0], NT) + mm(gp[...], w[2, :, width - N :], NT)
    sg[:, depth:] = late.astype(BF16)


def close_kernel(
    heads,
    low, x, bc, scal, gy, held, slope, edge_c, partner, *rest,
):
    far, *near, back, gp, lead, edge, wide = rest
    length, width = gy.shape
    state = carried(low[0] == 0, partner[...], far[...], near[0] if near else None, heads)
    back[0:width, width:] = state
    running, step = scal[0:heads, :], scal[heads : 2 * heads, :]
    remain = jnp.exp(running[:, length - 1 : length] - running)
    cols = columns(jnp.concatenate([remain, step, remain * step], axis=0))
    grown = held[:, 0:width] + widen(cols, heads, width) * mm(bc[:, 0:N], state, NT)
    back[0:length, 0:width] = grown
    grad_x = scal[SKIP : SKIP + 1, :] * gy[...] + widen(cols[:, heads:], heads, width) * grown
    grad_b = held[:, width : width + N] + mm(x[...].astype(F32) * widen(cols[:, 2 * heads :], heads, width), state)
    clear_ends(wide, length)
    wide[RIM : RIM + length, 0:width] = grad_x * slope[:, 0:width].astype(F32)
    wide[RIM : RIM + length, width:] = grad_b * slope[:, width : width + N].astype(F32)
    grad_x = conv_back(scal, wide, slice(0, width), length, 0, slice(0, width))
    grad_b = conv_back(scal, wide, slice(width, width + N), length, 1, slice(0, N))
    for out, cut in ((lead, slice(0, RIM)), (gp, slice(RIM, RIM + length))):
        out[:, 0:width] = grad_x[cut]
        out[:, width:] = grad_b[cut]
    edge[:, 0 : width + N] = lead[...]
    edge[:, width + N :] = edge_c[...]


def late_kernel(
    heads, count,
    low, x, scal, back, gp, lead, yb, held, series, rim,
    keep, send, graw, stage,
):
    length, width = x.shape
    depth = series.shape[1]
    w_xb = (mm(series[...], gp[...], TN) + mm(rim[...], lead[...], TN)).astype(BF16)
    rows = scal[0 : 4 * heads, :]
    step = rows[heads : 2 * heads]
    mask = head_mask(heads, width)
    x_back = mm_exact(mask, x[...].astype(F32) * back[0:length, 0:width], NT)[0:heads]
    ends = jnp.sum(mm_exact(mask, back[0:width, width:] * held[:, width + N :]), axis=1, keepdims=True)[0:heads]
    grad_log = running_sum_back(yb[0:heads, :] - step * x_back) + ends
    grad_step = x_back - rows[3 * heads :] * grad_log
    grad_raw = grad_step * rows[2 * heads : 3 * heads]
    grad_raw = jnp.concatenate([grad_raw, jnp.zeros_like(grad_raw)], axis=0)
    graw[...] = grad_raw
    dt = mm(grad_raw, series[...])
    piece = depth // count
    blank = jnp.zeros((LOGS, N), F32)
    for at in range(count):
        stack_columns(stage, w_xb, at, 0, piece)
        dt_piece = jnp.concatenate(
            [dt[:, at * piece : (at + 1) * piece], blank[0 : 2 * heads, 0 : N - piece]], axis=1
        )
        dt_piece = jnp.concatenate([dt_piece, blank[0 : LOGS - 2 * heads]], axis=0)
        stage[at, 3 * piece :, :] = dt_piece.astype(BF16)
    split_pair(low[0], stage, keep, send)


def halve_kernel(high, keep, other, own, *parts):
    at = high[0]
    own[0 : other.shape[1], :] = keep[at].astype(F32) + other[at].astype(F32)
    for k, part in enumerate(parts):
        at = high[0] ^ (k + 1)
        part[...] = (keep[at].astype(F32) + other[at].astype(F32)).astype(BF16)


def rows_kernel(low, sg, gp, graw, edge, w, dtw, keep, send, stage):
    length, depth = sg.shape[0], sg.shape[1] // 2
    width = w.shape[2]
    heads = dtw.shape[0]
    total = sg[:, depth:].astype(F32) + mm(graw[0:heads, :], dtw[...], TN)
    total = total + mm(gp[:, 0:width], w[1], NT) + mm(gp[:, width:], w[2, :, 0:N], NT)
    late = mm(edge[:, 0:width], w[1], NT) + mm(edge[:, width:], w[2], NT)
    stage[:, 0:depth] = sg[:, 0:depth]
    stage[:, depth:] = total.astype(BF16)
    stage[length - RIM :, depth:] = (total[length - RIM :, :] + late).astype(BF16)
    piece = keep.shape[1]
    for at in range(send.shape[0]):
        start = pl.multiple_of((2 * at + low[0]) * piece, piece)
        keep[at] = stage[pl.ds(start, piece), :]
        start = pl.multiple_of((2 * at + 1 - low[0]) * piece, piece)
        send[at] = stage[pl.ds(start, piece), :]


def sum_of(parts):
    rows = parts[-1].shape[0]
    total = parts[0][0:rows, :]
    for part in parts[1:]:
        total = total + part[...].astype(F32)
    return total


def outputs_kernel(*refs):
    *parts, layer, grad = refs
    depth = layer.shape[1]
    total = sum_of(parts)
    layer[...] = total[:, 0:depth].astype(BF16)
    grad[...] = total[:, depth:]


def total_kernel(early, *refs):
    *parts, w_in, w_dt, w_out = refs
    piece, width = w_out.shape
    w_out[...] = early[:, 0:width].astype(F32)
    w_in[0] = early[:, width : 2 * width].astype(F32)
    w_in[2, :, N:] = early[:, 2 * width :].astype(F32)
    late = sum_of(parts)
    for q in range(2):
        w_in[1, :, q * N : (q + 1) * N] = late[q * piece : (q + 1) * piece, :]
    w_in[2, :, 0:N] = late[2 * piece : 3 * piece, :]
    w_dt[...] = late[3 * piece : 3 * piece + w_dt.shape[0], 0:piece]


VMEM = pl.BlockSpec(memory_space=pltpu.VMEM)
SMEM = pl.BlockSpec(memory_space=pltpu.SMEM)
HBM = pl.BlockSpec(memory_space=pltpu.HBM)


def run(kernel, name, outs, args, scalars=(), fetched=(), scratch=()):
    args = [
        pltpu.with_memory_space_constraint(a, pltpu.HBM) if i in fetched else a
        for i, a in enumerate(args)
    ]

    def place(i):
        if i in fetched:
            return HBM
        return SMEM if i in scalars else VMEM

    def whole(*refs):
        held, sems = refs[len(refs) - len(fetched) - 1 : -1], refs[-1]
        refs = list(refs[: len(refs) - len(fetched) - 1])
        copies = []
        for k, i in enumerate(fetched):
            copies.append(pltpu.make_async_copy(refs[i], held[k], sems.at[k]))
            refs[i] = held[k]
        for copy in copies:
            copy.start()
        for copy in copies:
            copy.wait()
        kernel(*refs)

    holders = []
    if fetched:
        for i in fetched:
            kind = pltpu.SMEM if i in scalars else pltpu.VMEM
            holders.append(kind(args[i].shape, args[i].dtype))
        holders.append(pltpu.SemaphoreType.DMA((len(fetched),)))
    return pl.pallas_call(
        whole if fetched else kernel,
        name=name,
        out_shape=[jax.ShapeDtypeStruct(shape, kind) for shape, kind in outs],
        in_specs=[place(i) for i in range(len(args))],
        out_specs=[VMEM] * len(outs),
        scratch_shapes=list(scratch) + holders,
        compiler_params=pltpu.CompilerParams(vmem_limit_bytes=LIMIT),
        cost_estimate=pl.CostEstimate(flops=10**6, bytes_accessed=2**14, transcendentals=0),
    )(*args)


def shifted(block, axis, distance):
    devices = range(lax.axis_size(axis))
    route = [(i - distance, i) for i in devices if i - distance in devices]
    return lax.ppermute(block, axis, route)


def swapped(block, axis, flip):
    return lax.ppermute(block, axis, [(i, i ^ flip) for i in range(lax.axis_size(axis))])


def body(
    series,
    in_weight,
    step_weight,
    step_bias,
    log_rate,
    conv_weight,
    conv_bias,
    skip_gain,
    norm_gain,
    out_weight,
    cotangent,
):
    length, depth = series.shape
    width = in_weight.shape[2]
    heads = step_weight.shape[1]
    count = lax.axis_size("tm")
    parts = lax.axis_size("head")
    every = width * parts
    assert width == 2 * N and heads == 4
    part = functools.partial
    w = in_weight.transpose(1, 0, 2)
    dtw = step_weight.T
    gain = norm_gain.reshape(1, width)
    hops = count // 2
    piece = depth // count
    position = lax.axis_index("tm").astype(jnp.int32)
    spot = lax.axis_index("head").astype(jnp.int32)
    low, high = (position % 2).reshape(1), (position // 2).reshape(1)
    low_spot, high_spot = (spot % 2).reshape(1), (spot // 2).reshape(1)
    rim = shifted(series[length - RIM :], "tm", 1)
    state_msg = ((width + LOGS, N), BF16)

    def passed(msg, back, during):
        made = []

        def meanwhile(k, block):
            if k < len(during):
                block, extra = lax.optimization_barrier((block, during[k](made)))
                made.append(extra)
            return block

        partner = meanwhile(0, swapped(msg, "tm", 1))
        (msg,) = run(part(pair_kernel, heads, back), "pair", [state_msg], [low, msg, partner], (0,))
        near = []
        hop = 1
        while hop < hops:
            far = meanwhile(len(made), shifted(msg, "tm", (-2 if back else 2) * hop))
            hop *= 2
            if hop < hops:
                msg, *near = run(
                    part(link_kernel, heads), "link",
                    [state_msg, ((width, 2 * N), F32)], [far, msg] + near,
                )
        return [partner, far] + near, made

    def halved(keep, send, axis, where, name):
        most, rows, cols = send.shape
        return run(
            halve_kernel, name, [((rows, cols), F32)] + [((rows, cols), BF16)] * (most - 1),
            [where, keep, swapped(send, axis, 1)], (0,),
        )

    def gathered(blocks, axis):
        return [blocks[0]] + [swapped(block, axis, 2 * k) for k, block in enumerate(blocks) if k]

    gate, pre, scal, w_xbc = run(
        part(project_kernel, heads), "project",
        [
            ((length, width), BF16),
            ((length, 2 * width), BF16),
            ((SCALARS, length), F32),
            ((2, depth, width), BF16),
        ],
        [series, w, dtw, step_bias, log_rate, skip_gain, gain, conv_weight, conv_bias],
        (3, 4, 5), tuple(range(9)),
    )
    x, bc, conv, msg = run(
        part(conv_kernel, heads), "conv",
        [((length, width), BF16), ((length, width), BF16), ((length, 2 * width), F32), state_msg],
        [pre, rim, w_xbc, scal],
        scratch=[pltpu.VMEM((length + 8, 2 * width), F32)],
    )

    def inner(made):
        return run(
            part(inside_kernel, heads), "inside",
            [((length, width), F32), ((length, width), F32), ((length, 2 * width), BF16)],
            [x, bc, scal, cotangent, out_weight, conv],
        )

    ahead, ((inside, gg, slope),) = passed(msg, False, [inner])
    y, sin, sums = run(
        part(join_kernel, heads), "join",
        [((length, width), F32), ((width, N), F32), ((8, length), F32)],
        [low, inside, gg, gate, bc, scal] + ahead, (0,),
    )
    flip = 1
    while 2 * flip < parts:
        sums = sums + swapped(sums, "head", flip)
        flip *= 2
    gy, msg, total = run(
        part(grad_y_kernel, heads, every), "grad_y",
        [((length, width), F32), state_msg, ((8, length), F32)],
        [sums, swapped(sums, "head", flip), y, gate, gg, bc, scal],
    )
    late = 3 * piece + LOGS

    def early_part(made):
        return run(
            part(early_kernel, heads, every), "early",
            [
                ((length, width), BF16),
                ((length, width), BF16),
                ((length, N), BF16),
                ((length, N), F32),
                ((RIM, N), BF16),
                ((depth, 2 * width + N), BF16),
            ],
            [
                low, total, y, gate, gg, gy, x, bc, scal, sin, cotangent, series, rim, slope,
            ],
            (0,),
            scratch=[pltpu.VMEM((length + RIM + 8, N), F32)],
        )

    def beside_part(made):
        normed, grad_gate, gp_c, gb = made[0][0:4]
        return run(
            part(beside_kernel, heads), "beside",
            [
                ((length, 2 * depth), BF16),
                ((length, 2 * width), F32),
                ((8, length), F32),
            ],
            [normed, grad_gate, gp_c, gb, y, gy, x, bc, scal, sin, out_weight, w],
        )

    behind, (firsts, (sg, held, yb)) = passed(msg, True, [early_part, beside_part])
    edge_c, early = firsts[4:]
    early = lax.psum_scatter(early, "tm", scatter_dimension=0, tiled=True)
    back, gp, lead, edge = run(
        part(close_kernel, heads), "close",
        [
            ((length, width + N), F32),
            ((length, width + N), BF16),
            ((RIM, width + N), BF16),
            ((RIM, 2 * width), BF16),
        ],
        [low, x, bc, scal, gy, held, slope, edge_c] + behind, (0,),
        scratch=[pltpu.VMEM((length + RIM + 8, width + N), F32)],
    )
    edge = shifted(edge, "tm", -1)
    keep, send, graw = run(
        part(late_kernel, heads, count), "late",
        [((hops, late, N), BF16), ((hops, late, N), BF16), ((2 * heads, length), F32)],
        [low, x, scal, back, gp, lead, yb, held, series, rim], (0,),
        scratch=[pltpu.VMEM((count, late, N), BF16)],
    )
    late_parts = halved(keep, send, "tm", high, "halve_late")
    late_parts = gathered(late_parts, "tm")
    rows = length // parts
    keep, send = run(
        rows_kernel, "rows",
        [((parts // 2, rows, 2 * depth), BF16), ((parts // 2, rows, 2 * depth), BF16)],
        [low_spot, sg, gp, graw, edge, w, dtw], (0,),
        scratch=[pltpu.VMEM((length, 2 * depth), BF16)],
    )
    both = gathered(halved(keep, send, "head", high_spot, "halve_rows"), "head")
    layer_out, series_grad = run(
        outputs_kernel, "outputs", [((rows, depth), BF16), ((rows, depth), F32)], both,
    )
    late_parts, layer_out = lax.optimization_barrier((late_parts, layer_out))
    w_in_grad, w_dt_grad, w_out_grad = run(
        total_kernel, "total",
        [((3, piece, width), F32), ((heads, piece), F32), ((piece, width), F32)],
        [early] + late_parts,
    )
    return (layer_out, series_grad, w_in_grad.transpose(1, 0, 2), w_dt_grad.T, w_out_grad)


def solution(mesh):
    in_specs = (
        P("tm", None),
        P(None, None, "head"),
        P(None, "head"),
        P("head"),
        P("head"),
        P(None, None, "head"),
        P(None, "head"),
        P("head"),
        P("head"),
        P(None, "head"),
        P("tm", None),
    )
    out_specs = (
        P(("tm", "head"), None),
        P(("tm", "head"), None),
        P("tm", None, "head"),
        P("tm", "head"),
        P("tm", "head"),
    )
    return jax.shard_map(body, mesh=mesh, in_specs=in_specs, out_specs=out_specs, check_vma=False)
```

```python
import functools

import jax
import jax.numpy as jnp
from jax import lax
from jax.experimental import pallas as pl
from jax.experimental.pallas import tpu as pltpu
from jax.sharding import PartitionSpec as P

N = 128
KW = 4
RIM = 16
LIMIT = 6 * 2**20
SKIP, GAIN, BIAS, TAPS, SCALARS = 16, 17, 18, 20, 32
LOGS = 16
NORM_EPSILON = 1e-05

F32 = jnp.float32
BF16 = jnp.bfloat16
NN = (((1,), (0,)), ((), ()))
NT = (((1,), (1,)), ((), ()))
TN = (((0,), (0,)), ((), ()))


def mm(a, b, dims=NN):
    return lax.dot_general(a.astype(BF16), b.astype(BF16), dims, preferred_element_type=F32)


def mm_exact(a, b, dims=NN):
    return lax.dot_general(
        a, b, dims, precision=lax.Precision.HIGHEST, preferred_element_type=F32
    )


def lanes_of(shape):
    return lax.broadcasted_iota(jnp.int32, shape, len(shape) - 1)


def rows_of(shape):
    return lax.broadcasted_iota(jnp.int32, shape, len(shape) - 2)


def per_row(ref, shape):
    rows = rows_of(shape)
    out = jnp.full(shape, ref[0], F32)
    for h in range(1, shape[0]):
        out = jnp.where(rows == h, ref[h], out)
    return out


def per_lane(ref, heads, width):
    head = lanes_of((1, width)) // (width // heads)
    out = jnp.full((1, width), ref[0], F32)
    for h in range(1, heads):
        out = jnp.where(head == h, ref[h], out)
    return out


def widen(cols, heads, width):
    head = lanes_of((cols.shape[0], width)) // (width // heads)
    out = jnp.broadcast_to(cols[:, 0:1], (cols.shape[0], width))
    for h in range(1, heads):
        out = jnp.where(head == h, cols[:, h : h + 1], out)
    return out


def head_mask(heads, width):
    shape = (8, width)
    return jnp.where(lanes_of(shape) // (width // heads) == rows_of(shape), 1.0, 0.0)


def only_head(x, h, heads):
    width = x.shape[1]
    return jnp.where(lanes_of(x.shape) // (width // heads) == h, x, jnp.zeros_like(x))


def tap(scal, k, slot):
    return scal[TAPS + 2 * k + slot : TAPS + 2 * k + slot + 1, :]


def columns(rows):
    short = -rows.shape[0] % 8
    if short:
        rows = jnp.concatenate([rows, jnp.zeros((short, rows.shape[1]), F32)], axis=0)
    return jnp.transpose(rows)


def sigmoid(v):
    return 1.0 / (1.0 + jnp.exp(-v))


def running_sum(x):
    width = x.shape[1]
    lanes = lanes_of(x.shape)
    hop = 1
    while hop < width:
        x = x + jnp.where(lanes >= hop, pltpu.roll(x, hop, 1), 0.0)
        hop *= 2
    return x


def running_sum_back(x):
    width = x.shape[1]
    lanes = lanes_of(x.shape)
    hop = 1
    while hop < width:
        x = x + jnp.where(lanes < width - hop, pltpu.roll(x, width - hop, 1), 0.0)
        hop *= 2
    return x


def decay_of(cols, rows, h):
    length = cols.shape[0]
    gap = cols[:, h : h + 1] - rows[h : h + 1, :]
    shape = (length, length)
    return jnp.exp(jnp.where(lanes_of(shape) <= rows_of(shape), gap, -1e30))


def logs_of(msg, heads):
    logs = msg[msg.shape[0] - LOGS :].astype(F32)
    return logs[0:heads] + logs[heads : 2 * heads] + logs[2 * heads : 3 * heads]


def spread_rows(logs, heads, size):
    return jnp.concatenate(
        [jnp.broadcast_to(logs[h : h + 1], (size // heads, N)) for h in range(heads)], axis=0
    )


def state_of(msg):
    return msg[0 : msg.shape[0] - LOGS].astype(F32)


def packed(state, logs):
    high = logs.astype(BF16).astype(F32)
    middle = (logs - high).astype(BF16).astype(F32)
    low = logs - high - middle
    logs = jnp.concatenate([high, middle, low, jnp.zeros_like(low)], axis=0)
    return jnp.concatenate([state.astype(BF16), logs.astype(BF16)], axis=0)


def carried(own_turn, partner, far, near, heads):
    state = state_of(far)
    size = state.shape[0]
    if near is not None:
        state = near[0:size, 0:N] + near[0:size, N:] * state
    with_partner = jnp.exp(spread_rows(logs_of(partner, heads), heads, size)) * state
    return jnp.where(own_turn, with_partner + state_of(partner), state)


def project_kernel(
    heads, series, w, dtw, bias, rate, skip, gain, cw, cb, gate, pre, scal, w_xbc,
):
    width = w.shape[2]
    s = series[...]
    gate[...] = mm(s, w[0]).astype(BF16)
    pre[:, 0:width] = mm(s, w[1]).astype(BF16)
    pre[:, width:] = mm(s, w[2]).astype(BF16)
    w_xbc[0] = w[1]
    w_xbc[1] = w[2]
    raw = mm(dtw[...], s, NT)
    shifted = raw + per_row(bias, raw.shape)
    step = jnp.maximum(shifted, 0.0) + jnp.log1p(jnp.exp(-jnp.abs(shifted)))
    rates = jnp.exp(per_row(rate, raw.shape))
    scal[0:heads, :] = running_sum(-step * rates)
    scal[heads : 2 * heads, :] = step
    scal[2 * heads : 3 * heads, :] = sigmoid(shifted)
    scal[3 * heads : SKIP, :] = rates
    scal[SKIP : SKIP + 1, :] = per_lane(skip, heads, width)
    scal[GAIN : GAIN + 1, :] = gain[...]
    scal[BIAS : BIAS + 2, :] = cb[...]
    for k in range(KW):
        scal[TAPS + 2 * k : TAPS + 2 * k + 2, :] = cw[k]
    scal[TAPS + 2 * KW :, :] = jnp.zeros((SCALARS - TAPS - 2 * KW, width), F32)


def conv_kernel(heads, pre, rim, w, scal, x, bc, conv, msg, wide):
    length, both = pre.shape
    width = both // 2
    for s in range(2):
        cut = slice(s * width, (s + 1) * width)
        rims = mm(rim[...], w[s]).astype(BF16).astype(F32)
        wide[0:8, cut] = rims[RIM - 8 :, :]
        wide[8:, cut] = pre[:, cut].astype(F32)
        acc = scal[BIAS + s : BIAS + s + 1, :] + tap(scal, 0, s) * wide[5 : 5 + length, cut]
        for k in range(1, KW):
            acc = acc + tap(scal, k, s) * wide[5 + k : 5 + k + length, cut]
        conv[:, cut] = acc
        act = (acc * sigmoid(acc)).astype(BF16)
        if s == 0:
            x[...] = act
        else:
            bc[...] = act
    running = scal[0:heads, :]
    last = running[:, length - 1 : length]
    remain = jnp.exp(last - running) * scal[heads : 2 * heads, :]
    scaled = x[...].astype(F32) * widen(columns(remain), heads, width)
    state = mm(scaled, bc[:, 0:N], TN)
    msg[...] = packed(state, jnp.broadcast_to(last, (heads, N)))


def pair_kernel(heads, back, low, mine, other, msg):
    mine, other = mine[...], other[...]
    size = mine.shape[0] - LOGS
    mine_first = low[0] == 0
    mine_logs, other_logs = logs_of(mine, heads), logs_of(other, heads)
    crossed = jnp.logical_not(mine_first) if back else mine_first
    mine_scale = jnp.where(crossed, jnp.exp(other_logs), 1.0)
    other_scale = jnp.where(crossed, 1.0, jnp.exp(mine_logs))
    state = spread_rows(mine_scale, heads, size) * state_of(mine)
    state = state + spread_rows(other_scale, heads, size) * state_of(other)
    msg[...] = packed(state, mine_logs + other_logs)


def link_kernel(heads, farther, nearer, *rest):
    *before, msg, near = rest
    farther, nearer = farther[...], nearer[...]
    size = nearer.shape[0] - LOGS
    logs, more = logs_of(nearer, heads), logs_of(farther, heads)
    state = state_of(farther)
    msg[...] = packed(
        jnp.exp(spread_rows(logs, heads, size)) * state + state_of(nearer), logs + more
    )
    scale = jnp.exp(spread_rows(more, heads, size))
    if before:
        state = before[0][0:size, 0:N] + before[0][0:size, N:] * state
        scale = before[0][0:size, N:] * scale
    near[0:size, 0:N] = state
    near[0:size, N:] = scale


def inside_kernel(heads, x, bc, scal, cot, ow, conv, y, gg, slope):
    length, width = x.shape
    xv = x[...].astype(F32)
    rows = scal[0 : 2 * heads, :]
    cols = columns(rows)
    scores = mm(bc[:, N:], bc[:, 0:N], NT)
    acc = scal[SKIP : SKIP + 1, :] * xv
    for h in range(heads):
        mixing = scores * decay_of(cols, rows, h) * rows[heads + h : heads + h + 1, :]
        acc = acc + mm(mixing, only_head(xv, h, heads))
    y[...] = acc
    gg[...] = scal[GAIN : GAIN + 1, :] * mm(cot[...], ow[...])
    v = conv[...]
    sig = sigmoid(v)
    slope[...] = (sig * (1.0 + v * (1.0 - sig))).astype(BF16)


def join_kernel(heads, low, yi, gg, gate, bc, scal, partner, *rest):
    far, *near, y, sin, sums = rest
    length, width = yi.shape
    start = carried(low[0] == 1, partner[...], far[...], near[0] if near else None, heads)
    sin[...] = start
    grow = widen(columns(jnp.exp(scal[0:heads, :])), heads, width)
    yv = yi[...] + grow * mm(bc[:, N:], start, NT)
    y[...] = yv
    g = gate[...].astype(F32)
    gated = yv * (g * sigmoid(g))
    ones = jnp.ones((8, width), F32)
    square = mm_exact(ones, gated * gated, NT)
    inner = mm_exact(ones, gated * gg[...], NT)
    sums[...] = jnp.where(rows_of(square.shape) == 0, square, inner)


def norm_columns(total, every):
    inv = lax.rsqrt(total[0:1, :] / every + NORM_EPSILON)
    coef = inv * inv * inv * total[1:2, :] / every
    return columns(jnp.concatenate([inv, coef], axis=0))


def grad_y_kernel(heads, every, sums, other, y, gate, gg, bc, scal, gy, msg, total):
    length, width = y.shape
    total[...] = sums[...] + other[...]
    cols = norm_columns(total[...], every)
    g = gate[...].astype(F32)
    act = g * sigmoid(g)
    gated = y[...] * act
    grad = (cols[:, 0:1] * gg[...] - gated * cols[:, 1:2]) * act
    gy[...] = grad
    grow = widen(columns(jnp.exp(scal[0:heads, :])), heads, width)
    last = scal[0:heads, length - 1 : length]
    msg[...] = packed(mm(grad * grow, bc[:, N:], TN), jnp.broadcast_to(last, (heads, N)))


def conv_back(scal, wide, cut, length, slot, slot_cut):
    acc = tap(scal, 0, slot)[:, slot_cut] * wide[KW - 1 : KW - 1 + RIM + length, cut]
    for k in range(1, KW):
        at = KW - 1 - k
        acc = acc + tap(scal, k, slot)[:, slot_cut] * wide[at : at + RIM + length, cut]
    return acc.astype(BF16)


def clear_ends(wide, length):
    zeros = jnp.zeros((RIM, wide.shape[1]), F32)
    wide[0:RIM, :] = zeros
    wide[RIM + length :, :] = zeros[0:8]


def stack_columns(msg, grad, at, base, piece):
    for q in range(grad.shape[1] // N):
        msg[at, (base + q) * piece : (base + q + 1) * piece, :] = grad[
            at * piece : (at + 1) * piece, q * N : (q + 1) * N
        ]


def split_pair(low, every, keep, send):
    for at in range(send.shape[0]):
        keep[at] = every[2 * at + low]
        send[at] = every[2 * at + 1 - low]


def early_kernel(
    heads, every,
    low, total, y, gate, gg, gy, x, bc, scal, sin, cot, series, rim, slope,
    normed, grad_gate, gp, gb, edge, sums, wide,
):
    length, width = y.shape
    depth = series.shape[1]
    rows = scal[0 : 2 * heads, :]
    cols = columns(rows)
    xv = x[...]
    gyv = gy[...].astype(BF16)
    b, c = bc[:, 0:N], bc[:, N:]
    group = jnp.zeros((length, length), F32)
    for h in range(heads):
        pairs = mm(only_head(gyv, h, heads), xv, NT)
        group = group + decay_of(cols, rows, h) * pairs * rows[heads + h : heads + h + 1, :]
    gb[...] = mm(group, c, TN)
    grow = widen(columns(jnp.exp(rows[0:heads])), heads, width)
    grad_c = mm(group, b) + mm(gy[...] * grow, sin[...])
    clear_ends(wide, length)
    wide[RIM : RIM + length, :] = grad_c * slope[:, 2 * width - N :].astype(F32)
    grad_pre = conv_back(scal, wide, slice(0, N), length, 1, slice(width - N, width))
    edge[...] = grad_pre[0:RIM]
    gp[...] = grad_pre[RIM:]
    cols = norm_columns(total[...], every)
    g = gate[...].astype(F32)
    sig = sigmoid(g)
    yv = y[...]
    gated = yv * (g * sig)
    normed[...] = (gated * cols[:, 0:1] * scal[GAIN : GAIN + 1, :]).astype(BF16)
    grad_gated = cols[:, 0:1] * gg[...] - gated * cols[:, 1:2]
    grad_gate[...] = (grad_gated * yv * (sig * (1.0 + g * (1.0 - sig)))).astype(BF16)
    sums[:, 0:width] = mm(cot[...], normed[...], TN).astype(BF16)
    sums[:, width : 2 * width] = mm(series[...], grad_gate[...], TN).astype(BF16)
    w_c = mm(series[...], gp[...], TN) + mm(rim[...], edge[...], TN)
    sums[:, 2 * width :] = w_c.astype(BF16)


def beside_kernel(
    heads, normed, grad_gate, gp, gb, y, gy, x, bc, scal, sin, ow, w,
    sg, held, yb,
):
    length, width = y.shape
    rows = scal[0 : 2 * heads, :]
    cols = columns(rows)
    xv = x[...].astype(F32)
    gyv = gy[...]
    scores = mm(bc[:, N:], bc[:, 0:N], NT)
    back = jnp.zeros((length, width), F32)
    for h in range(heads):
        back = back + mm(scores * decay_of(cols, rows, h), only_head(gyv, h, heads), TN)
    held[:, 0:width] = back
    held[:, width : width + N] = gb[...]
    last = rows[0:heads, length - 1 : length]
    remain = jnp.exp(last - rows[0:heads]) * rows[heads:]
    own = mm(xv * widen(columns(remain), heads, width), bc[:, 0:N], TN)
    whole = jnp.exp(spread_rows(jnp.broadcast_to(last, (heads, N)), heads, width))
    held[:, width + N :] = whole * sin[...] + own
    skips = scal[SKIP : SKIP + 1, :]
    yb[...] = mm_exact(head_mask(heads, width), gyv * (y[...] - skips * xv), NT)
    depth = ow.shape[0]
    sg[:, 0:depth] = mm(normed[...], ow[...], NT).astype(BF16)
    late = mm(grad_gate[...], w[0], NT) + mm(gp[...], w[2, :, width - N :], NT)
    sg[:, depth:] = late.astype(BF16)


def close_kernel(
    heads,
    low, x, bc, scal, gy, held, slope, edge_c, partner, *rest,
):
    far, *near, back, gp, lead, edge, wide = rest
    length, width = gy.shape
    state = carried(low[0] == 0, partner[...], far[...], near[0] if near else None, heads)
    back[0:width, width:] = state
    running, step = scal[0:heads, :], scal[heads : 2 * heads, :]
    remain = jnp.exp(running[:, length - 1 : length] - running)
    cols = columns(jnp.concatenate([remain, step, remain * step], axis=0))
    grown = held[:, 0:width] + widen(cols, heads, width) * mm(bc[:, 0:N], state, NT)
    back[0:length, 0:width] = grown
    grad_x = scal[SKIP : SKIP + 1, :] * gy[...] + widen(cols[:, heads:], heads, width) * grown
    grad_b = held[:, width : width + N] + mm(x[...].astype(F32) * widen(cols[:, 2 * heads :], heads, width), state)
    clear_ends(wide, length)
    wide[RIM : RIM + length, 0:width] = grad_x * slope[:, 0:width].astype(F32)
    wide[RIM : RIM + length, width:] = grad_b * slope[:, width : width + N].astype(F32)
    grad_x = conv_back(scal, wide, slice(0, width), length, 0, slice(0, width))
    grad_b = conv_back(scal, wide, slice(width, width + N), length, 1, slice(0, N))
    for out, cut in ((lead, slice(0, RIM)), (gp, slice(RIM, RIM + length))):
        out[:, 0:width] = grad_x[cut]
        out[:, width:] = grad_b[cut]
    edge[:, 0 : width + N] = lead[...]
    edge[:, width + N :] = edge_c[...]


def late_kernel(
    heads, count,
    low, x, scal, back, gp, lead, yb, held, series, rim,
    keep, send, graw, stage,
):
    length, width = x.shape
    depth = series.shape[1]
    w_xb = (mm(series[...], gp[...], TN) + mm(rim[...], lead[...], TN)).astype(BF16)
    rows = scal[0 : 4 * heads, :]
    step = rows[heads : 2 * heads]
    mask = head_mask(heads, width)
    x_back = mm_exact(mask, x[...].astype(F32) * back[0:length, 0:width], NT)[0:heads]
    ends = jnp.sum(mm_exact(mask, back[0:width, width:] * held[:, width + N :]), axis=1, keepdims=True)[0:heads]
    grad_log = running_sum_back(yb[0:heads, :] - step * x_back) + ends
    grad_step = x_back - rows[3 * heads :] * grad_log
    grad_raw = grad_step * rows[2 * heads : 3 * heads]
    grad_raw = jnp.concatenate([grad_raw, jnp.zeros_like(grad_raw)], axis=0)
    graw[...] = grad_raw
    dt = mm(grad_raw, series[...])
    piece = depth // count
    blank = jnp.zeros((LOGS, N), F32)
    for at in range(count):
        stack_columns(stage, w_xb, at, 0, piece)
        dt_piece = jnp.concatenate(
            [dt[:, at * piece : (at + 1) * piece], blank[0 : 2 * heads, 0 : N - piece]], axis=1
        )
        dt_piece = jnp.concatenate([dt_piece, blank[0 : LOGS - 2 * heads]], axis=0)
        stage[at, 3 * piece :, :] = dt_piece.astype(BF16)
    split_pair(low[0], stage, keep, send)


def halve_kernel(high, keep, other, own, *parts):
    at = high[0]
    own[0 : other.shape[1], :] = keep[at].astype(F32) + other[at].astype(F32)
    for k, part in enumerate(parts):
        at = high[0] ^ (k + 1)
        part[...] = (keep[at].astype(F32) + other[at].astype(F32)).astype(BF16)


def rows_kernel(low, sg, gp, graw, edge, w, dtw, keep, send, stage):
    length, depth = sg.shape[0], sg.shape[1] // 2
    width = w.shape[2]
    heads = dtw.shape[0]
    total = sg[:, depth:].astype(F32) + mm(graw[0:heads, :], dtw[...], TN)
    total = total + mm(gp[:, 0:width], w[1], NT) + mm(gp[:, width:], w[2, :, 0:N], NT)
    late = mm(edge[:, 0:width], w[1], NT) + mm(edge[:, width:], w[2], NT)
    stage[:, 0:depth] = sg[:, 0:depth]
    stage[:, depth:] = total.astype(BF16)
    stage[length - RIM :, depth:] = (total[length - RIM :, :] + late).astype(BF16)
    piece = keep.shape[1]
    for at in range(send.shape[0]):
        start = pl.multiple_of((2 * at + low[0]) * piece, piece)
        keep[at] = stage[pl.ds(start, piece), :]
        start = pl.multiple_of((2 * at + 1 - low[0]) * piece, piece)
        send[at] = stage[pl.ds(start, piece), :]


def sum_of(parts):
    rows = parts[-1].shape[0]
    total = parts[0][0:rows, :]
    for part in parts[1:]:
        total = total + part[...].astype(F32)
    return total


def outputs_kernel(*refs):
    *parts, layer, grad = refs
    depth = layer.shape[1]
    total = sum_of(parts)
    layer[...] = total[:, 0:depth].astype(BF16)
    grad[...] = total[:, depth:]


def early_sum_kernel(early, w_out, others):
    width = w_out.shape[1]
    for cut, out in ((slice(0, width), w_out), (slice(width, early.shape[2]), others)):
        total = early[0, :, cut].astype(F32)
        for at in range(1, early.shape[0]):
            total = total + early[at, :, cut].astype(F32)
        out[...] = total


def total_kernel(early, *refs):
    *parts, w_in, w_dt = refs
    piece, width = w_in.shape[1:]
    w_in[0] = early[:, 0:width]
    w_in[2, :, N:] = early[:, width:]
    late = sum_of(parts)
    for q in range(2):
        w_in[1, :, q * N : (q + 1) * N] = late[q * piece : (q + 1) * piece, :]
    w_in[2, :, 0:N] = late[2 * piece : 3 * piece, :]
    w_dt[...] = late[3 * piece : 3 * piece + w_dt.shape[0], 0:piece]


VMEM = pl.BlockSpec(memory_space=pltpu.VMEM)
SMEM = pl.BlockSpec(memory_space=pltpu.SMEM)
HBM = pl.BlockSpec(memory_space=pltpu.HBM)


def run(kernel, name, outs, args, scalars=(), fetched=(), scratch=()):
    args = [
        pltpu.with_memory_space_constraint(a, pltpu.HBM) if i in fetched else a
        for i, a in enumerate(args)
    ]

    def place(i):
        if i in fetched:
            return HBM
        return SMEM if i in scalars else VMEM

    def whole(*refs):
        held, sems = refs[len(refs) - len(fetched) - 1 : -1], refs[-1]
        refs = list(refs[: len(refs) - len(fetched) - 1])
        copies = []
        for k, i in enumerate(fetched):
            copies.append(pltpu.make_async_copy(refs[i], held[k], sems.at[k]))
            refs[i] = held[k]
        for copy in copies:
            copy.start()
        for copy in copies:
            copy.wait()
        kernel(*refs)

    holders = []
    if fetched:
        for i in fetched:
            kind = pltpu.SMEM if i in scalars else pltpu.VMEM
            holders.append(kind(args[i].shape, args[i].dtype))
        holders.append(pltpu.SemaphoreType.DMA((len(fetched),)))
    return pl.pallas_call(
        whole if fetched else kernel,
        name=name,
        out_shape=[jax.ShapeDtypeStruct(shape, kind) for shape, kind in outs],
        in_specs=[place(i) for i in range(len(args))],
        out_specs=[VMEM] * len(outs),
        scratch_shapes=list(scratch) + holders,
        compiler_params=pltpu.CompilerParams(vmem_limit_bytes=LIMIT),
        cost_estimate=pl.CostEstimate(flops=10**6, bytes_accessed=2**14, transcendentals=0),
    )(*args)


def shifted(block, axis, distance):
    devices = range(lax.axis_size(axis))
    route = [(i - distance, i) for i in devices if i - distance in devices]
    return lax.ppermute(block, axis, route)


def swapped(block, axis, flip):
    return lax.ppermute(block, axis, [(i, i ^ flip) for i in range(lax.axis_size(axis))])


def body(
    series,
    in_weight,
    step_weight,
    step_bias,
    log_rate,
    conv_weight,
    conv_bias,
    skip_gain,
    norm_gain,
    out_weight,
    cotangent,
):
    length, depth = series.shape
    width = in_weight.shape[2]
    heads = step_weight.shape[1]
    count = lax.axis_size("tm")
    parts = lax.axis_size("head")
    every = width * parts
    assert width == 2 * N and heads == 4
    part = functools.partial
    w = in_weight.transpose(1, 0, 2)
    dtw = step_weight.T
    gain = norm_gain.reshape(1, width)
    hops = count // 2
    piece = depth // count
    position = lax.axis_index("tm").astype(jnp.int32)
    spot = lax.axis_index("head").astype(jnp.int32)
    low, high = (position % 2).reshape(1), (position // 2).reshape(1)
    low_spot, high_spot = (spot % 2).reshape(1), (spot // 2).reshape(1)
    rim = shifted(series[length - RIM :], "tm", 1)
    state_msg = ((width + LOGS, N), BF16)

    def passed(msg, back, during):
        made = []

        def meanwhile(k, block):
            if k < len(during):
                block, extra = lax.optimization_barrier((block, during[k](made)))
                made.append(extra)
            return block

        partner = meanwhile(0, swapped(msg, "tm", 1))
        (msg,) = run(part(pair_kernel, heads, back), "pair", [state_msg], [low, msg, partner], (0,))
        near = []
        hop = 1
        while hop < hops:
            far = meanwhile(len(made), shifted(msg, "tm", (-2 if back else 2) * hop))
            hop *= 2
            if hop < hops:
                msg, *near = run(
                    part(link_kernel, heads), "link",
                    [state_msg, ((width, 2 * N), F32)], [far, msg] + near,
                )
                if 2 * hop >= hops and made and len(made) > 1:
                    first = list(made[0])
                    msg, first[-1] = lax.optimization_barrier((msg, first[-1]))
                    made[0] = first
        return [partner, far] + near, made

    def halved(keep, send, axis, where, name):
        most, rows, cols = send.shape
        return run(
            halve_kernel, name, [((rows, cols), F32)] + [((rows, cols), BF16)] * (most - 1),
            [where, keep, swapped(send, axis, 1)], (0,),
        )

    def gathered(blocks, axis):
        return [blocks[0]] + [swapped(block, axis, 2 * k) for k, block in enumerate(blocks) if k]

    gate, pre, scal, w_xbc = run(
        part(project_kernel, heads), "project",
        [
            ((length, width), BF16),
            ((length, 2 * width), BF16),
            ((SCALARS, length), F32),
            ((2, depth, width), BF16),
        ],
        [series, w, dtw, step_bias, log_rate, skip_gain, gain, conv_weight, conv_bias],
        (3, 4, 5), tuple(range(9)),
    )
    x, bc, conv, msg = run(
        part(conv_kernel, heads), "conv",
        [((length, width), BF16), ((length, width), BF16), ((length, 2 * width), F32), state_msg],
        [pre, rim, w_xbc, scal],
        scratch=[pltpu.VMEM((length + 8, 2 * width), F32)],
    )

    def inner(made):
        return run(
            part(inside_kernel, heads), "inside",
            [((length, width), F32), ((length, width), F32), ((length, 2 * width), BF16)],
            [x, bc, scal, cotangent, out_weight, conv],
        )

    ahead, ((inside, gg, slope),) = passed(msg, False, [inner])
    y, sin, sums = run(
        part(join_kernel, heads), "join",
        [((length, width), F32), ((width, N), F32), ((8, length), F32)],
        [low, inside, gg, gate, bc, scal] + ahead, (0,),
    )
    flip = 1
    while 2 * flip < parts:
        sums = sums + swapped(sums, "head", flip)
        flip *= 2
    gy, msg, total = run(
        part(grad_y_kernel, heads, every), "grad_y",
        [((length, width), F32), state_msg, ((8, length), F32)],
        [sums, swapped(sums, "head", flip), y, gate, gg, bc, scal],
    )
    late = 3 * piece + LOGS

    def early_part(made):
        return run(
            part(early_kernel, heads, every), "early",
            [
                ((length, width), BF16),
                ((length, width), BF16),
                ((length, N), BF16),
                ((length, N), F32),
                ((RIM, N), BF16),
                ((depth, 2 * width + N), BF16),
            ],
            [
                low, total, y, gate, gg, gy, x, bc, scal, sin, cotangent, series, rim, slope,
            ],
            (0,),
            scratch=[pltpu.VMEM((length + RIM + 8, N), F32)],
        )

    def beside_part(made):
        normed, grad_gate, gp_c, gb = made[0][0:4]
        return run(
            part(beside_kernel, heads), "beside",
            [
                ((length, 2 * depth), BF16),
                ((length, 2 * width), F32),
                ((8, length), F32),
            ],
            [normed, grad_gate, gp_c, gb, y, gy, x, bc, scal, sin, out_weight, w], (), (10, 11),
        )

    behind, (firsts, (sg, held, yb)) = passed(msg, True, [early_part, beside_part])
    edge_c, early = firsts[4:]
    early = lax.all_to_all(early.reshape(count, piece, 2 * width + N), "tm", 0, 0)
    back, gp, lead, edge = run(
        part(close_kernel, heads), "close",
        [
            ((length, width + N), F32),
            ((length, width + N), BF16),
            ((RIM, width + N), BF16),
            ((RIM, 2 * width), BF16),
        ],
        [low, x, bc, scal, gy, held, slope, edge_c] + behind, (0,),
        scratch=[pltpu.VMEM((length + RIM + 8, width + N), F32)],
    )
    edge = shifted(edge, "tm", -1)
    keep, send, graw = run(
        part(late_kernel, heads, count), "late",
        [((hops, late, N), BF16), ((hops, late, N), BF16), ((2 * heads, length), F32)],
        [low, x, scal, back, gp, lead, yb, held, series, rim], (0,),
        scratch=[pltpu.VMEM((count, late, N), BF16)],
    )
    late_parts = halved(keep, send, "tm", high, "halve_late")
    late_parts = gathered(late_parts, "tm")
    rows = length // parts
    edge, early = lax.optimization_barrier((edge, early))
    w_out_grad, early = run(
        early_sum_kernel, "early_sum",
        [((piece, width), F32), ((piece, width + N), F32)], [early],
    )
    keep, send = run(
        rows_kernel, "rows",
        [((parts // 2, rows, 2 * depth), BF16), ((parts // 2, rows, 2 * depth), BF16)],
        [low_spot, sg, gp, graw, edge, w, dtw], (0,),
        scratch=[pltpu.VMEM((length, 2 * depth), BF16)],
    )
    both = gathered(halved(keep, send, "head", high_spot, "halve_rows"), "head")
    layer_out, series_grad = run(
        outputs_kernel, "outputs", [((rows, depth), BF16), ((rows, depth), F32)], both,
    )
    late_parts, layer_out = lax.optimization_barrier((late_parts, layer_out))
    w_in_grad, w_dt_grad = run(
        total_kernel, "total",
        [((3, piece, width), F32), ((heads, piece), F32)],
        [early] + late_parts,
    )
    return (layer_out, series_grad, w_in_grad.transpose(1, 0, 2), w_dt_grad.T, w_out_grad)


def solution(mesh):
    in_specs = (
        P("tm", None),
        P(None, None, "head"),
        P(None, "head"),
        P("head"),
        P("head"),
        P(None, None, "head"),
        P(None, "head"),
        P("head"),
        P("head"),
        P(None, "head"),
        P("tm", None),
    )
    out_specs = (
        P(("tm", "head"), None),
        P(("tm", "head"), None),
        P("tm", None, "head"),
        P("tm", "head"),
        P("tm", "head"),
    )
    return jax.shard_map(body, mesh=mesh, in_specs=in_specs, out_specs=out_specs, check_vma=False)
```

```python
import functools

import jax
import jax.numpy as jnp
from jax import lax
from jax.experimental import pallas as pl
from jax.experimental.pallas import tpu as pltpu
from jax.sharding import PartitionSpec as P

N = 128
KW = 4
RIM = 16
LIMIT = 6 * 2**20
SKIP, GAIN, BIAS, TAPS, SCALARS = 16, 17, 18, 20, 32
LOGS = 16
NORM_EPSILON = 1e-05

F32 = jnp.float32
BF16 = jnp.bfloat16
NN = (((1,), (0,)), ((), ()))
NT = (((1,), (1,)), ((), ()))
TN = (((0,), (0,)), ((), ()))


def mm(a, b, dims=NN):
    return lax.dot_general(a.astype(BF16), b.astype(BF16), dims, preferred_element_type=F32)


def mm_exact(a, b, dims=NN):
    return lax.dot_general(
        a, b, dims, precision=lax.Precision.HIGHEST, preferred_element_type=F32
    )


def lanes_of(shape):
    return lax.broadcasted_iota(jnp.int32, shape, len(shape) - 1)


def rows_of(shape):
    return lax.broadcasted_iota(jnp.int32, shape, len(shape) - 2)


def per_row(ref, shape):
    rows = rows_of(shape)
    out = jnp.full(shape, ref[0], F32)
    for h in range(1, shape[0]):
        out = jnp.where(rows == h, ref[h], out)
    return out


def per_lane(ref, heads, width):
    head = lanes_of((1, width)) // (width // heads)
    out = jnp.full((1, width), ref[0], F32)
    for h in range(1, heads):
        out = jnp.where(head == h, ref[h], out)
    return out


def widen(cols, heads, width):
    head = lanes_of((cols.shape[0], width)) // (width // heads)
    out = jnp.broadcast_to(cols[:, 0:1], (cols.shape[0], width))
    for h in range(1, heads):
        out = jnp.where(head == h, cols[:, h : h + 1], out)
    return out


def head_mask(heads, width):
    shape = (8, width)
    return jnp.where(lanes_of(shape) // (width // heads) == rows_of(shape), 1.0, 0.0)


def only_head(x, h, heads):
    width = x.shape[1]
    return jnp.where(lanes_of(x.shape) // (width // heads) == h, x, jnp.zeros_like(x))


def tap(scal, k, slot):
    return scal[TAPS + 2 * k + slot : TAPS + 2 * k + slot + 1, :]


def columns(rows):
    short = -rows.shape[0] % 8
    if short:
        rows = jnp.concatenate([rows, jnp.zeros((short, rows.shape[1]), F32)], axis=0)
    return jnp.transpose(rows)


def sigmoid(v):
    return 1.0 / (1.0 + jnp.exp(-v))


def running_sum(x):
    width = x.shape[1]
    lanes = lanes_of(x.shape)
    hop = 1
    while hop < width:
        x = x + jnp.where(lanes >= hop, pltpu.roll(x, hop, 1), 0.0)
        hop *= 2
    return x


def running_sum_back(x):
    width = x.shape[1]
    lanes = lanes_of(x.shape)
    hop = 1
    while hop < width:
        x = x + jnp.where(lanes < width - hop, pltpu.roll(x, width - hop, 1), 0.0)
        hop *= 2
    return x


def decay_of(cols, rows, h):
    length = cols.shape[0]
    gap = cols[:, h : h + 1] - rows[h : h + 1, :]
    shape = (length, length)
    return jnp.exp(jnp.where(lanes_of(shape) <= rows_of(shape), gap, -1e30))


def logs_of(msg, heads):
    logs = msg[msg.shape[0] - LOGS :].astype(F32)
    return logs[0:heads] + logs[heads : 2 * heads] + logs[2 * heads : 3 * heads]


def spread_rows(logs, heads, size):
    return jnp.concatenate(
        [jnp.broadcast_to(logs[h : h + 1], (size // heads, N)) for h in range(heads)], axis=0
    )


def state_of(msg):
    return msg[0 : msg.shape[0] - LOGS].astype(F32)


def packed(state, logs):
    high = logs.astype(BF16).astype(F32)
    middle = (logs - high).astype(BF16).astype(F32)
    low = logs - high - middle
    logs = jnp.concatenate([high, middle, low, jnp.zeros_like(low)], axis=0)
    return jnp.concatenate([state.astype(BF16), logs.astype(BF16)], axis=0)


def carried(own_turn, partner, far, near, heads):
    state = state_of(far)
    size = state.shape[0]
    if near is not None:
        state = near[0:size, 0:N] + near[0:size, N:] * state
    with_partner = jnp.exp(spread_rows(logs_of(partner, heads), heads, size)) * state
    return jnp.where(own_turn, with_partner + state_of(partner), state)


def project_kernel(
    heads, series, w, dtw, bias, rate, skip, gain, cw, cb, gate, pre, scal, w_xbc,
):
    width = w.shape[2]
    s = series[...]
    gate[...] = mm(s, w[0]).astype(BF16)
    pre[:, 0:width] = mm(s, w[1]).astype(BF16)
    pre[:, width:] = mm(s, w[2]).astype(BF16)
    w_xbc[0] = w[1]
    w_xbc[1] = w[2]
    raw = mm(dtw[...], s, NT)
    shifted = raw + per_row(bias, raw.shape)
    step = jnp.maximum(shifted, 0.0) + jnp.log1p(jnp.exp(-jnp.abs(shifted)))
    rates = jnp.exp(per_row(rate, raw.shape))
    scal[0:heads, :] = running_sum(-step * rates)
    scal[heads : 2 * heads, :] = step
    scal[2 * heads : 3 * heads, :] = sigmoid(shifted)
    scal[3 * heads : SKIP, :] = rates
    scal[SKIP : SKIP + 1, :] = per_lane(skip, heads, width)
    scal[GAIN : GAIN + 1, :] = gain[...]
    scal[BIAS : BIAS + 2, :] = cb[...]
    for k in range(KW):
        scal[TAPS + 2 * k : TAPS + 2 * k + 2, :] = cw[k]
    scal[TAPS + 2 * KW :, :] = jnp.zeros((SCALARS - TAPS - 2 * KW, width), F32)


def conv_kernel(heads, pre, rim, w, scal, x, bc, conv, msg, wide):
    length, both = pre.shape
    width = both // 2
    for s in range(2):
        cut = slice(s * width, (s + 1) * width)
        rims = mm(rim[...], w[s]).astype(BF16).astype(F32)
        wide[0:8, cut] = rims[RIM - 8 :, :]
        wide[8:, cut] = pre[:, cut].astype(F32)
        acc = scal[BIAS + s : BIAS + s + 1, :] + tap(scal, 0, s) * wide[5 : 5 + length, cut]
        for k in range(1, KW):
            acc = acc + tap(scal, k, s) * wide[5 + k : 5 + k + length, cut]
        conv[:, cut] = acc
        act = (acc * sigmoid(acc)).astype(BF16)
        if s == 0:
            x[...] = act
        else:
            bc[...] = act
    running = scal[0:heads, :]
    last = running[:, length - 1 : length]
    remain = jnp.exp(last - running) * scal[heads : 2 * heads, :]
    scaled = x[...].astype(F32) * widen(columns(remain), heads, width)
    state = mm(scaled, bc[:, 0:N], TN)
    msg[...] = packed(state, jnp.broadcast_to(last, (heads, N)))


def pair_kernel(heads, back, low, mine, other, msg):
    mine, other = mine[...], other[...]
    size = mine.shape[0] - LOGS
    mine_first = low[0] == 0
    mine_logs, other_logs = logs_of(mine, heads), logs_of(other, heads)
    crossed = jnp.logical_not(mine_first) if back else mine_first
    mine_scale = jnp.where(crossed, jnp.exp(other_logs), 1.0)
    other_scale = jnp.where(crossed, 1.0, jnp.exp(mine_logs))
    state = spread_rows(mine_scale, heads, size) * state_of(mine)
    state = state + spread_rows(other_scale, heads, size) * state_of(other)
    msg[...] = packed(state, mine_logs + other_logs)


def link_kernel(heads, farther, nearer, *rest):
    *before, msg, near = rest
    farther, nearer = farther[...], nearer[...]
    size = nearer.shape[0] - LOGS
    logs, more = logs_of(nearer, heads), logs_of(farther, heads)
    state = state_of(farther)
    msg[...] = packed(
        jnp.exp(spread_rows(logs, heads, size)) * state + state_of(nearer), logs + more
    )
    scale = jnp.exp(spread_rows(more, heads, size))
    if before:
        state = before[0][0:size, 0:N] + before[0][0:size, N:] * state
        scale = before[0][0:size, N:] * scale
    near[0:size, 0:N] = state
    near[0:size, N:] = scale


def inside_kernel(heads, x, bc, scal, cot, ow, conv, y, gg, slope):
    length, width = x.shape
    xv = x[...].astype(F32)
    rows = scal[0 : 2 * heads, :]
    cols = columns(rows)
    scores = mm(bc[:, N:], bc[:, 0:N], NT)
    acc = scal[SKIP : SKIP + 1, :] * xv
    for h in range(heads):
        mixing = scores * decay_of(cols, rows, h) * rows[heads + h : heads + h + 1, :]
        acc = acc + mm(mixing, only_head(xv, h, heads))
    y[...] = acc
    gg[...] = scal[GAIN : GAIN + 1, :] * mm(cot[...], ow[...])
    v = conv[...]
    sig = sigmoid(v)
    slope[...] = (sig * (1.0 + v * (1.0 - sig))).astype(BF16)


def join_kernel(heads, low, yi, gg, gate, bc, scal, partner, *rest):
    far, *near, y, sin, sums = rest
    length, width = yi.shape
    start = carried(low[0] == 1, partner[...], far[...], near[0] if near else None, heads)
    sin[...] = start
    grow = widen(columns(jnp.exp(scal[0:heads, :])), heads, width)
    yv = yi[...] + grow * mm(bc[:, N:], start, NT)
    y[...] = yv
    g = gate[...].astype(F32)
    gated = yv * (g * sigmoid(g))
    ones = jnp.ones((8, width), F32)
    square = mm_exact(ones, gated * gated, NT)
    inner = mm_exact(ones, gated * gg[...], NT)
    sums[...] = jnp.where(rows_of(square.shape) == 0, square, inner)


def norm_columns(total, every):
    inv = lax.rsqrt(total[0:1, :] / every + NORM_EPSILON)
    coef = inv * inv * inv * total[1:2, :] / every
    return columns(jnp.concatenate([inv, coef], axis=0))


def grad_y_kernel(heads, every, sums, other, y, gate, gg, bc, scal, gy, msg, total):
    length, width = y.shape
    total[...] = sums[...] + other[...]
    cols = norm_columns(total[...], every)
    g = gate[...].astype(F32)
    act = g * sigmoid(g)
    gated = y[...] * act
    grad = (cols[:, 0:1] * gg[...] - gated * cols[:, 1:2]) * act
    gy[...] = grad
    grow = widen(columns(jnp.exp(scal[0:heads, :])), heads, width)
    last = scal[0:heads, length - 1 : length]
    msg[...] = packed(mm(grad * grow, bc[:, N:], TN), jnp.broadcast_to(last, (heads, N)))


def conv_back(scal, wide, cut, length, slot, slot_cut):
    acc = tap(scal, 0, slot)[:, slot_cut] * wide[KW - 1 : KW - 1 + RIM + length, cut]
    for k in range(1, KW):
        at = KW - 1 - k
        acc = acc + tap(scal, k, slot)[:, slot_cut] * wide[at : at + RIM + length, cut]
    return acc.astype(BF16)


def clear_ends(wide, length):
    zeros = jnp.zeros((RIM, wide.shape[1]), F32)
    wide[0:RIM, :] = zeros
    wide[RIM + length :, :] = zeros[0:8]


def stack_columns(msg, grad, at, base, piece):
    for q in range(grad.shape[1] // N):
        msg[at, (base + q) * piece : (base + q + 1) * piece, :] = grad[
            at * piece : (at + 1) * piece, q * N : (q + 1) * N
        ]


def split_pair(low, every, keep, send):
    for at in range(send.shape[0]):
        keep[at] = every[2 * at + low]
        send[at] = every[2 * at + 1 - low]


def early_kernel(
    heads, count, every,
    low, total, y, gate, gg, gy, x, bc, scal, sin, cot, series, rim, slope,
    normed, grad_gate, gp, gb, edge, keep, send, wide, stage,
):
    length, width = y.shape
    depth = series.shape[1]
    rows = scal[0 : 2 * heads, :]
    cols = columns(rows)
    xv = x[...]
    gyv = gy[...].astype(BF16)
    b, c = bc[:, 0:N], bc[:, N:]
    group = jnp.zeros((length, length), F32)
    for h in range(heads):
        pairs = mm(only_head(gyv, h, heads), xv, NT)
        group = group + decay_of(cols, rows, h) * pairs * rows[heads + h : heads + h + 1, :]
    gb[...] = mm(group, c, TN)
    grow = widen(columns(jnp.exp(rows[0:heads])), heads, width)
    grad_c = mm(group, b) + mm(gy[...] * grow, sin[...])
    clear_ends(wide, length)
    wide[RIM : RIM + length, :] = grad_c * slope[:, 2 * width - N :].astype(F32)
    grad_pre = conv_back(scal, wide, slice(0, N), length, 1, slice(width - N, width))
    edge[...] = grad_pre[0:RIM]
    gp[...] = grad_pre[RIM:]
    cols = norm_columns(total[...], every)
    g = gate[...].astype(F32)
    sig = sigmoid(g)
    yv = y[...]
    gated = yv * (g * sig)
    normed[...] = (gated * cols[:, 0:1] * scal[GAIN : GAIN + 1, :]).astype(BF16)
    grad_gated = cols[:, 0:1] * gg[...] - gated * cols[:, 1:2]
    grad_gate[...] = (grad_gated * yv * (sig * (1.0 + g * (1.0 - sig)))).astype(BF16)
    w_out = mm(cot[...], normed[...], TN).astype(BF16)
    w_gate = mm(series[...], grad_gate[...], TN).astype(BF16)
    w_c = (mm(series[...], gp[...], TN) + mm(rim[...], edge[...], TN)).astype(BF16)
    piece = depth // count
    for at in range(count):
        stack_columns(stage, w_out, at, 0, piece)
        stack_columns(stage, w_gate, at, 2, piece)
        stack_columns(stage, w_c, at, 4, piece)
    split_pair(low[0], stage, keep, send)


def beside_kernel(
    heads, normed, grad_gate, gp, gb, y, gy, x, bc, scal, sin, ow, w,
    sg, held, yb,
):
    length, width = y.shape
    rows = scal[0 : 2 * heads, :]
    cols = columns(rows)
    xv = x[...].astype(F32)
    gyv = gy[...]
    scores = mm(bc[:, N:], bc[:, 0:N], NT)
    back = jnp.zeros((length, width), F32)
    for h in range(heads):
        back = back + mm(scores * decay_of(cols, rows, h), only_head(gyv, h, heads), TN)
    held[:, 0:width] = back
    held[:, width : width + N] = gb[...]
    last = rows[0:heads, length - 1 : length]
    remain = jnp.exp(last - rows[0:heads]) * rows[heads:]
    own = mm(xv * widen(columns(remain), heads, width), bc[:, 0:N], TN)
    whole = jnp.exp(spread_rows(jnp.broadcast_to(last, (heads, N)), heads, width))
    held[:, width + N :] = whole * sin[...] + own
    skips = scal[SKIP : SKIP + 1, :]
    yb[...] = mm_exact(head_mask(heads, width), gyv * (y[...] - skips * xv), NT)
    depth = ow.shape[0]
    sg[:, 0:depth] = mm(normed[...], ow[...], NT).astype(BF16)
    late = mm(grad_gate[...], w[0], NT) + mm(gp[...], w[2, :, width - N :], NT)
    sg[:, depth:] = late.astype(BF16)


def close_kernel(
    heads,
    low, x, bc, scal, gy, held, slope, edge_c, partner, *rest,
):
    far, *near, ends, gp, lead, edge, wide = rest
    length, width = gy.shape
    state = carried(low[0] == 0, partner[...], far[...], near[0] if near else None, heads)
    running, step = scal[0:heads, :], scal[heads : 2 * heads, :]
    remain = jnp.exp(running[:, length - 1 : length] - running)
    cols = columns(jnp.concatenate([remain, step, remain * step], axis=0))
    grown = held[:, 0:width] + widen(cols, heads, width) * mm(bc[:, 0:N], state, NT)
    mask = head_mask(heads, width)
    ends[0 : 2 * heads, :] = mm_exact(mask, x[...].astype(F32) * grown, NT)
    whole = jnp.sum(mm_exact(mask, state * held[:, width + N :]), axis=1, keepdims=True)
    ends[2 * heads :, :] = jnp.broadcast_to(whole, (2 * heads, length))
    grad_x = scal[SKIP : SKIP + 1, :] * gy[...] + widen(cols[:, heads:], heads, width) * grown
    grad_b = held[:, width : width + N] + mm(x[...].astype(F32) * widen(cols[:, 2 * heads :], heads, width), state)
    clear_ends(wide, length)
    wide[RIM : RIM + length, 0:width] = grad_x * slope[:, 0:width].astype(F32)
    wide[RIM : RIM + length, width:] = grad_b * slope[:, width : width + N].astype(F32)
    grad_x = conv_back(scal, wide, slice(0, width), length, 0, slice(0, width))
    grad_b = conv_back(scal, wide, slice(width, width + N), length, 1, slice(0, N))
    for out, cut in ((lead, slice(0, RIM)), (gp, slice(RIM, RIM + length))):
        out[:, 0:width] = grad_x[cut]
        out[:, width:] = grad_b[cut]
    edge[:, 0 : width + N] = lead[...]
    edge[:, width + N :] = edge_c[...]


def late_kernel(
    heads, count,
    low, scal, ends, gp, lead, yb, series, rim,
    keep, send, graw, stage,
):
    depth = rim.shape[1]
    rows = scal[0 : 4 * heads, :]
    step = rows[heads : 2 * heads]
    x_back = ends[0:heads, :]
    grad_log = running_sum_back(yb[0:heads, :] - step * x_back)
    grad_log = grad_log + ends[2 * heads : 3 * heads, :]
    grad_step = x_back - rows[3 * heads :] * grad_log
    grad_raw = grad_step * rows[2 * heads : 3 * heads]
    grad_raw = jnp.concatenate([grad_raw, jnp.zeros_like(grad_raw)], axis=0)
    graw[...] = grad_raw
    series = series()
    w_xb = (mm(series[...], gp[...], TN) + mm(rim[...], lead[...], TN)).astype(BF16)
    dt = mm(grad_raw, series[...])
    piece = depth // count
    blank = jnp.zeros((LOGS, N), F32)
    for at in range(count):
        stack_columns(stage, w_xb, at, 0, piece)
        dt_piece = jnp.concatenate(
            [dt[:, at * piece : (at + 1) * piece], blank[0 : 2 * heads, 0 : N - piece]], axis=1
        )
        dt_piece = jnp.concatenate([dt_piece, blank[0 : LOGS - 2 * heads]], axis=0)
        stage[at, 3 * piece :, :] = dt_piece.astype(BF16)
    split_pair(low[0], stage, keep, send)


def halve_kernel(high, keep, other, own, *parts):
    at = high[0]
    own[0 : other.shape[1], :] = keep[at].astype(F32) + other[at].astype(F32)
    for k, part in enumerate(parts):
        at = high[0] ^ (k + 1)
        part[...] = (keep[at].astype(F32) + other[at].astype(F32)).astype(BF16)


def rows_kernel(low, sg, gp, graw, edge, w, dtw, keep, send, stage):
    length, depth = sg.shape[0], sg.shape[1] // 2
    width = w.shape[2]
    heads = dtw.shape[0]
    total = sg[:, depth:].astype(F32) + mm(graw[0:heads, :], dtw[...], TN)
    total = total + mm(gp[:, 0:width], w[1], NT) + mm(gp[:, width:], w[2, :, 0:N], NT)
    late = mm(edge[:, 0:width], w[1], NT) + mm(edge[:, width:], w[2], NT)
    stage[:, 0:depth] = sg[:, 0:depth]
    stage[:, depth:] = total.astype(BF16)
    stage[length - RIM :, depth:] = (total[length - RIM :, :] + late).astype(BF16)
    piece = keep.shape[1]
    for at in range(send.shape[0]):
        start = pl.multiple_of((2 * at + low[0]) * piece, piece)
        keep[at] = stage[pl.ds(start, piece), :]
        start = pl.multiple_of((2 * at + 1 - low[0]) * piece, piece)
        send[at] = stage[pl.ds(start, piece), :]


def sum_of(parts):
    rows = parts[-1].shape[0]
    total = parts[0][0:rows, :]
    for part in parts[1:]:
        total = total + part[...].astype(F32)
    return total


def outputs_kernel(*refs):
    *parts, layer, grad = refs
    depth = layer.shape[1]
    total = sum_of(parts)
    layer[...] = total[:, 0:depth].astype(BF16)
    grad[...] = total[:, depth:]


def early_sum_kernel(*refs):
    *parts, w_out, others = refs
    piece = w_out.shape[0]
    total = sum_of(parts)
    for q in range(2):
        w_out[:, q * N : (q + 1) * N] = total[q * piece : (q + 1) * piece, :]
    others[0 : 3 * piece, :] = total[2 * piece :, :]


def total_kernel(early, *refs):
    *parts, w_in, w_dt = refs
    piece = w_in.shape[1]
    late = sum_of(parts)
    for q in range(2):
        cut = slice(q * N, (q + 1) * N)
        w_in[0, :, cut] = early[q * piece : (q + 1) * piece, :]
        w_in[1, :, cut] = late[q * piece : (q + 1) * piece, :]
    w_in[2, :, 0:N] = late[2 * piece : 3 * piece, :]
    w_in[2, :, N:] = early[2 * piece : 3 * piece, :]
    w_dt[...] = late[3 * piece : 3 * piece + w_dt.shape[0], 0:piece]


VMEM = pl.BlockSpec(memory_space=pltpu.VMEM)
SMEM = pl.BlockSpec(memory_space=pltpu.SMEM)
HBM = pl.BlockSpec(memory_space=pltpu.HBM)


def waited(copy, ref):
    copy.wait()
    return ref


def run(kernel, name, outs, args, scalars=(), fetched=(), lazy=False, scratch=()):
    args = [
        pltpu.with_memory_space_constraint(a, pltpu.HBM) if i in fetched else a
        for i, a in enumerate(args)
    ]

    def place(i):
        if i in fetched:
            return HBM
        return SMEM if i in scalars else VMEM

    def whole(*refs):
        held, sems = refs[len(refs) - len(fetched) - 1 : -1], refs[-1]
        refs = list(refs[: len(refs) - len(fetched) - 1])
        copies = []
        for k, i in enumerate(fetched):
            copies.append(pltpu.make_async_copy(refs[i], held[k], sems.at[k]))
            refs[i] = held[k]
        for copy in copies:
            copy.start()
        for copy, i in zip(copies, fetched):
            if lazy:
                refs[i] = functools.partial(waited, copy, refs[i])
            else:
                copy.wait()
        kernel(*refs)

    holders = []
    if fetched:
        for i in fetched:
            kind = pltpu.SMEM if i in scalars else pltpu.VMEM
            holders.append(kind(args[i].shape, args[i].dtype))
        holders.append(pltpu.SemaphoreType.DMA((len(fetched),)))
    return pl.pallas_call(
        whole if fetched else kernel,
        name=name,
        out_shape=[jax.ShapeDtypeStruct(shape, kind) for shape, kind in outs],
        in_specs=[place(i) for i in range(len(args))],
        out_specs=[VMEM] * len(outs),
        scratch_shapes=list(scratch) + holders,
        compiler_params=pltpu.CompilerParams(vmem_limit_bytes=LIMIT),
        cost_estimate=pl.CostEstimate(flops=10**6, bytes_accessed=2**14, transcendentals=0),
    )(*args)


def shifted(block, axis, distance):
    devices = range(lax.axis_size(axis))
    route = [(i - distance, i) for i in devices if i - distance in devices]
    return lax.ppermute(block, axis, route)


def swapped(block, axis, flip):
    return lax.ppermute(block, axis, [(i, i ^ flip) for i in range(lax.axis_size(axis))])


def body(
    series,
    in_weight,
    step_weight,
    step_bias,
    log_rate,
    conv_weight,
    conv_bias,
    skip_gain,
    norm_gain,
    out_weight,
    cotangent,
):
    length, depth = series.shape
    width = in_weight.shape[2]
    heads = step_weight.shape[1]
    count = lax.axis_size("tm")
    parts = lax.axis_size("head")
    every = width * parts
    assert width == 2 * N and heads == 4
    part = functools.partial
    w = in_weight.transpose(1, 0, 2)
    dtw = step_weight.T
    gain = norm_gain.reshape(1, width)
    hops = count // 2
    piece = depth // count
    position = lax.axis_index("tm").astype(jnp.int32)
    spot = lax.axis_index("head").astype(jnp.int32)
    low, high = (position % 2).reshape(1), (position // 2).reshape(1)
    low_spot, high_spot = (spot % 2).reshape(1), (spot // 2).reshape(1)
    rim = shifted(series[length - RIM :], "tm", 1)
    state_msg = ((width + LOGS, N), BF16)

    def passed(msg, back, during):
        made = []

        def meanwhile(k, block):
            if k < len(during):
                block, extra = lax.optimization_barrier((block, during[k](made)))
                made.append(extra)
            return block

        partner = meanwhile(0, swapped(msg, "tm", 1))
        (msg,) = run(part(pair_kernel, heads, back), "pair", [state_msg], [low, msg, partner], (0,))
        near = []
        hop = 1
        while hop < hops:
            far = meanwhile(len(made), shifted(msg, "tm", (-2 if back else 2) * hop))
            hop *= 2
            if hop < hops:
                msg, *near = run(
                    part(link_kernel, heads), "link",
                    [state_msg, ((width, 2 * N), F32)], [far, msg] + near,
                )
        return [partner, far] + near, made

    def halved(keep, send, axis, where, name):
        most, rows, cols = send.shape
        return run(
            halve_kernel, name, [((rows, cols), F32)] + [((rows, cols), BF16)] * (most - 1),
            [where, keep, swapped(send, axis, 1)], (0,),
        )

    def gathered(blocks, axis):
        return [blocks[0]] + [swapped(block, axis, 2 * k) for k, block in enumerate(blocks) if k]

    gate, pre, scal, w_xbc = run(
        part(project_kernel, heads), "project",
        [
            ((length, width), BF16),
            ((length, 2 * width), BF16),
            ((SCALARS, length), F32),
            ((2, depth, width), BF16),
        ],
        [series, w, dtw, step_bias, log_rate, skip_gain, gain, conv_weight, conv_bias],
        (3, 4, 5), tuple(range(9)),
    )
    x, bc, conv, msg = run(
        part(conv_kernel, heads), "conv",
        [((length, width), BF16), ((length, width), BF16), ((length, 2 * width), F32), state_msg],
        [pre, rim, w_xbc, scal],
        scratch=[pltpu.VMEM((length + 8, 2 * width), F32)],
    )

    def inner(made):
        return run(
            part(inside_kernel, heads), "inside",
            [((length, width), F32), ((length, width), F32), ((length, 2 * width), BF16)],
            [x, bc, scal, cotangent, out_weight, conv],
        )

    ahead, ((inside, gg, slope),) = passed(msg, False, [inner])
    y, sin, sums = run(
        part(join_kernel, heads), "join",
        [((length, width), F32), ((width, N), F32), ((8, length), F32)],
        [low, inside, gg, gate, bc, scal] + ahead, (0,),
    )
    flip = 1
    while 2 * flip < parts:
        sums = sums + swapped(sums, "head", flip)
        flip *= 2
    gy, msg, total = run(
        part(grad_y_kernel, heads, every), "grad_y",
        [((length, width), F32), state_msg, ((8, length), F32)],
        [sums, swapped(sums, "head", flip), y, gate, gg, bc, scal],
    )
    early, late = 5 * piece, 3 * piece + LOGS

    def early_part(made):
        return run(
            part(early_kernel, heads, count, every), "early",
            [
                ((length, width), BF16),
                ((length, width), BF16),
                ((length, N), BF16),
                ((length, N), F32),
                ((RIM, N), BF16),
                ((hops, early, N), BF16),
                ((hops, early, N), BF16),
            ],
            [
                low, total, y, gate, gg, gy, x, bc, scal, sin, cotangent, series, rim, slope,
            ],
            (0,), (10, 11),
            scratch=[
                pltpu.VMEM((length + RIM + 8, N), F32),
                pltpu.VMEM((count, early, N), BF16),
            ],
        )

    def beside_part(made):
        normed, grad_gate, gp_c, gb = made[0][0:4]
        return run(
            part(beside_kernel, heads), "beside",
            [
                ((length, 2 * depth), BF16),
                ((length, 2 * width), F32),
                ((8, length), F32),
            ],
            [normed, grad_gate, gp_c, gb, y, gy, x, bc, scal, sin, out_weight, w], (), (10, 11),
        )

    behind, (firsts, (sg, held, yb)) = passed(msg, True, [early_part, beside_part])
    edge_c, keep, send = firsts[4:]
    early_parts = halved(keep, send, "tm", high, "halve_early")
    early_parts = gathered(early_parts, "tm")
    ends, gp, lead, edge = run(
        part(close_kernel, heads), "close",
        [
            ((4 * heads, length), F32),
            ((length, width + N), BF16),
            ((RIM, width + N), BF16),
            ((RIM, 2 * width), BF16),
        ],
        [low, x, bc, scal, gy, held, slope, edge_c] + behind, (0,),
        scratch=[pltpu.VMEM((length + RIM + 8, width + N), F32)],
    )
    edge = shifted(edge, "tm", -1)
    keep, send, graw = run(
        part(late_kernel, heads, count), "late",
        [((hops, late, N), BF16), ((hops, late, N), BF16), ((2 * heads, length), F32)],
        [low, scal, ends, gp, lead, yb, series, rim], (0,), (6,), True,
        scratch=[pltpu.VMEM((count, late, N), BF16)],
    )
    late_parts = halved(keep, send, "tm", high, "halve_late")
    late_parts = gathered(late_parts, "tm")
    rows = length // parts
    edge, early_parts = lax.optimization_barrier((edge, early_parts))
    w_out_grad, early_total = run(
        early_sum_kernel, "early_sum",
        [((piece, width), F32), ((3 * piece, N), F32)], early_parts,
    )
    keep, send = run(
        rows_kernel, "rows",
        [((parts // 2, rows, 2 * depth), BF16), ((parts // 2, rows, 2 * depth), BF16)],
        [low_spot, sg, gp, graw, edge, w, dtw], (0,),
        scratch=[pltpu.VMEM((length, 2 * depth), BF16)],
    )
    both = gathered(halved(keep, send, "head", high_spot, "halve_rows"), "head")
    layer_out, series_grad = run(
        outputs_kernel, "outputs", [((rows, depth), BF16), ((rows, depth), F32)], both,
    )
    late_parts, layer_out = lax.optimization_barrier((late_parts, layer_out))
    w_in_grad, w_dt_grad = run(
        total_kernel, "total",
        [((3, piece, width), F32), ((heads, piece), F32)], [early_total] + late_parts,
    )
    return (layer_out, series_grad, w_in_grad.transpose(1, 0, 2), w_dt_grad.T, w_out_grad)


def solution(mesh):
    in_specs = (
        P("tm", None),
        P(None, None, "head"),
        P(None, "head"),
        P("head"),
        P("head"),
        P(None, None, "head"),
        P(None, "head"),
        P("head"),
        P("head"),
        P(None, "head"),
        P("tm", None),
    )
    out_specs = (
        P(("tm", "head"), None),
        P(("tm", "head"), None),
        P("tm", None, "head"),
        P("tm", "head"),
        P("tm", "head"),
    )
    return jax.shard_map(body, mesh=mesh, in_specs=in_specs, out_specs=out_specs, check_vma=False)
```

```python
import functools

import jax
import jax.numpy as jnp
from jax import lax
from jax.experimental import pallas as pl
from jax.experimental.pallas import tpu as pltpu
from jax.sharding import PartitionSpec as P

N = 128
KW = 4
RIM = 16
LIMIT = 6 * 2**20
SKIP, GAIN, BIAS, TAPS, SCALARS = 16, 17, 18, 20, 32
LOGS = 16
NORM_EPSILON = 1e-05

F32 = jnp.float32
BF16 = jnp.bfloat16
NN = (((1,), (0,)), ((), ()))
NT = (((1,), (1,)), ((), ()))
TN = (((0,), (0,)), ((), ()))


def mm(a, b, dims=NN):
    return lax.dot_general(a.astype(BF16), b.astype(BF16), dims, preferred_element_type=F32)


def mm_exact(a, b, dims=NN):
    return lax.dot_general(
        a, b, dims, precision=lax.Precision.HIGHEST, preferred_element_type=F32
    )


def lanes_of(shape):
    return lax.broadcasted_iota(jnp.int32, shape, len(shape) - 1)


def rows_of(shape):
    return lax.broadcasted_iota(jnp.int32, shape, len(shape) - 2)


def per_row(ref, shape):
    rows = rows_of(shape)
    out = jnp.full(shape, ref[0], F32)
    for h in range(1, shape[0]):
        out = jnp.where(rows == h, ref[h], out)
    return out


def per_lane(ref, heads, width):
    head = lanes_of((1, width)) // (width // heads)
    out = jnp.full((1, width), ref[0], F32)
    for h in range(1, heads):
        out = jnp.where(head == h, ref[h], out)
    return out


def widen(cols, heads, width):
    head = lanes_of((cols.shape[0], width)) // (width // heads)
    out = jnp.broadcast_to(cols[:, 0:1], (cols.shape[0], width))
    for h in range(1, heads):
        out = jnp.where(head == h, cols[:, h : h + 1], out)
    return out


def head_mask(heads, width):
    shape = (8, width)
    return jnp.where(lanes_of(shape) // (width // heads) == rows_of(shape), 1.0, 0.0)


def only_head(x, h, heads):
    width = x.shape[1]
    return jnp.where(lanes_of(x.shape) // (width // heads) == h, x, jnp.zeros_like(x))


def tap(scal, k, slot):
    return scal[TAPS + 2 * k + slot : TAPS + 2 * k + slot + 1, :]


def columns(rows):
    short = -rows.shape[0] % 8
    if short:
        rows = jnp.concatenate([rows, jnp.zeros((short, rows.shape[1]), F32)], axis=0)
    return jnp.transpose(rows)


def sigmoid(v):
    return 1.0 / (1.0 + jnp.exp(-v))


def running_sum(x):
    width = x.shape[1]
    lanes = lanes_of(x.shape)
    hop = 1
    while hop < width:
        x = x + jnp.where(lanes >= hop, pltpu.roll(x, hop, 1), 0.0)
        hop *= 2
    return x


def running_sum_back(x):
    width = x.shape[1]
    lanes = lanes_of(x.shape)
    hop = 1
    while hop < width:
        x = x + jnp.where(lanes < width - hop, pltpu.roll(x, width - hop, 1), 0.0)
        hop *= 2
    return x


def decay_of(cols, rows, h):
    length = cols.shape[0]
    gap = cols[:, h : h + 1] - rows[h : h + 1, :]
    shape = (length, length)
    return jnp.exp(jnp.where(lanes_of(shape) <= rows_of(shape), gap, -1e30))


def logs_of(msg, heads):
    logs = msg[msg.shape[0] - LOGS :].astype(F32)
    return logs[0:heads] + logs[heads : 2 * heads] + logs[2 * heads : 3 * heads]


def spread_rows(logs, heads, size):
    return jnp.concatenate(
        [jnp.broadcast_to(logs[h : h + 1], (size // heads, N)) for h in range(heads)], axis=0
    )


def state_of(msg):
    return msg[0 : msg.shape[0] - LOGS].astype(F32)


def packed(state, logs):
    high = logs.astype(BF16).astype(F32)
    middle = (logs - high).astype(BF16).astype(F32)
    low = logs - high - middle
    logs = jnp.concatenate([high, middle, low, jnp.zeros_like(low)], axis=0)
    return jnp.concatenate([state.astype(BF16), logs.astype(BF16)], axis=0)


def carried(own_turn, partner, far, near, heads):
    state = state_of(far)
    size = state.shape[0]
    if near is not None:
        state = near[0:size, 0:N] + near[0:size, N:] * state
    with_partner = jnp.exp(spread_rows(logs_of(partner, heads), heads, size)) * state
    return jnp.where(own_turn, with_partner + state_of(partner), state)


def project_kernel(
    heads, series, w, dtw, bias, rate, skip, gain, cw, cb, gate, pre, scal, w_xbc,
):
    width = w.shape[2]
    s = series[...]
    gate[...] = mm(s, w[0]).astype(BF16)
    pre[:, 0:width] = mm(s, w[1]).astype(BF16)
    pre[:, width:] = mm(s, w[2]).astype(BF16)
    w_xbc[0] = w[1]
    w_xbc[1] = w[2]
    raw = mm(dtw[...], s, NT)
    shifted = raw + per_row(bias, raw.shape)
    step = jnp.maximum(shifted, 0.0) + jnp.log1p(jnp.exp(-jnp.abs(shifted)))
    rates = jnp.exp(per_row(rate, raw.shape))
    scal[0:heads, :] = running_sum(-step * rates)
    scal[heads : 2 * heads, :] = step
    scal[2 * heads : 3 * heads, :] = sigmoid(shifted)
    scal[3 * heads : SKIP, :] = rates
    scal[SKIP : SKIP + 1, :] = per_lane(skip, heads, width)
    scal[GAIN : GAIN + 1, :] = gain[...]
    scal[BIAS : BIAS + 2, :] = cb[...]
    for k in range(KW):
        scal[TAPS + 2 * k : TAPS + 2 * k + 2, :] = cw[k]
    scal[TAPS + 2 * KW :, :] = jnp.zeros((SCALARS - TAPS - 2 * KW, width), F32)


def conv_kernel(heads, pre, rim, w, scal, x, bc, conv, msg, wide):
    length, both = pre.shape
    width = both // 2
    for s in range(2):
        cut = slice(s * width, (s + 1) * width)
        rims = mm(rim[...], w[s]).astype(BF16).astype(F32)
        wide[0:8, cut] = rims[RIM - 8 :, :]
        wide[8:, cut] = pre[:, cut].astype(F32)
        acc = scal[BIAS + s : BIAS + s + 1, :] + tap(scal, 0, s) * wide[5 : 5 + length, cut]
        for k in range(1, KW):
            acc = acc + tap(scal, k, s) * wide[5 + k : 5 + k + length, cut]
        conv[:, cut] = acc
        act = (acc * sigmoid(acc)).astype(BF16)
        if s == 0:
            x[...] = act
        else:
            bc[...] = act
    running = scal[0:heads, :]
    last = running[:, length - 1 : length]
    remain = jnp.exp(last - running) * scal[heads : 2 * heads, :]
    scaled = x[...].astype(F32) * widen(columns(remain), heads, width)
    state = mm(scaled, bc[:, 0:N], TN)
    msg[...] = packed(state, jnp.broadcast_to(last, (heads, N)))


def pair_kernel(heads, back, low, mine, other, msg):
    mine, other = mine[...], other[...]
    size = mine.shape[0] - LOGS
    mine_first = low[0] == 0
    mine_logs, other_logs = logs_of(mine, heads), logs_of(other, heads)
    crossed = jnp.logical_not(mine_first) if back else mine_first
    mine_scale = jnp.where(crossed, jnp.exp(other_logs), 1.0)
    other_scale = jnp.where(crossed, 1.0, jnp.exp(mine_logs))
    state = spread_rows(mine_scale, heads, size) * state_of(mine)
    state = state + spread_rows(other_scale, heads, size) * state_of(other)
    msg[...] = packed(state, mine_logs + other_logs)


def link_kernel(heads, farther, nearer, *rest):
    *before, msg, near = rest
    farther, nearer = farther[...], nearer[...]
    size = nearer.shape[0] - LOGS
    logs, more = logs_of(nearer, heads), logs_of(farther, heads)
    state = state_of(farther)
    msg[...] = packed(
        jnp.exp(spread_rows(logs, heads, size)) * state + state_of(nearer), logs + more
    )
    scale = jnp.exp(spread_rows(more, heads, size))
    if before:
        state = before[0][0:size, 0:N] + before[0][0:size, N:] * state
        scale = before[0][0:size, N:] * scale
    near[0:size, 0:N] = state
    near[0:size, N:] = scale


def inside_kernel(heads, x, bc, scal, cot, ow, conv, y, gg, slope):
    length, width = x.shape
    xv = x[...].astype(F32)
    rows = scal[0 : 2 * heads, :]
    cols = columns(rows)
    scores = mm(bc[:, N:], bc[:, 0:N], NT)
    acc = scal[SKIP : SKIP + 1, :] * xv
    for h in range(heads):
        mixing = scores * decay_of(cols, rows, h) * rows[heads + h : heads + h + 1, :]
        acc = acc + mm(mixing, only_head(xv, h, heads))
    y[...] = acc
    gg[...] = scal[GAIN : GAIN + 1, :] * mm(cot[...], ow[...])
    v = conv[...]
    sig = sigmoid(v)
    slope[...] = (sig * (1.0 + v * (1.0 - sig))).astype(BF16)


def join_kernel(heads, low, yi, gg, gate, bc, scal, partner, *rest):
    far, *near, y, sin, sums = rest
    length, width = yi.shape
    start = carried(low[0] == 1, partner[...], far[...], near[0] if near else None, heads)
    sin[...] = start
    grow = widen(columns(jnp.exp(scal[0:heads, :])), heads, width)
    yv = yi[...] + grow * mm(bc[:, N:], start, NT)
    y[...] = yv
    g = gate[...].astype(F32)
    gated = yv * (g * sigmoid(g))
    ones = jnp.ones((8, width), F32)
    square = mm_exact(ones, gated * gated, NT)
    inner = mm_exact(ones, gated * gg[...], NT)
    sums[...] = jnp.where(rows_of(square.shape) == 0, square, inner)


def norm_columns(total, every):
    inv = lax.rsqrt(total[0:1, :] / every + NORM_EPSILON)
    coef = inv * inv * inv * total[1:2, :] / every
    return columns(jnp.concatenate([inv, coef], axis=0))


def grad_y_kernel(heads, every, sums, other, y, gate, gg, bc, scal, gy, msg, total):
    length, width = y.shape
    total[...] = sums[...] + other[...]
    cols = norm_columns(total[...], every)
    g = gate[...].astype(F32)
    act = g * sigmoid(g)
    gated = y[...] * act
    grad = (cols[:, 0:1] * gg[...] - gated * cols[:, 1:2]) * act
    gy[...] = grad
    grow = widen(columns(jnp.exp(scal[0:heads, :])), heads, width)
    last = scal[0:heads, length - 1 : length]
    msg[...] = packed(mm(grad * grow, bc[:, N:], TN), jnp.broadcast_to(last, (heads, N)))


def conv_back(scal, wide, cut, length, slot, slot_cut):
    acc = tap(scal, 0, slot)[:, slot_cut] * wide[KW - 1 : KW - 1 + RIM + length, cut]
    for k in range(1, KW):
        at = KW - 1 - k
        acc = acc + tap(scal, k, slot)[:, slot_cut] * wide[at : at + RIM + length, cut]
    return acc.astype(BF16)


def clear_ends(wide, length):
    zeros = jnp.zeros((RIM, wide.shape[1]), F32)
    wide[0:RIM, :] = zeros
    wide[RIM + length :, :] = zeros[0:8]


def stack_columns(msg, grad, at, base, piece):
    for q in range(grad.shape[1] // N):
        msg[at, (base + q) * piece : (base + q + 1) * piece, :] = grad[
            at * piece : (at + 1) * piece, q * N : (q + 1) * N
        ]


def split_pair(low, every, keep, send):
    for at in range(send.shape[0]):
        keep[at] = every[2 * at + low]
        send[at] = every[2 * at + 1 - low]


def early_kernel(
    heads, count, every,
    low, total, y, gate, gg, gy, x, bc, scal, sin, cot, series, rim, slope,
    normed, grad_gate, gp, gb, edge, keep, send, wide, stage,
):
    length, width = y.shape
    depth = series.shape[1]
    rows = scal[0 : 2 * heads, :]
    cols = columns(rows)
    xv = x[...]
    gyv = gy[...].astype(BF16)
    b, c = bc[:, 0:N], bc[:, N:]
    group = jnp.zeros((length, length), F32)
    for h in range(heads):
        pairs = mm(only_head(gyv, h, heads), xv, NT)
        group = group + decay_of(cols, rows, h) * pairs * rows[heads + h : heads + h + 1, :]
    gb[...] = mm(group, c, TN)
    grow = widen(columns(jnp.exp(rows[0:heads])), heads, width)
    grad_c = mm(group, b) + mm(gy[...] * grow, sin[...])
    clear_ends(wide, length)
    wide[RIM : RIM + length, :] = grad_c * slope[:, 2 * width - N :].astype(F32)
    grad_pre = conv_back(scal, wide, slice(0, N), length, 1, slice(width - N, width))
    edge[...] = grad_pre[0:RIM]
    gp[...] = grad_pre[RIM:]
    cols = norm_columns(total[...], every)
    g = gate[...].astype(F32)
    sig = sigmoid(g)
    yv = y[...]
    gated = yv * (g * sig)
    normed[...] = (gated * cols[:, 0:1] * scal[GAIN : GAIN + 1, :]).astype(BF16)
    grad_gated = cols[:, 0:1] * gg[...] - gated * cols[:, 1:2]
    grad_gate[...] = (grad_gated * yv * (sig * (1.0 + g * (1.0 - sig)))).astype(BF16)
    w_out = mm(cot[...], normed[...], TN).astype(BF16)
    w_gate = mm(series[...], grad_gate[...], TN).astype(BF16)
    w_c = (mm(series[...], gp[...], TN) + mm(rim[...], edge[...], TN)).astype(BF16)
    piece = depth // count
    for at in range(count):
        stack_columns(stage, w_out, at, 0, piece)
        stack_columns(stage, w_gate, at, 2, piece)
        stack_columns(stage, w_c, at, 4, piece)
    split_pair(low[0], stage, keep, send)


def beside_kernel(
    heads, normed, grad_gate, gp, gb, y, gy, x, bc, scal, sin, ow, w,
    sg, held, yb,
):
    length, width = y.shape
    rows = scal[0 : 2 * heads, :]
    cols = columns(rows)
    xv = x[...].astype(F32)
    gyv = gy[...]
    scores = mm(bc[:, N:], bc[:, 0:N], NT)
    back = jnp.zeros((length, width), F32)
    for h in range(heads):
        back = back + mm(scores * decay_of(cols, rows, h), only_head(gyv, h, heads), TN)
    held[:, 0:width] = back
    held[:, width : width + N] = gb[...]
    last = rows[0:heads, length - 1 : length]
    remain = jnp.exp(last - rows[0:heads]) * rows[heads:]
    own = mm(xv * widen(columns(remain), heads, width), bc[:, 0:N], TN)
    whole = jnp.exp(spread_rows(jnp.broadcast_to(last, (heads, N)), heads, width))
    held[:, width + N :] = whole * sin[...] + own
    skips = scal[SKIP : SKIP + 1, :]
    yb[...] = mm_exact(head_mask(heads, width), gyv * (y[...] - skips * xv), NT)
    depth = ow.shape[0]
    sg[:, 0:depth] = mm(normed[...], ow[...], NT).astype(BF16)
    late = mm(grad_gate[...], w[0], NT) + mm(gp[...], w[2, :, width - N :], NT)
    sg[:, depth:] = late.astype(BF16)


def close_kernel(
    heads,
    low, x, bc, scal, gy, held, slope, edge_c, partner, *rest,
):
    far, *near, ends, gp, lead, edge, wide = rest
    length, width = gy.shape
    state = carried(low[0] == 0, partner[...], far[...], near[0] if near else None, heads)
    running, step = scal[0:heads, :], scal[heads : 2 * heads, :]
    remain = jnp.exp(running[:, length - 1 : length] - running)
    cols = columns(jnp.concatenate([remain, step, remain * step], axis=0))
    grown = held[:, 0:width] + widen(cols, heads, width) * mm(bc[:, 0:N], state, NT)
    mask = head_mask(heads, width)
    ends[0 : 2 * heads, :] = mm_exact(mask, x[...].astype(F32) * grown, NT)
    whole = jnp.sum(mm_exact(mask, state * held[:, width + N :]), axis=1, keepdims=True)
    ends[2 * heads :, :] = jnp.broadcast_to(whole, (2 * heads, length))
    grad_x = scal[SKIP : SKIP + 1, :] * gy[...] + widen(cols[:, heads:], heads, width) * grown
    grad_b = held[:, width : width + N] + mm(x[...].astype(F32) * widen(cols[:, 2 * heads :], heads, width), state)
    clear_ends(wide, length)
    wide[RIM : RIM + length, 0:width] = grad_x * slope[:, 0:width].astype(F32)
    wide[RIM : RIM + length, width:] = grad_b * slope[:, width : width + N].astype(F32)
    grad_x = conv_back(scal, wide, slice(0, width), length, 0, slice(0, width))
    grad_b = conv_back(scal, wide, slice(width, width + N), length, 1, slice(0, N))
    for out, cut in ((lead, slice(0, RIM)), (gp, slice(RIM, RIM + length))):
        out[:, 0:width] = grad_x[cut]
        out[:, width:] = grad_b[cut]
    edge[:, 0 : width + N] = lead[...]
    edge[:, width + N :] = edge_c[...]


def late_kernel(
    heads, count,
    low, scal, ends, gp, lead, yb, series, rim,
    keep, send, graw, stage,
):
    depth = rim.shape[1]
    rows = scal[0 : 4 * heads, :]
    step = rows[heads : 2 * heads]
    x_back = ends[0:heads, :]
    grad_log = running_sum_back(yb[0:heads, :] - step * x_back)
    grad_log = grad_log + ends[2 * heads : 3 * heads, :]
    grad_step = x_back - rows[3 * heads :] * grad_log
    grad_raw = grad_step * rows[2 * heads : 3 * heads]
    grad_raw = jnp.concatenate([grad_raw, jnp.zeros_like(grad_raw)], axis=0)
    graw[...] = grad_raw
    series = series()
    w_xb = (mm(series[...], gp[...], TN) + mm(rim[...], lead[...], TN)).astype(BF16)
    dt = mm(grad_raw, series[...])
    piece = depth // count
    blank = jnp.zeros((LOGS, N), F32)
    for at in range(count):
        stack_columns(stage, w_xb, at, 0, piece)
        dt_piece = jnp.concatenate(
            [dt[:, at * piece : (at + 1) * piece], blank[0 : 2 * heads, 0 : N - piece]], axis=1
        )
        dt_piece = jnp.concatenate([dt_piece, blank[0 : LOGS - 2 * heads]], axis=0)
        stage[at, 3 * piece :, :] = dt_piece.astype(BF16)
    split_pair(low[0], stage, keep, send)


def halve_kernel(high, keep, other, own, *parts):
    at = high[0]
    own[0 : other.shape[1], :] = keep[at].astype(F32) + other[at].astype(F32)
    for k, part in enumerate(parts):
        at = high[0] ^ (k + 1)
        part[...] = (keep[at].astype(F32) + other[at].astype(F32)).astype(BF16)


def rows_kernel(spot, sg, gp, graw, edge, w, dtw, *rest):
    *parts, stage = rest
    length, depth = sg.shape[0], sg.shape[1] // 2
    width = w.shape[2]
    heads = dtw.shape[0]
    total = sg[:, depth:].astype(F32) + mm(graw[0:heads, :], dtw[...], TN)
    total = total + mm(gp[:, 0:width], w[1], NT) + mm(gp[:, width:], w[2, :, 0:N], NT)
    late = mm(edge[:, 0:width], w[1], NT) + mm(edge[:, width:], w[2], NT)
    stage[:, 0:depth] = sg[:, 0:depth]
    stage[:, depth:] = total.astype(BF16)
    stage[length - RIM :, depth:] = (total[length - RIM :, :] + late).astype(BF16)
    piece = parts[0].shape[0]
    for k, part in enumerate(parts):
        start = pl.multiple_of((spot[0] ^ k) * piece, piece)
        part[...] = stage[pl.ds(start, piece), :]


def sum_of(parts):
    rows = parts[-1].shape[0]
    total = parts[0][0:rows, :].astype(F32)
    for part in parts[1:]:
        total = total + part[...].astype(F32)
    return total


def early_sum_kernel(*refs):
    *parts, w_out, others = refs
    piece = w_out.shape[0]
    total = sum_of(parts)
    for q in range(2):
        w_out[:, q * N : (q + 1) * N] = total[q * piece : (q + 1) * piece, :]
    others[0 : 3 * piece, :] = total[2 * piece :, :]


def final_kernel(hops, early, *refs):
    *blocks, layer, grad, w_in, w_dt = refs
    parts, blocks = blocks[:hops], blocks[hops:]
    depth = layer.shape[1]
    total = sum_of(blocks)
    layer[...] = total[:, 0:depth].astype(BF16)
    grad[...] = total[:, depth:]
    piece = w_in.shape[1]
    late = sum_of(parts)
    for q in range(2):
        cut = slice(q * N, (q + 1) * N)
        w_in[0, :, cut] = early[q * piece : (q + 1) * piece, :]
        w_in[1, :, cut] = late[q * piece : (q + 1) * piece, :]
    w_in[2, :, 0:N] = late[2 * piece : 3 * piece, :]
    w_in[2, :, N:] = early[2 * piece : 3 * piece, :]
    w_dt[...] = late[3 * piece : 3 * piece + w_dt.shape[0], 0:piece]


VMEM = pl.BlockSpec(memory_space=pltpu.VMEM)
SMEM = pl.BlockSpec(memory_space=pltpu.SMEM)
HBM = pl.BlockSpec(memory_space=pltpu.HBM)


def waited(copy, ref):
    copy.wait()
    return ref


def run(kernel, name, outs, args, scalars=(), fetched=(), lazy=False, scratch=()):
    args = [
        pltpu.with_memory_space_constraint(a, pltpu.HBM) if i in fetched else a
        for i, a in enumerate(args)
    ]

    def place(i):
        if i in fetched:
            return HBM
        return SMEM if i in scalars else VMEM

    def whole(*refs):
        held, sems = refs[len(refs) - len(fetched) - 1 : -1], refs[-1]
        refs = list(refs[: len(refs) - len(fetched) - 1])
        copies = []
        for k, i in enumerate(fetched):
            copies.append(pltpu.make_async_copy(refs[i], held[k], sems.at[k]))
            refs[i] = held[k]
        for copy in copies:
            copy.start()
        for copy, i in zip(copies, fetched):
            if lazy:
                refs[i] = functools.partial(waited, copy, refs[i])
            else:
                copy.wait()
        kernel(*refs)

    holders = []
    if fetched:
        for i in fetched:
            kind = pltpu.SMEM if i in scalars else pltpu.VMEM
            holders.append(kind(args[i].shape, args[i].dtype))
        holders.append(pltpu.SemaphoreType.DMA((len(fetched),)))
    return pl.pallas_call(
        whole if fetched else kernel,
        name=name,
        out_shape=[jax.ShapeDtypeStruct(shape, kind) for shape, kind in outs],
        in_specs=[place(i) for i in range(len(args))],
        out_specs=[VMEM] * len(outs),
        scratch_shapes=list(scratch) + holders,
        compiler_params=pltpu.CompilerParams(vmem_limit_bytes=LIMIT),
        cost_estimate=pl.CostEstimate(flops=10**6, bytes_accessed=2**14, transcendentals=0),
    )(*args)


def shifted(block, axis, distance):
    devices = range(lax.axis_size(axis))
    route = [(i - distance, i) for i in devices if i - distance in devices]
    return lax.ppermute(block, axis, route)


def swapped(block, axis, flip):
    return lax.ppermute(block, axis, [(i, i ^ flip) for i in range(lax.axis_size(axis))])


def body(
    series,
    in_weight,
    step_weight,
    step_bias,
    log_rate,
    conv_weight,
    conv_bias,
    skip_gain,
    norm_gain,
    out_weight,
    cotangent,
):
    length, depth = series.shape
    width = in_weight.shape[2]
    heads = step_weight.shape[1]
    count = lax.axis_size("tm")
    parts = lax.axis_size("head")
    every = width * parts
    assert width == 2 * N and heads == 4
    part = functools.partial
    w = in_weight.transpose(1, 0, 2)
    dtw = step_weight.T
    gain = norm_gain.reshape(1, width)
    hops = count // 2
    piece = depth // count
    position = lax.axis_index("tm").astype(jnp.int32)
    spot = lax.axis_index("head").astype(jnp.int32)
    low, high = (position % 2).reshape(1), (position // 2).reshape(1)
    rim = shifted(series[length - RIM :], "tm", 1)
    state_msg = ((width + LOGS, N), BF16)

    def passed(msg, back, during):
        made = []

        def meanwhile(k, block):
            if k < len(during):
                block, extra = lax.optimization_barrier((block, during[k](made)))
                made.append(extra)
            return block

        partner = meanwhile(0, swapped(msg, "tm", 1))
        (msg,) = run(part(pair_kernel, heads, back), "pair", [state_msg], [low, msg, partner], (0,))
        near = []
        hop = 1
        while hop < hops:
            far = meanwhile(len(made), shifted(msg, "tm", (-2 if back else 2) * hop))
            hop *= 2
            if hop < hops:
                msg, *near = run(
                    part(link_kernel, heads), "link",
                    [state_msg, ((width, 2 * N), F32)], [far, msg] + near,
                )
        return [partner, far] + near, made

    def halved(keep, send, axis, where, name):
        most, rows, cols = send.shape
        return run(
            halve_kernel, name, [((rows, cols), F32)] + [((rows, cols), BF16)] * (most - 1),
            [where, keep, swapped(send, axis, 1)], (0,),
        )

    def gathered(blocks, axis):
        return [blocks[0]] + [swapped(block, axis, 2 * k) for k, block in enumerate(blocks) if k]

    gate, pre, scal, w_xbc = run(
        part(project_kernel, heads), "project",
        [
            ((length, width), BF16),
            ((length, 2 * width), BF16),
            ((SCALARS, length), F32),
            ((2, depth, width), BF16),
        ],
        [series, w, dtw, step_bias, log_rate, skip_gain, gain, conv_weight, conv_bias],
        (3, 4, 5), tuple(range(9)),
    )
    x, bc, conv, msg = run(
        part(conv_kernel, heads), "conv",
        [((length, width), BF16), ((length, width), BF16), ((length, 2 * width), F32), state_msg],
        [pre, rim, w_xbc, scal],
        scratch=[pltpu.VMEM((length + 8, 2 * width), F32)],
    )

    def inner(made):
        return run(
            part(inside_kernel, heads), "inside",
            [((length, width), F32), ((length, width), F32), ((length, 2 * width), BF16)],
            [x, bc, scal, cotangent, out_weight, conv],
        )

    ahead, ((inside, gg, slope),) = passed(msg, False, [inner])
    y, sin, sums = run(
        part(join_kernel, heads), "join",
        [((length, width), F32), ((width, N), F32), ((8, length), F32)],
        [low, inside, gg, gate, bc, scal] + ahead, (0,),
    )
    flip = 1
    while 2 * flip < parts:
        sums = sums + swapped(sums, "head", flip)
        flip *= 2
    gy, msg, total = run(
        part(grad_y_kernel, heads, every), "grad_y",
        [((length, width), F32), state_msg, ((8, length), F32)],
        [sums, swapped(sums, "head", flip), y, gate, gg, bc, scal],
    )
    early, late = 5 * piece, 3 * piece + LOGS

    def early_part(made):
        return run(
            part(early_kernel, heads, count, every), "early",
            [
                ((length, width), BF16),
                ((length, width), BF16),
                ((length, N), BF16),
                ((length, N), F32),
                ((RIM, N), BF16),
                ((hops, early, N), BF16),
                ((hops, early, N), BF16),
            ],
            [
                low, total, y, gate, gg, gy, x, bc, scal, sin, cotangent, series, rim, slope,
            ],
            (0,), (10, 11),
            scratch=[
                pltpu.VMEM((length + RIM + 8, N), F32),
                pltpu.VMEM((count, early, N), BF16),
            ],
        )

    def beside_part(made):
        normed, grad_gate, gp_c, gb = made[0][0:4]
        return run(
            part(beside_kernel, heads), "beside",
            [
                ((length, 2 * depth), BF16),
                ((length, 2 * width), F32),
                ((8, length), F32),
            ],
            [normed, grad_gate, gp_c, gb, y, gy, x, bc, scal, sin, out_weight, w], (), (10, 11),
        )

    behind, (firsts, (sg, held, yb)) = passed(msg, True, [early_part, beside_part])
    edge_c, keep, send = firsts[4:]
    early_parts = halved(keep, send, "tm", high, "halve_early")
    early_parts = gathered(early_parts, "tm")
    ends, gp, lead, edge = run(
        part(close_kernel, heads), "close",
        [
            ((4 * heads, length), F32),
            ((length, width + N), BF16),
            ((RIM, width + N), BF16),
            ((RIM, 2 * width), BF16),
        ],
        [low, x, bc, scal, gy, held, slope, edge_c] + behind, (0,),
        scratch=[pltpu.VMEM((length + RIM + 8, width + N), F32)],
    )
    edge = shifted(edge, "tm", -1)
    keep, send, graw = run(
        part(late_kernel, heads, count), "late",
        [((hops, late, N), BF16), ((hops, late, N), BF16), ((2 * heads, length), F32)],
        [low, scal, ends, gp, lead, yb, series, rim], (0,), (6,), True,
        scratch=[pltpu.VMEM((count, late, N), BF16)],
    )
    late_parts = halved(keep, send, "tm", high, "halve_late")
    late_parts = gathered(late_parts, "tm")
    rows = length // parts
    w_out_grad, early_total = run(
        early_sum_kernel, "early_sum",
        [((piece, width), F32), ((3 * piece, N), F32)], early_parts,
    )
    blocks = run(
        rows_kernel, "rows",
        [((rows, 2 * depth), BF16)] * parts,
        [spot.reshape(1), sg, gp, graw, edge, w, dtw], (0,),
        scratch=[pltpu.VMEM((length, 2 * depth), BF16)],
    )
    blocks = [blocks[0]] + [swapped(blocks[k], "head", k) for k in range(1, parts)]
    layer_out, series_grad, w_in_grad, w_dt_grad = run(
        part(final_kernel, hops), "final",
        [
            ((rows, depth), BF16),
            ((rows, depth), F32),
            ((3, piece, width), F32),
            ((heads, piece), F32),
        ],
        [early_total] + late_parts + blocks,
    )
    return (layer_out, series_grad, w_in_grad.transpose(1, 0, 2), w_dt_grad.T, w_out_grad)


def solution(mesh):
    in_specs = (
        P("tm", None),
        P(None, None, "head"),
        P(None, "head"),
        P("head"),
        P("head"),
        P(None, None, "head"),
        P(None, "head"),
        P("head"),
        P("head"),
        P(None, "head"),
        P("tm", None),
    )
    out_specs = (
        P(("tm", "head"), None),
        P(("tm", "head"), None),
        P("tm", None, "head"),
        P("tm", "head"),
        P("tm", "head"),
    )
    return jax.shard_map(body, mesh=mesh, in_specs=in_specs, out_specs=out_specs, check_vma=False)
```
